32 devices in a mesh: dp: 4 (over x, core), gx: 2 (over y), gy: 4 (over z).
Axes of the slice: x: 2, y: 2, z: 4, core: 2. Of those that a mesh axis runs over, the one named last changes fastest.
Arguments:
- layer_input: bfloat16 [18464, 1024], P(('dp', 'gx'), 'gy'), may hold values from -70 to 70
- output_grad: bfloat16 [18464, 1024], P(('dp', 'gx'), 'gy'), may hold values from -6 to 6
- first_gain: bfloat16 [1024], P('gy'), may hold values from 0.099609375 to 1.8984375
- first_shift: bfloat16 [1024], P('gy'), may hold values from -4 to 4
- query_weight: bfloat16 [1024, 1024], P('gy', 'gx'), may hold values from -0.375 to 0.375
- key_weight: bfloat16 [1024, 1024], P('gy', 'gx'), may hold values from -0.1875 to 0.1875
- value_weight: bfloat16 [1024, 1024], P('gy', 'gx'), may hold values from -0.1875 to 0.1875
- query_bias: bfloat16 [1024], P('gx'), may hold values from -4 to 4
- value_bias: bfloat16 [1024], P('gx'), may hold values from -3 to 3
- out_weight: bfloat16 [1024, 1024], P('gx', 'gy'), may hold values from -0.75 to 0.75
- out_bias: bfloat16 [1024], P('gy'), may hold values from -4 to 4
- second_gain: bfloat16 [1024], P('gy'), may hold values from 0.099609375 to 1.8984375
- second_shift: bfloat16 [1024], P('gy'), may hold values from -4 to 4
- up_weight: bfloat16 [1024, 4096], P('gy', 'gx'), may hold values from -0.1875 to 0.1875
- up_bias: bfloat16 [4096], P('gx'), may hold values from -6 to 6
- down_weight: bfloat16 [4096, 1024], P('gx', 'gy'), may hold values from -0.09375 to 0.09375
- down_bias: bfloat16 [1024], P('gy'), may hold values from -4 to 4
Outputs:
- layer_output: bfloat16 [18464, 1024], P(('dp', 'gx'), 'gy')
- input_grad: bfloat16 [18464, 1024], P(('dp', 'gx'), 'gy')
- first_gain_grad: float32 [1024], P('gy')
- first_shift_grad: float32 [1024], P('gy')
- query_weight_grad: float32 [1024, 1024], P('gy', 'gx')
- key_weight_grad: float32 [1024, 1024], P('gy', 'gx')
- value_weight_grad: float32 [1024, 1024], P('gy', 'gx')
- query_bias_grad: float32 [1024], P('gx')
- value_bias_grad: float32 [1024], P('gx')
- out_weight_grad: float32 [1024, 1024], P('gx', 'gy')
- out_bias_grad: float32 [1024], P('gy')
- second_gain_grad: float32 [1024], P('gy')
- second_shift_grad: float32 [1024], P('gy')
- up_weight_grad: float32 [1024, 4096], P('gy', 'gx')
- up_bias_grad: float32 [4096], P('gx')
- down_weight_grad: float32 [4096, 1024], P('gx', 'gy')
- down_bias_grad: float32 [1024], P('gy')
The draws below stay inside these ranges and needn't reach their ends.
All inputs are finite; a program needn't handle non-finite values.
Results may differ from the reference program's by a relative error of at most 0.018.
Values may be sent and summed in bfloat16 or wider, within the bound.
No kernel may reach another device: no remote copies, remote signals or barrier semaphores. Data moves between devices by JAX's collectives and lax.ppermute only.
A program may use at most 256 MiB of HBM per device.

```python
import math
import jax
import jax.numpy as jnp
from jax import lax

D = 1024
HEADS = 16
HEAD_DIM = 64
FF = 4096
SEQ = 577
IMGS = 4
TOKENS = 18464


def draw_layer_input(key, part):
    base_key, row_key, column_key = jax.random.split(key, 3)
    ramp = 3.0 ** (jnp.arange(D, dtype=jnp.float32) / (D - 1))
    column_scale = ramp * jnp.exp(jax.random.uniform(column_key, (D,), jnp.float32, math.log(0.7), math.log(1.4)))
    base_draw = jnp.clip(jax.random.normal(base_key, (TOKENS, D), jnp.float32), -4.0, 4.0)
    row_scale = jnp.exp(jax.random.uniform(row_key, (TOKENS, 1), jnp.float32, math.log(0.5), math.log(4.0)))
    return (base_draw * row_scale * column_scale).astype(jnp.bfloat16)


def steps_of(stream_key, extent, shards, least, high):
    gain = 1.0
    for position, blocks in shards:
        steps = jax.random.uniform(jax.random.fold_in(jax.random.fold_in(stream_key, 6), position), (blocks,), jnp.float32, least / len(shards), high / len(shards))
        gain = gain * jnp.repeat(jnp.exp(steps), extent[position] // blocks).reshape((-1,) + (1,) * (len(extent) - 1 - position))
    return gain


def centred(key, dims, scale, most, cuts=(), kind=jnp.bfloat16):
    drawn = scale * jax.random.normal(key, dims, jnp.float32)
    if cuts:
        drawn = drawn * steps_of(key, dims, cuts, -0.22, 0.18)
    return jnp.clip(drawn, -most, most).astype(kind)


def setup_inputs(seed: int = 0) -> dict:
    keys = jax.random.split(jax.random.key(seed), 18)
    return {
        "layer_input": draw_layer_input(jax.random.fold_in(keys[17], 71), 0),
        "output_grad": centred(keys[1], (TOKENS, D), 1.0, 6.0, ((0, 8), (1, 4))),
        "first_gain": jnp.clip(1.0 + 0.18 * jax.random.normal(keys[2], (D,), jnp.float32), 0.099609375, 1.8984375).astype(jnp.bfloat16),
        "first_shift": centred(keys[3], (D,), 0.3, 4.0, ((0, 4),)),
        "query_weight": centred(keys[4], (D, D), (D // 4) ** -0.5, 0.375, ((0, 4), (1, 2))),
        "key_weight": centred(keys[5], (D, D), D ** -0.5, 0.1875, ((0, 4), (1, 2))),
        "value_weight": centred(keys[6], (D, D), D ** -0.5, 0.1875, ((0, 4), (1, 2))),
        "query_bias": centred(keys[7], (D,), 0.3, 4.0, ((0, 2),)),
        "value_bias": centred(keys[8], (D,), 0.2, 3.0, ((0, 2),)),
        "out_weight": centred(keys[9], (D, D), (D // 16) ** -0.5, 0.75, ((0, 2), (1, 4))),
        "out_bias": centred(keys[10], (D,), 0.3, 4.0, ((0, 4),)),
        "second_gain": jnp.clip(1.0 + 0.18 * jax.random.normal(keys[11], (D,), jnp.float32), 0.099609375, 1.8984375).astype(jnp.bfloat16),
        "second_shift": centred(keys[12], (D,), 0.3, 4.0, ((0, 4),)),
        "up_weight": centred(keys[13], (D, FF), D ** -0.5, 0.1875, ((0, 4), (1, 2))),
        "up_bias": centred(keys[14], (FF,), 0.5, 6.0, ((0, 2),)),
        "down_weight": centred(keys[15], (FF, D), FF ** -0.5, 0.09375, ((0, 2), (1, 4))),
        "down_bias": centred(keys[16], (D,), 0.3, 4.0, ((0, 4),)),
    }


EPSILON = 1e-06
PRECISE = lax.Precision.HIGHEST

@jax.custom_vjp
def low(v):
    return lax.optimization_barrier(v.astype(jnp.bfloat16)).astype(jnp.float32)

@jax.custom_vjp
def low_back(v):
    return v

def low_keep(v):
    return (low(v), None)

def low_pass(kept, grad):
    return (grad,)

def back_keep(v):
    return (v, None)

def back_low(kept, grad):
    return (low(grad),)
low.defvjp(low_keep, low_pass)
low_back.defvjp(back_keep, back_low)

def layer_norm(values, gain_vector, shift_vector):
    center = values - lax.optimization_barrier(jnp.mean(values, axis=1, keepdims=True))
    spread = lax.optimization_barrier(jnp.mean(center * center, axis=1, keepdims=True))
    return center * lax.rsqrt(spread + EPSILON) * gain_vector + shift_vector

def attention(queries, key_rows, value_rows):
    scores = low_back(jnp.einsum('bqhd,bkhd->bhqk', queries, key_rows, precision=PRECISE) * HEAD_DIM ** (-0.5))
    weights = low(jax.nn.softmax(scores, axis=-1))
    mixture = jnp.einsum('bhqk,bkhd->bqhd', weights, value_rows, precision=PRECISE)
    return low(low_back(mixture))

def forward(params, inputs):
    first_gain, first_shift, query_weight, key_weight, value_weight, query_bias, value_bias, out_weight, out_bias, second_gain, second_shift, up_weight, up_bias, down_weight, down_bias = params
    row_total = inputs.shape[0]
    image_shape = (row_total // SEQ, SEQ, HEADS, HEAD_DIM)
    normed = low(layer_norm(inputs, first_gain, first_shift))
    queries = low(low_back(jnp.dot(normed, query_weight, precision=PRECISE) + query_bias))
    key_rows = low(low_back(jnp.dot(normed, key_weight, precision=PRECISE)))
    value_rows = low(low_back(jnp.dot(normed, value_weight, precision=PRECISE) + value_bias))
    mixture = attention(queries.reshape(image_shape), key_rows.reshape(image_shape), value_rows.reshape(image_shape))
    mixture = mixture.reshape(row_total, D)
    branch = low_back(jnp.dot(mixture, out_weight, precision=PRECISE) + out_bias)
    middle = inputs + branch
    normed_two = low(layer_norm(middle, second_gain, second_shift))
    hidden_pre = low_back(jnp.dot(normed_two, up_weight, precision=PRECISE) + up_bias)
    hidden = low(jax.nn.gelu(hidden_pre, approximate=False))
    feed_out = low_back(jnp.dot(hidden, down_weight, precision=PRECISE) + down_bias)
    return middle + feed_out

def reference(layer_input, output_grad, first_gain, first_shift, query_weight, key_weight, value_weight, query_bias, value_bias, out_weight, out_bias, second_gain, second_shift, up_weight, up_bias, down_weight, down_bias):
    params = (first_gain.astype(jnp.float32), first_shift.astype(jnp.float32), query_weight.astype(jnp.float32), key_weight.astype(jnp.float32), value_weight.astype(jnp.float32), query_bias.astype(jnp.float32), value_bias.astype(jnp.float32), out_weight.astype(jnp.float32), out_bias.astype(jnp.float32), second_gain.astype(jnp.float32), second_shift.astype(jnp.float32), up_weight.astype(jnp.float32), up_bias.astype(jnp.float32), down_weight.astype(jnp.float32), down_bias.astype(jnp.float32))
    group_rows = IMGS * SEQ
    block_count = TOKENS // group_rows
    inputs = layer_input.astype(jnp.float32).reshape(block_count, group_rows, D)
    cotangents = output_grad.astype(jnp.float32).reshape(block_count, group_rows, D)

    def advance(running, blocks):
        block_in, block_cot = blocks
        result, pullback = jax.vjp(forward, params, block_in)
        param_grads, in_grad = pullback(block_cot)
        running = jax.tree.map(lambda earlier, update: earlier + update, running, param_grads)
        return (running, (result.astype(jnp.bfloat16), in_grad.astype(jnp.bfloat16)))
    initial = tuple((jnp.zeros(p_item.shape, jnp.float32) for p_item in params))
    totals, (outputs, input_grads) = lax.scan(advance, initial, (inputs, cotangents))
    return (outputs.reshape(TOKENS, D), input_grads.reshape(TOKENS, D), totals[0], totals[1], totals[2], totals[3], totals[4], totals[5], totals[6], totals[7], totals[8], totals[9], totals[10], totals[11], totals[12], totals[13], totals[14])
```

```python
from functools import partial

import jax
import jax.numpy as jnp
from jax import lax
from jax.experimental import pallas as pl
from jax.experimental.pallas import tpu as pltpu
from jax.sharding import PartitionSpec as P

D = 1024
HEAD_DIM = 64
SEQ = 577
EPSILON = 1e-06
F32 = jnp.float32
BF16 = jnp.bfloat16
CONTRACT_ROWS = (((0,), (0,)), ((), ()))


def halvings(size):
    steps = []
    step = size >> 1
    while step:
        steps.append(step)
        step >>= 1
    return steps


def swap(value, axis, step):
    size = lax.axis_size(axis)
    return lax.ppermute(value, axis, [(i, i ^ step) for i in range(size)])


AXES = ("dp", "gx", "gy")


def shifted(offsets, axis, step):
    place = AXES.index(axis)
    return [o[:place] + (o[place] ^ step,) + o[place + 1 :] for o in offsets]


def doubled(pieces, offsets, axis, step):
    return (
        jnp.concatenate([pieces, swap(pieces, axis, step)], axis=0),
        offsets + shifted(offsets, axis, step),
    )


def gather_pieces(block):
    rows = block.shape[1]
    share = lax.axis_size("dp")
    quarter = rows // share
    piece = lax.dynamic_slice_in_dim(block, lax.axis_index("dp") * quarter, quarter, axis=1)
    pieces, offsets = piece[None], [(0, 0, 0)]
    for step in halvings(lax.axis_size("gy")):
        pieces, offsets = doubled(pieces, offsets, "gy", step)
    halves = [pieces[:, :, : quarter // 2], pieces[:, :, quarter // 2 :]]
    orders = [
        [("gx", s) for s in halvings(lax.axis_size("gx"))] + [("dp", s) for s in halvings(share)[:-1]],
        [("dp", s) for s in halvings(share)[:-1]] + [("gx", s) for s in halvings(lax.axis_size("gx"))],
    ]
    bundles = []
    for half in range(2):
        got, offs = halves[half], offsets
        for axis, step in orders[half]:
            got, offs = doubled(got, offs, axis, step)
        bundles.append((got, offs, half))
        bundles.append((swap(got, "dp", 1), shifted(offs, "dp", 1), half))
    return bundles


def assemble(block, rows_axis):
    cols_axis = "gx" if rows_axis == "gy" else "gy"
    m, rows, cols = block.shape
    share = lax.axis_size("dp")
    part = rows // share // 2
    whole = (m, rows * lax.axis_size(rows_axis), cols * lax.axis_size(cols_axis))
    bundles = gather_pieces(block)
    place = jnp.stack([lax.axis_index(a) for a in AXES]).astype(jnp.int32)

    def kernel(place_ref, *refs):
        sources, out, sem = refs[: len(bundles)], refs[-2], refs[-1]
        for source, (_, offs, half) in zip(sources, bundles):
            for i, offset in enumerate(offs):
                at = {a: place_ref[j] ^ offset[j] for j, a in enumerate(AXES)}
                row = at[rows_axis] * rows + at["dp"] * (2 * part) + half * part
                col = at[cols_axis] * cols
                pltpu.make_async_copy(
                    source.at[i],
                    out.at[:, pl.ds(pl.multiple_of(row, 16), part), pl.ds(pl.multiple_of(col, 128), cols)],
                    sem,
                ).start()
        pltpu.make_async_copy(out, out, sem).wait()

    return pl.pallas_call(
        kernel,
        grid_spec=pltpu.PrefetchScalarGridSpec(
            num_scalar_prefetch=1,
            grid=(),
            in_specs=[pl.BlockSpec(memory_space=pl.ANY)] * len(bundles),
            out_specs=pl.BlockSpec(memory_space=pltpu.VMEM),
            scratch_shapes=[pltpu.SemaphoreType.DMA],
        ),
        compiler_params=pltpu.CompilerParams(vmem_limit_bytes=40 * 1024 * 1024),
        out_shape=jax.ShapeDtypeStruct(whole, BF16),
        cost_estimate=pl.CostEstimate(
            flops=0, bytes_accessed=4 * whole[0] * whole[1] * whole[2], transcendentals=0
        ),
    )(place, *[b[0] for b in bundles])


def halve(value, axis, bit):
    size = value.shape[axis] // 2
    return (
        lax.dynamic_slice_in_dim(value, bit * size, size, axis),
        lax.dynamic_slice_in_dim(value, (1 - bit) * size, size, axis),
    )


def fold(value, axis, mesh_axis, step):
    bit = (lax.axis_index(mesh_axis) & step) // step
    kept, sent = halve(value, axis, bit)
    return (kept.astype(F32) + swap(sent, mesh_axis, step).astype(F32)).astype(BF16)


def scatter_sum(grad, rows_axis):
    cols_axis = "gx" if rows_axis == "gy" else "gy"
    m, whole_rows, whole_cols = grad.shape
    share = lax.axis_size("dp")
    count = lax.axis_size(rows_axis)
    rows = whole_rows // count
    part = rows // share // 2
    view = grad.astype(BF16).reshape(m, count, share // 2, 2, 2, part, whole_cols)
    core = lax.axis_index("dp") & 1
    kept, sent = (
        lax.dynamic_index_in_dim(view, core, 3, keepdims=False),
        lax.dynamic_index_in_dim(view, 1 - core, 3, keepdims=False),
    )
    total = (kept.astype(F32) + swap(sent, "dp", 1).astype(F32)).astype(BF16)
    halves = [total[:, :, :, 0], total[:, :, :, 1]]

    def over_dp(value):
        for step in halvings(share)[:-1]:
            value = fold(value, 2, "dp", step)
        return value

    def over_blocks(value, axis):
        for step in halvings(lax.axis_size(axis)):
            value = fold(value, 1 if axis == rows_axis else 4, axis, step)
        return value

    first = over_blocks(over_dp(halves[0]), "gx")
    second = over_dp(over_blocks(halves[1], "gx"))
    total = over_blocks(jnp.concatenate([first, second], axis=3), "gy")
    total = total[:, 0, 0]
    got = total[None]
    index = lax.axis_index("dp")
    for step in reversed(halvings(share)):
        bit = (index & step) // step
        other = swap(got, "dp", step)
        got = jnp.concatenate([jnp.where(bit == 0, got, other), jnp.where(bit == 0, other, got)], axis=0)
    return got.transpose(1, 0, 2, 3).reshape(m, rows, got.shape[3]).astype(F32)


def spread_vector(vector, axis):
    size = lax.axis_size(axis)
    pieces, offsets = vector[None], [0]
    for step in halvings(size):
        pieces = jnp.concatenate([pieces, swap(pieces, axis, step)], axis=0)
        offsets = offsets + [o ^ step for o in offsets]
    index = lax.axis_index(axis)
    wanted = jnp.arange(size)[:, None]
    total = jnp.zeros((size, vector.shape[0]), F32)
    for i, offset in enumerate(offsets):
        total = total + jnp.where(wanted == (index ^ offset), pieces[i][None].astype(F32), 0.0)
    return total


def product(left_rows, weight, weight_axis):
    return lax.dot_general(
        left_rows, weight, (((1,), (weight_axis,)), ((), ())), preferred_element_type=jnp.float32
    )


def row_product(left_rows, right_rows):
    return lax.dot_general(left_rows, right_rows, CONTRACT_ROWS, preferred_element_type=jnp.float32)


def norm_forward(values, gain_vector, shift_vector, row_reduce):
    row_mean = row_reduce(jnp.sum(values, axis=1)) / D
    center = values - row_mean[:, None]
    spread = row_reduce(jnp.sum(center * center, axis=1)) / D
    inverse = lax.rsqrt(spread + EPSILON)
    normal_rows = center * inverse[:, None]
    return (normal_rows * gain_vector + shift_vector, normal_rows, inverse)


def norm_backward(row_grad, normal_rows, inverse, gain_vector, pair_reduce):
    scaled = row_grad * gain_vector
    first_total, second_total = pair_reduce(
        jnp.sum(scaled, axis=1), jnp.sum(scaled * normal_rows, axis=1)
    )
    back_rows = inverse[:, None] * (
        scaled - first_total[:, None] / D - normal_rows * (second_total[:, None] / D)
    )
    return (back_rows, jnp.sum(row_grad * normal_rows, axis=0), jnp.sum(row_grad, axis=0))


def attend(query_rows, key_rows, value_rows):
    head_count = query_rows.shape[1] // HEAD_DIM
    image_shape = (query_rows.shape[0] // SEQ, SEQ, head_count, HEAD_DIM)

    def one_image(blocks):
        query_img, key_img, value_img = blocks
        scores = jnp.einsum(
            "qhd,khd->hqk", query_img, key_img, preferred_element_type=jnp.float32
        ) * HEAD_DIM ** (-0.5)
        largest = jnp.max(scores, axis=2, keepdims=True)
        exponent = jnp.exp(scores - largest)
        totals = jnp.sum(exponent, axis=2, keepdims=True)
        weights = (exponent / totals).astype(jnp.bfloat16)
        mixture = jnp.einsum("hqk,khd->qhd", weights, value_img, preferred_element_type=jnp.float32)
        return (mixture.astype(jnp.bfloat16), largest[:, :, 0] + jnp.log(totals[:, :, 0]))

    mixture, logsum = lax.map(
        one_image,
        (
            query_rows.reshape(image_shape),
            key_rows.reshape(image_shape),
            value_rows.reshape(image_shape),
        ),
    )
    return (mixture.reshape(query_rows.shape), logsum)


def attend_back(query_rows, key_rows, value_rows, logsum, mixture_grad):
    head_count = query_rows.shape[1] // HEAD_DIM
    image_shape = (query_rows.shape[0] // SEQ, SEQ, head_count, HEAD_DIM)

    def one_image(blocks):
        query_img, key_img, value_img, logsum_img, grad_img = blocks
        scores = jnp.einsum(
            "qhd,khd->hqk", query_img, key_img, preferred_element_type=jnp.float32
        ) * HEAD_DIM ** (-0.5)
        probability = jnp.exp(scores - logsum_img[:, :, None])
        weights = probability.astype(jnp.bfloat16)
        value_grad = jnp.einsum(
            "hqk,qhd->khd", weights, grad_img, preferred_element_type=jnp.float32
        )
        prob_grad = jnp.einsum(
            "qhd,khd->hqk", grad_img, value_img, preferred_element_type=jnp.float32
        )
        score_grad = probability * (
            prob_grad - jnp.sum(prob_grad * probability, axis=2, keepdims=True)
        )
        score_grad = score_grad.astype(jnp.bfloat16)
        query_grad = jnp.einsum(
            "hqk,khd->qhd", score_grad, key_img, preferred_element_type=jnp.float32
        ) * HEAD_DIM ** (-0.5)
        key_grad = jnp.einsum(
            "hqk,qhd->khd", score_grad, query_img, preferred_element_type=jnp.float32
        ) * HEAD_DIM ** (-0.5)
        return (
            query_grad.astype(jnp.bfloat16),
            key_grad.astype(jnp.bfloat16),
            value_grad.astype(jnp.bfloat16),
        )

    query_grad, key_grad, value_grad = lax.map(
        one_image,
        (
            query_rows.reshape(image_shape),
            key_rows.reshape(image_shape),
            value_rows.reshape(image_shape),
            logsum,
            mixture_grad.reshape(image_shape),
        ),
    )
    return (
        query_grad.reshape(query_rows.shape),
        key_grad.reshape(query_rows.shape),
        value_grad.reshape(query_rows.shape),
    )


def gelu_grad(hidden_pre, hidden_grad):
    unused, pullback = jax.vjp(partial(jax.nn.gelu, approximate=False), hidden_pre)
    return pullback(hidden_grad)[0]


def layer_body(*args):
    (
        layer_input,
        output_grad,
        first_gain,
        first_shift,
        query_weight,
        key_weight,
        value_weight,
        query_bias,
        value_bias,
        out_weight,
        out_bias,
        second_gain,
        second_shift,
        up_weight,
        up_bias,
        down_weight,
        down_bias,
    ) = args
    width = first_gain.shape[0]
    head = query_bias.shape[0]
    feed = up_bias.shape[0]
    rows_in = lax.all_to_all(layer_input, "gy", split_axis=0, concat_axis=1, tiled=True)
    joined = assemble(jnp.stack([query_weight, key_weight, value_weight]), "gy")
    wide = spread_vector(
        jnp.concatenate([first_gain, first_shift, out_bias, second_gain, second_shift, down_bias]), "gy"
    ).reshape(-1, 6, width)
    gain_one, shift_one, bias_out, gain_two, shift_two, bias_down = (
        wide[:, i].reshape(-1) for i in range(6)
    )
    tall = spread_vector(jnp.concatenate([query_bias, value_bias, up_bias]), "gx")
    bias_query = tall[:, :head].reshape(-1)
    bias_value = tall[:, head : 2 * head].reshape(-1)
    bias_up = tall[:, 2 * head :].reshape(-1)
    cotangent = lax.all_to_all(output_grad, "gy", split_axis=0, concat_axis=1, tiled=True)
    out_whole = assemble(out_weight[None], "gx")[0]
    up_whole = assemble(up_weight[None], "gy")[0]
    down_whole = assemble(down_weight[None], "gx")[0]

    same = lambda v: v
    pair = lambda a, b: (a, b)
    inputs = rows_in.astype(F32)
    normed, normal_one, inverse_one = norm_forward(inputs, gain_one, shift_one, same)
    normed = normed.astype(BF16)
    query = (product(normed, joined[0], 0) + bias_query).astype(BF16)
    key = product(normed, joined[1], 0).astype(BF16)
    value = (product(normed, joined[2], 0) + bias_value).astype(BF16)
    mixture, logsum = attend(query, key, value)
    middle = inputs + (product(mixture, out_whole, 0) + bias_out)
    normed_two, normal_two, inverse_two = norm_forward(middle, gain_two, shift_two, same)
    normed_two = normed_two.astype(BF16)
    hidden_pre = product(normed_two, up_whole, 0) + bias_up
    hidden = jax.nn.gelu(hidden_pre, approximate=False).astype(BF16)
    result = (middle + (product(hidden, down_whole, 0) + bias_down)).astype(BF16)
    down_grad = row_product(hidden, cotangent)
    down_bias_grad = jnp.sum(cotangent.astype(F32), axis=0)
    hidden_grad = product(cotangent, down_whole, 1)
    pre_grad = gelu_grad(hidden_pre, hidden_grad).astype(BF16)
    up_bias_grad = jnp.sum(pre_grad.astype(F32), axis=0)
    up_grad = row_product(normed_two, pre_grad)
    normed_two_grad = product(pre_grad, up_whole, 1)
    back_two, gain_two_grad, shift_two_grad = norm_backward(
        normed_two_grad, normal_two, inverse_two, gain_two, pair
    )
    middle_grad = cotangent.astype(F32) + back_two
    branch_grad = middle_grad.astype(BF16)
    out_bias_grad = jnp.sum(branch_grad.astype(F32), axis=0)
    out_grad = row_product(mixture, branch_grad)
    mixture_grad = product(branch_grad, out_whole, 1).astype(BF16)
    query_grad, key_grad, value_grad = attend_back(query, key, value, logsum, mixture_grad)
    query_bias_grad = jnp.sum(query_grad.astype(F32), axis=0)
    value_bias_grad = jnp.sum(value_grad.astype(F32), axis=0)
    joined_grad = jnp.stack([row_product(normed, g) for g in (query_grad, key_grad, value_grad)])
    normed_grad = (
        product(query_grad, joined[0], 1) + product(key_grad, joined[1], 1) + product(value_grad, joined[2], 1)
    )
    back_one, gain_one_grad, shift_one_grad = norm_backward(
        normed_grad, normal_one, inverse_one, gain_one, pair
    )
    input_grad = (middle_grad + back_one).astype(BF16)

    result = lax.all_to_all(result, "gy", split_axis=1, concat_axis=0, tiled=True)
    input_grad = lax.all_to_all(input_grad, "gy", split_axis=1, concat_axis=0, tiled=True)
    down_block = scatter_sum(down_grad[None], "gx")[0]
    up_block = scatter_sum(up_grad[None], "gy")[0]
    out_block = scatter_sum(out_grad[None], "gx")[0]
    joined_block = scatter_sum(joined_grad, "gy")

    packed = jnp.concatenate(
        [
            gain_one_grad,
            shift_one_grad,
            out_bias_grad,
            gain_two_grad,
            shift_two_grad,
            down_bias_grad,
            query_bias_grad,
            value_bias_grad,
            up_bias_grad,
        ]
    )
    packed = lax.psum(packed, AXES)
    mine = lax.axis_index("gy")
    wide_grads = [
        lax.dynamic_slice_in_dim(packed, i * D + mine * width, width) for i in range(6)
    ]
    tall_index = lax.axis_index("gx")
    query_bias_grad = lax.dynamic_slice_in_dim(packed, 6 * D + tall_index * head, head)
    value_bias_grad = lax.dynamic_slice_in_dim(packed, 7 * D + tall_index * head, head)
    up_bias_grad = lax.dynamic_slice_in_dim(packed, 8 * D + tall_index * feed, feed)
    return (
        result,
        input_grad,
        wide_grads[0],
        wide_grads[1],
        joined_block[0],
        joined_block[1],
        joined_block[2],
        query_bias_grad,
        value_bias_grad,
        out_block,
        wide_grads[2],
        wide_grads[3],
        wide_grads[4],
        up_block,
        up_bias_grad,
        down_block,
        wide_grads[5],
    )


def solution(mesh):
    tokens = P(("dp", "gx"), "gy")
    wide, tall = P("gy"), P("gx")
    down_rows, across = P("gy", "gx"), P("gx", "gy")
    params = (
        wide, wide, down_rows, down_rows, down_rows, tall, tall, across, wide,
        wide, wide, down_rows, tall, across, wide,
    )
    return jax.shard_map(
        layer_body,
        mesh=mesh,
        in_specs=(tokens, tokens) + params,
        out_specs=(tokens, tokens) + params,
        check_vma=False,
    )
```

```python
import jax
import jax.numpy as jnp
from jax import lax
from jax.experimental import pallas as pl
from jax.experimental.pallas import tpu as pltpu
from jax.sharding import PartitionSpec as P

D = 1024
HEAD_DIM = 64
SEQ = 577
EPSILON = 1e-06
F32 = jnp.float32
BF16 = jnp.bfloat16

CELL = 256
NT = (((1,), (1,)), ((), ()))
TN = (((0,), (0,)), ((), ()))
ANY = pl.BlockSpec(memory_space=pl.ANY)
WHOLE = pl.BlockSpec(memory_space=pltpu.VMEM)
SMEM = pl.BlockSpec(memory_space=pltpu.SMEM)
LIMIT = 32 * 1024 * 1024
FEED_LIMIT = 40 * 1024 * 1024


def dot(left, right, dims=(((1,), (0,)), ((), ()))):
    return lax.dot_general(left, right, dims, preferred_element_type=F32)


def cost(flops, moved, transcendentals=0):
    return pl.CostEstimate(flops=flops, bytes_accessed=moved, transcendentals=transcendentals)


AXES = ("dp", "gx", "gy")


def swap(value, axis, step):
    return lax.ppermute(value, axis, [(i, i ^ step) for i in range(lax.axis_size(axis))])


def shifted(offsets, axis, step):
    place = AXES.index(axis)
    return [o[:place] + (o[place] ^ step,) + o[place + 1 :] for o in offsets]


def doubled(pieces, offsets, axis, step):
    return (
        jnp.concatenate([pieces, swap(pieces, axis, step)], axis=0),
        offsets + shifted(offsets, axis, step),
    )


class Gather:
    orders = ((("gx", 1), ("dp", 2)), (("dp", 2), ("gx", 1)))

    def __init__(self, cells, place):
        self.place = place
        self.arrays = [lax.dynamic_index_in_dim(cells, lax.axis_index("dp"), 0)]
        self.offsets = [[(0, 0, 0)]]

    def z(self, step):
        got, offsets = doubled(self.arrays[0], self.offsets[0], "gy", step)
        self.arrays, self.offsets = [got], [offsets]

    def xy(self, turn):
        if turn == 0:
            self.arrays = [self.arrays[0][:, half] for half in range(2)]
            self.offsets = self.offsets * 2
            for half in range(2):
                self.arrays[half], self.offsets[half] = doubled(
                    self.arrays[half], self.offsets[half], *self.orders[half][turn]
                )
        else:
            self.arrays = self.arrays + [swap(self.arrays[half], *self.orders[half][turn]) for half in range(2)]
            self.offsets = self.offsets + [shifted(self.offsets[half], *self.orders[half][turn]) for half in range(2)]

    def core(self):
        self.arrays = self.arrays + [swap(a, "dp", 1) for a in self.arrays]
        self.offsets = self.offsets + [shifted(o, "dp", 1) for o in self.offsets]

    def bundles(self, part=slice(None)):
        parts = [(a, o, i % 2) for i, (a, o) in enumerate(zip(self.arrays, self.offsets))]
        return Bundles(self.place, parts[part])


def fold(value, dim, bit, axis, step):
    kept = lax.dynamic_index_in_dim(value, bit, dim, keepdims=False)
    sent = lax.dynamic_index_in_dim(value, 1 - bit, dim, keepdims=False)
    return (kept.astype(F32) + swap(sent, axis, step).astype(F32)).astype(BF16)


class Scatter:
    def __init__(self, place, theirs):
        self.place = place
        self.share, self.x_at, self.z_at = (lax.axis_index(a) for a in AXES)
        self.arrays = [theirs]

    def core(self):
        self.arrays = [swap(self.arrays[0], "dp", 1)]

    def split(self, mine):
        self.arrays = list(add_split(self.place, mine, self.arrays[0]))

    def xy(self, turn):
        high = self.share >> 1
        if turn == 0:
            kept_a, sent_a, kept_b, sent_b = self.arrays
            got_a, got_b = swap(sent_a, "dp", 2), swap(sent_b, "gx", 1)
            add = lambda u, v: (u.astype(F32) + v.astype(F32)).astype(BF16)
            self.arrays = [add(kept_a, got_a), add(kept_b, got_b)]
        else:
            first, second = self.arrays
            first, second = fold(first, 0, self.x_at, "gx", 1), fold(second, 0, high, "dp", 2)
            self.arrays = [jnp.stack([first, second]).reshape(1, 2, 2, 2, CELL, CELL)]

    def z(self, step):
        dim, bit = (3, self.z_at & 1) if step == 1 else (2, self.z_at >> 1)
        self.arrays = [fold(self.arrays[0], dim, bit, "gy", step)]

    def spread(self, step):
        both = self.arrays[0]
        other = swap(both, "dp", step)
        if step == 2:
            bit = self.share >> 1
            self.arrays = [jnp.stack([jnp.where(bit == 0, both, other), jnp.where(bit == 0, other, both)], axis=1)]
        else:
            self.arrays = [both, other]


def merged(first, second):
    both = Scatter(first.place, None)
    both.arrays = [jnp.concatenate([first.arrays[0], second.arrays[0]])]
    return both


def add_split(place, mine, got):
    block = (1, 1, 1, 4, CELL, CELL)
    flip = lambda bit, sent: 1 - bit if sent else bit
    over_dp = lambda sent: lambda j, p: (flip(p[0] >> 1, sent), 0, j, 0, 0, 0)
    over_gx = lambda sent: lambda j, p: (j, 1, flip(p[1], sent), 0, 0, 0)
    maps = [over_dp(0), over_dp(1), over_gx(0), over_gx(1)]

    def kernel(place, *refs):
        for i in range(4):
            refs[8 + i][0] = (refs[i][0, 0, 0].astype(F32) + refs[4 + i][0, 0, 0].astype(F32)).astype(BF16)

    return pl.pallas_call(
        kernel,
        grid_spec=pltpu.PrefetchScalarGridSpec(
            num_scalar_prefetch=1,
            grid=(2,),
            in_specs=[pl.BlockSpec(block, f) for f in maps] * 2,
            out_specs=[pl.BlockSpec((1, 4, CELL, CELL), lambda j, p: (j, 0, 0, 0))] * 4,
        ),
        out_shape=[jax.ShapeDtypeStruct((2, 4, CELL, CELL), BF16)] * 4,
        compiler_params=pltpu.CompilerParams(vmem_limit_bytes=24 * 1024 * 1024),
        cost_estimate=cost(0, 2 * 3 * 32 * CELL * CELL),
        name="add_split",
    )(place, mine, mine, mine, mine, got, got, got, got)


def pin(chains, *values):
    arrays = [c.arrays for c in chains]
    values, arrays = lax.optimization_barrier((values, arrays))
    for c, held in zip(chains, arrays):
        c.arrays = list(held)
    return values[0] if len(values) == 1 else values


def spread_vector(vector, axis):
    size = lax.axis_size(axis)
    pieces, offsets = vector[None], [0]
    step = size >> 1
    while step:
        pieces = jnp.concatenate([pieces, swap(pieces, axis, step)], axis=0)
        offsets = offsets + [o ^ step for o in offsets]
        step >>= 1
    index = lax.axis_index(axis)
    wanted = jnp.arange(size)[:, None]
    total = jnp.zeros((size, vector.shape[0]), F32)
    for i, offset in enumerate(offsets):
        total = total + jnp.where(wanted == (index ^ offset), pieces[i][None].astype(F32), 0.0)
    return total


def part_rows(place, block):
    parts = 4
    rows = block.shape[0] // parts

    def kernel(place, x_ref, *refs):
        buf = refs[parts]
        for z in range(parts):
            buf[z] = x_ref[z * rows : (z + 1) * rows, :]
        for k in range(parts):
            refs[k][...] = buf[place[2] ^ k]

    return pl.pallas_call(
        kernel,
        in_specs=[SMEM, WHOLE],
        out_specs=[WHOLE] * parts,
        out_shape=[jax.ShapeDtypeStruct((rows, block.shape[1]), BF16)] * parts,
        scratch_shapes=[pltpu.VMEM((parts, rows, block.shape[1]), BF16)],
        compiler_params=pltpu.CompilerParams(vmem_limit_bytes=24 * 1024 * 1024),
        cost_estimate=cost(0, 4 * block.size),
        name="part_rows",
    )(place, block)


def unite_rows(place, pieces):
    parts = len(pieces)
    rows, cols = pieces[0].shape

    def kernel(place, *refs):
        out, buf = refs[parts], refs[parts + 1]
        for k in range(parts):
            buf[place[2] ^ k] = refs[k][...]
        for z in range(parts):
            out[z * rows : (z + 1) * rows, :] = buf[z]

    return pl.pallas_call(
        kernel,
        in_specs=[SMEM] + [WHOLE] * parts,
        out_specs=WHOLE,
        out_shape=jax.ShapeDtypeStruct((parts * rows, cols), BF16),
        scratch_shapes=[pltpu.VMEM((parts, rows, cols), BF16)],
        compiler_params=pltpu.CompilerParams(vmem_limit_bytes=24 * 1024 * 1024),
        cost_estimate=cost(0, 4 * parts * rows * cols),
        name="unite_rows",
    )(place, *pieces)


def exchange(pieces):
    return [swap(p, "gy", k) if k else p for k, p in enumerate(pieces)]


def whole_weight(block, rows_axis, cols_axis):
    return lax.all_gather(lax.all_gather(block, rows_axis, axis=0, tiled=True), cols_axis, axis=1, tiled=True)


def weight_block(grad, rows_axis, cols_axis):
    part = lax.psum_scatter(grad, rows_axis, scatter_dimension=0, tiled=True)
    return lax.psum(lax.psum_scatter(part, cols_axis, scatter_dimension=1, tiled=True), "dp")


def projection_cells(weight):
    return weight.reshape(4, CELL, 2, 2, CELL).transpose(3, 2, 0, 1, 4)


def out_cells(weight):
    return weight.reshape(2, 2, CELL, 4, CELL).transpose(1, 0, 3, 2, 4)


def up_cells(weight):
    return weight.reshape(4, CELL, 2, 2, 2, 2, CELL).transpose(3, 4, 5, 2, 0, 1, 6)


def down_cells(weight):
    return weight.reshape(2, 2, 2, 2, CELL, 4, CELL).transpose(1, 2, 3, 0, 5, 4, 6)


def whole_bundles(cells, place, low=None):
    shares = range(4) if low is None else (low, low + 2)
    offsets = [(d, x, z) for d in shares for x in range(2) for z in range(4)]
    return Bundles(place, [(cells[:, half].reshape(-1, CELL, CELL), offsets, half) for half in range(2)])


def whole_shares(mine, theirs):
    return jnp.stack([mine, theirs], axis=1).reshape((4,) + mine.shape[1:])


class Bundles:
    def __init__(self, place, parts):
        self.place = place
        self.arrays = [p[0] for p in parts]
        self.meta = [(p[1], p[2]) for p in parts]

    def start(self, place_ref, refs, put):
        for ref, (offsets, half) in zip(refs, self.meta):
            for i, (od, ox, oz) in enumerate(offsets):
                put(ref.at[i], place_ref[0] ^ od, half, place_ref[1] ^ ox, place_ref[2] ^ oz)


def window(ref, row, col):
    return ref.at[pl.ds(pl.multiple_of(row, CELL), CELL), pl.ds(pl.multiple_of(col, CELL), CELL)]


def put_projections(weights, sems):
    def put(source, share, half, x, z):
        @pl.when(share < 3)
        def _():
            dest = window(weights.at[share], z * CELL, (2 * x + half) * CELL)
            pltpu.make_async_copy(source, dest, sems.at[share]).start()

    return put


def put_out(weight, sem):
    def put(source, share, half, x, z):
        @pl.when(share == 3)
        def _():
            pltpu.make_async_copy(source, window(weight, (2 * x + half) * CELL, z * CELL), sem).start()

    return put


def put_feed(up, down, sems):
    def put(source, share, half, x, z):
        at = (2 * x + half) * CELL

        @pl.when(share < 2)
        def _():
            pltpu.make_async_copy(source, window(up, z * CELL, at), sems.at[0]).start()

        @pl.when(share >= 2)
        def _():
            pltpu.make_async_copy(source, window(down, at, z * CELL), sems.at[1]).start()

    return put


def wait_all(ref, sem):
    pltpu.make_async_copy(ref, ref, sem).wait()


def normal(values):
    center = values - jnp.mean(values, axis=1, keepdims=True)
    inverse = lax.rsqrt(jnp.mean(center * center, axis=1, keepdims=True) + EPSILON)
    return center * inverse, inverse


def back_norm(grad, normal_rows, inverse, gain):
    scaled = grad * gain
    mean_one = jnp.mean(scaled, axis=1, keepdims=True)
    mean_two = jnp.mean(scaled * normal_rows, axis=1, keepdims=True)
    return inverse * (scaled - mean_one - normal_rows * mean_two)


def column_sum(values):
    return jnp.sum(values, axis=0, keepdims=True)


def project(pieces, vectors, bundles):
    rows = pieces[0].shape[0]
    count = len(bundles.arrays)
    parts = len(pieces)
    cols = pieces[0].shape[1]

    def kernel(place, vec, *refs):
        xs, sources = refs[:parts], refs[parts : parts + count]
        q_ref, x_ref, nt_ref, weights, xbuf, n_ref, sems = refs[parts + count :]
        step = pl.program_id(0)

        @pl.when(step == 0)
        def _():
            bundles.start(place, sources, put_projections(weights, sems))
            for k in range(parts):
                xbuf[place[2] ^ k] = xs[k][...]
            x = jnp.concatenate([xbuf[k] for k in range(parts)], axis=1)
            x_ref[...] = x
            normal_rows, _ = normal(x.astype(F32))
            normed = (normal_rows * vec[0:1, :] + vec[1:2, :]).astype(BF16)
            n_ref[...] = normed
            nt_ref[...] = normed.T

        for share in range(3):

            @pl.when(step == share)
            def _():
                wait_all(weights.at[share], sems.at[share])
                total = dot(n_ref[...], weights[share])
                if share != 1:
                    total = total + vec[2 + share // 2 : 3 + share // 2, :]
                q_ref[0] = total.astype(BF16)

    full = jax.ShapeDtypeStruct((rows, D), BF16)
    return pl.pallas_call(
        kernel,
        grid=(3,),
        in_specs=[SMEM, WHOLE] + [WHOLE] * parts + [ANY] * count,
        out_specs=[pl.BlockSpec((1, rows, D), lambda s: (s, 0, 0)), WHOLE, WHOLE],
        out_shape=[jax.ShapeDtypeStruct((3, rows, D), BF16), full, jax.ShapeDtypeStruct((D, rows), BF16)],
        scratch_shapes=[
            pltpu.VMEM((3, D, D), BF16),
            pltpu.VMEM((parts, rows, cols), BF16),
            pltpu.VMEM((rows, D), BF16),
            pltpu.SemaphoreType.DMA((3,)),
        ],
        compiler_params=pltpu.CompilerParams(vmem_limit_bytes=LIMIT),
        cost_estimate=cost(6 * rows * D * D, 6 * D * D + 12 * rows * D),
        name="project",
    )(bundles.place, vectors, *pieces, *bundles.arrays)


def attend(qkv, begin, end):
    rows = qkv.shape[1]
    pairs = end - begin

    def kernel(q_ref, k_ref, v_ref, o_ref, lse_ref, buf):
        q, k, v = q_ref[0], k_ref[0], v_ref[0]
        first = lax.broadcasted_iota(jnp.int32, (1, 128), 1) < 64
        scale = HEAD_DIM**-0.5
        outs = []
        for h in range(2):
            mine = first if h == 0 else jnp.logical_not(first)
            qh = jnp.where(mine, q.astype(F32) * scale, 0.0).astype(BF16)
            s = dot(qh, k, NT)
            top = jnp.max(s, axis=1, keepdims=True)
            p = jnp.exp(s - top)
            total = jnp.sum(p, axis=1, keepdims=True)
            outs.append(dot(p.astype(BF16), v) / total)
            buf[0:rows, h : h + 1] = top + jnp.log(total)
        o_ref[...] = jnp.where(first, outs[0], outs[1]).astype(BF16)
        lse_ref[0] = buf[...].T[0:8, 0:rows]

    spec = lambda i: pl.BlockSpec((1, rows, 128), lambda s, i=i: (i, 0, s + begin))
    return pl.pallas_call(
        kernel,
        grid=(pairs,),
        in_specs=[spec(0), spec(1), spec(2)],
        out_specs=[pl.BlockSpec((rows, 128), lambda s: (0, s)), pl.BlockSpec((1, 8, rows), lambda s: (s, 0, 0))],
        out_shape=[
            jax.ShapeDtypeStruct((rows, pairs * 128), BF16),
            jax.ShapeDtypeStruct((pairs, 8, rows), F32),
        ],
        scratch_shapes=[pltpu.VMEM((640, 128), F32)],
        compiler_params=pltpu.CompilerParams(vmem_limit_bytes=LIMIT),
        cost_estimate=cost(2048 * pairs * rows * rows, 1024 * pairs * rows, 2 * pairs * rows * rows),
        name="attend",
    )(qkv, qkv, qkv)


def attend_back(qkv, mixture, lse, mixture_grad, begin, end):
    rows = qkv.shape[1]
    pairs = end - begin

    def kernel(q_ref, k_ref, v_ref, o_ref, lse_ref, do_ref, g_ref, b_ref):
        q, k, v, grad = q_ref[0], k_ref[0], v_ref[0], do_ref[...]
        first = lax.broadcasted_iota(jnp.int32, (1, 128), 1) < 64
        scale = HEAD_DIM**-0.5
        pick = lax.broadcasted_iota(jnp.int32, (8, 128), 0) == lax.broadcasted_iota(jnp.int32, (8, 128), 1) // 64
        product = grad.astype(F32) * o_ref[...].astype(F32)
        delta = lax.dot_general(
            jnp.where(pick, 1.0, 0.0), product, NT, precision=lax.Precision.HIGHEST, preferred_element_type=F32
        )
        dqs, dks, dvs = [], [], []
        for h in range(2):
            mine = first if h == 0 else jnp.logical_not(first)
            qh = jnp.where(mine, q.astype(F32) * scale, 0.0).astype(BF16)
            gh = jnp.where(mine, grad, jnp.zeros_like(grad))
            p = jnp.exp(dot(k, qh, NT) - lse_ref[0, h : h + 1, :])
            dp = dot(v, gh, NT)
            ds = (p * (dp - delta[h : h + 1, :])).astype(BF16)
            dvs.append(dot(p.astype(BF16), grad))
            dks.append(dot(ds, q))
            dqs.append(dot(k, ds, TN))
        dq = (jnp.concatenate([dqs[0][:64], dqs[1][64:]], axis=0) * scale).T.astype(BF16)
        dk = (jnp.where(first, dks[0], dks[1]) * scale).astype(BF16)
        dv = jnp.where(first, dvs[0], dvs[1]).astype(BF16)
        g_ref[0], g_ref[1], g_ref[2] = dq, dk, dv
        b_ref[0:1, :] = column_sum(dq.astype(F32))
        b_ref[1:2, :] = column_sum(dv.astype(F32))

    spec = lambda i: pl.BlockSpec((1, rows, 128), lambda s, i=i: (i, 0, s + begin))
    flat = pl.BlockSpec((rows, 128), lambda s: (0, s))
    wide = pl.BlockSpec((rows, 128), lambda s: (0, s + begin))
    return pl.pallas_call(
        kernel,
        grid=(pairs,),
        in_specs=[spec(0), spec(1), spec(2), flat, pl.BlockSpec((1, 8, rows), lambda s: (s, 0, 0)), wide],
        out_specs=[pl.BlockSpec((3, rows, 128), lambda s: (0, 0, s)), pl.BlockSpec((8, 128), lambda s: (0, s))],
        out_shape=[
            jax.ShapeDtypeStruct((3, rows, pairs * 128), BF16),
            jax.ShapeDtypeStruct((8, pairs * 128), F32),
        ],
        compiler_params=pltpu.CompilerParams(vmem_limit_bytes=LIMIT),
        cost_estimate=cost(6000 * pairs * rows * rows, 2048 * pairs * rows, 2 * pairs * rows * rows),
        name="attend_back",
    )(qkv, qkv, qkv, mixture, lse, mixture_grad)


def mix_out(mixtures, inputs, vectors, bundles):
    rows = inputs.shape[0]
    count = len(bundles.arrays)

    def kernel(place, vec, m_ref, o_ref, x_ref, *refs):
        sources = refs[:count]
        mid_ref, n_ref, nt_ref, weight, sem = refs[count:]
        bundles.start(place, sources, put_out(weight, sem))
        wait_all(weight, sem)
        mixture = jnp.concatenate([m_ref[...], o_ref[...]], axis=1)
        middle = x_ref[...].astype(F32) + (dot(mixture, weight[...]) + vec[4:5, :])
        mid_ref[...] = middle
        normal_rows, _ = normal(middle)
        normed = (normal_rows * vec[5:6, :] + vec[6:7, :]).astype(BF16)
        n_ref[...] = normed
        nt_ref[...] = normed.T

    return pl.pallas_call(
        kernel,
        in_specs=[SMEM] + [WHOLE] * 4 + [ANY] * count,
        out_specs=[WHOLE] * 3,
        out_shape=[
            jax.ShapeDtypeStruct((rows, D), F32),
            jax.ShapeDtypeStruct((rows, D), BF16),
            jax.ShapeDtypeStruct((D, rows), BF16),
        ],
        scratch_shapes=[pltpu.VMEM((D, D), BF16), pltpu.SemaphoreType.DMA],
        compiler_params=pltpu.CompilerParams(vmem_limit_bytes=LIMIT),
        cost_estimate=cost(2 * rows * D * D, 2 * D * D + 10 * rows * D),
        name="mix_out",
    )(bundles.place, vectors, *mixtures, inputs, *bundles.arrays)


def gelu_pair(h):
    below = 0.5 * (1.0 + lax.erf(h * 0.7071067811865476))
    bell = jnp.exp(h * h * -0.5) * 0.3989422804014327
    return h * below, below + h * bell


def feed(normed, normed_t, cotangent, cotangent_t, up_bias, bundles, partials, other):
    rows = normed.shape[0]
    count = len(bundles.arrays)
    tile = 2 * CELL
    carried = 0 if partials is None else 2

    def kernel(place, bias, n_ref, nt_ref, g_ref, gt_ref, *refs):
        olds, sources = refs[:carried], refs[carried : carried + count]
        out_acc, back_acc, cells, bias_ref, up, down, sems = refs[carried + count :]
        step = pl.program_id(0)
        core = place[0] & 1
        sub = 1 - core if other else core

        @pl.when(step == 0)
        def _():
            bundles.start(place, sources, put_feed(up, down, sems))
            for acc, old in zip((out_acc, back_acc), olds):
                acc[...] = old[...]
            if not carried:
                out_acc[...] = jnp.zeros_like(out_acc)
                back_acc[...] = jnp.zeros_like(back_acc)
            wait_all(up, sems.at[0])
            wait_all(down, sems.at[1])

        at = pl.multiple_of(step * tile, tile)
        bias_at = pl.multiple_of((2 * step + sub) * tile, tile)
        up_tile = up[:, pl.ds(at, tile)]
        down_tile = down[pl.ds(at, tile), :]
        pre = dot(n_ref[...], up_tile) + bias[0:1, pl.ds(bias_at, tile)]
        hidden, slope = gelu_pair(pre)
        hidden = hidden.astype(BF16)
        out_acc[...] += dot(hidden, down_tile)
        pre_grad = (dot(g_ref[...], down_tile, NT) * slope).astype(BF16)
        back_acc[...] += dot(pre_grad, up_tile, NT)
        bias_ref[0] = column_sum(pre_grad.astype(F32))
        for i, grad in enumerate((dot(nt_ref[...], pre_grad), dot(gt_ref[...], hidden))):
            grad = grad.astype(BF16)
            for half in range(2):
                for z in range(4):
                    cells[i, half, 0, z] = grad[z * CELL : (z + 1) * CELL, half * CELL : (half + 1) * CELL]

    acc = jax.ShapeDtypeStruct((rows, D), F32)
    return pl.pallas_call(
        kernel,
        grid=(2,),
        in_specs=[SMEM] + [WHOLE] * (5 + carried) + [ANY] * count,
        out_specs=[
            WHOLE,
            WHOLE,
            pl.BlockSpec((2, 2, 1, 4, CELL, CELL), lambda s: (0, 0, s, 0, 0, 0)),
            pl.BlockSpec((1, 1, tile), lambda s: (s, 0, 0)),
        ],
        out_shape=[
            acc,
            acc,
            jax.ShapeDtypeStruct((2, 2, 2, 4, CELL, CELL), BF16),
            jax.ShapeDtypeStruct((2, 1, tile), F32),
        ],
        scratch_shapes=[
            pltpu.VMEM((D, 2 * tile), BF16),
            pltpu.VMEM((2 * tile, D), BF16),
            pltpu.SemaphoreType.DMA((2,)),
        ],
        compiler_params=pltpu.CompilerParams(vmem_limit_bytes=FEED_LIMIT),
        cost_estimate=cost(24 * rows * D * tile, 16 * D * tile + 28 * rows * D, 4 * rows * tile),
        name="feed",
    )(
        bundles.place,
        up_bias,
        normed,
        normed_t,
        cotangent,
        cotangent_t,
        *([] if partials is None else partials),
        *bundles.arrays,
    )


def turn(middle, cotangent, out_sum, back_sum, vectors, bundles):
    rows = middle.shape[0]
    count = len(bundles.arrays)
    parts = 4

    def kernel(place, vec, mid_ref, g_ref, out_ref, back_ref, *refs):
        sources = refs[:count]
        pieces = refs[count : count + parts]
        grad_ref, branch_t, mix_ref, sum_ref, weight, cols, sem = refs[count + parts :]
        bundles.start(place, sources, put_out(weight, sem))
        middle = mid_ref[...]
        result = (middle + (out_ref[...] + vec[7:8, :])).astype(BF16)
        for k in range(parts):
            cols[k] = result[:, k * CELL : (k + 1) * CELL]
        for k in range(parts):
            pieces[k][...] = cols[place[2] ^ k]
        normal_rows, inverse = normal(middle)
        back = back_ref[...]
        grads = g_ref[...].astype(F32)
        middle_grad = grads + back_norm(back, normal_rows, inverse, vec[5:6, :])
        grad_ref[...] = middle_grad
        branch = middle_grad.astype(BF16)
        branch_t[...] = branch.T
        sum_ref[0:1, :] = column_sum(branch.astype(F32))
        sum_ref[1:2, :] = column_sum(back * normal_rows)
        sum_ref[2:3, :] = column_sum(back)
        sum_ref[3:4, :] = column_sum(grads)
        wait_all(weight, sem)
        mix_ref[...] = dot(branch, weight[...], NT).astype(BF16)

    full = jax.ShapeDtypeStruct((rows, D), BF16)
    return pl.pallas_call(
        kernel,
        in_specs=[SMEM] + [WHOLE] * 5 + [ANY] * count,
        out_specs=[WHOLE] * (parts + 4),
        out_shape=[jax.ShapeDtypeStruct((rows, CELL), BF16)] * parts
        + [
            jax.ShapeDtypeStruct((rows, D), F32),
            jax.ShapeDtypeStruct((D, rows), BF16),
            full,
            jax.ShapeDtypeStruct((8, D), F32),
        ],
        scratch_shapes=[
            pltpu.VMEM((D, D), BF16),
            pltpu.VMEM((parts, rows, CELL), BF16),
            pltpu.SemaphoreType.DMA,
        ],
        compiler_params=pltpu.CompilerParams(vmem_limit_bytes=LIMIT),
        cost_estimate=cost(2 * rows * D * D, 2 * D * D + 24 * rows * D),
        name="turn",
    )(bundles.place, vectors, middle, cotangent, out_sum, back_sum, *bundles.arrays)


def weigh(place, normed_t, branch_t, grads, mixtures, other):
    rows = normed_t.shape[1]

    def kernel(place, n_t, b_t, g0, g1, m0, m1, cells):
        core = place[0] & 1
        share = 2 * pl.program_id(0) + (1 - core if other else core)

        def fill(left, right):
            for x in range(2):
                for half in range(2):
                    grad = dot(left, right(x, half * CELL)).astype(BF16)
                    cells[0, half, x] = grad.reshape(4, CELL, CELL)

        for k in range(3):

            @pl.when(share == k)
            def _():
                fill(n_t[...], lambda x, at: (g0, g1)[x][k, :, at : at + CELL])

        @pl.when(share == 3)
        def _():
            fill(b_t[...], lambda x, at: (m0, m1)[x][:, at : at + CELL])

    return pl.pallas_call(
        kernel,
        grid=(2,),
        in_specs=[SMEM] + [WHOLE] * 6,
        out_specs=pl.BlockSpec((1, 2, 2, 4, CELL, CELL), lambda s: (s, 0, 0, 0, 0, 0)),
        out_shape=jax.ShapeDtypeStruct((2, 2, 2, 4, CELL, CELL), BF16),
        compiler_params=pltpu.CompilerParams(vmem_limit_bytes=LIMIT),
        cost_estimate=cost(4 * rows * D * D, 4 * D * D + 12 * rows * D),
        name="weigh",
    )(place, normed_t, branch_t, *grads, *mixtures)


def finish(inputs, middle_grad, grads, vectors, bundles):
    rows = inputs.shape[0]
    count = len(bundles.arrays)
    parts = 4

    def kernel(place, vec, x_ref, mid_ref, g0, g1, *refs):
        sources = refs[:count]
        pieces = refs[count : count + parts]
        sum_ref, weights, cols, sems = refs[count + parts :]
        bundles.start(place, sources, put_projections(weights, sems))
        normal_rows, inverse = normal(x_ref[...].astype(F32))
        back = None
        for k in range(3):
            wait_all(weights.at[k], sems.at[k])
            term = dot(jnp.concatenate([g0[k], g1[k]], axis=1), weights[k], NT)
            back = term if back is None else back + term
        result = (mid_ref[...] + back_norm(back, normal_rows, inverse, vec[0:1, :])).astype(BF16)
        for k in range(parts):
            cols[k] = result[:, k * CELL : (k + 1) * CELL]
        for k in range(parts):
            pieces[k][...] = cols[place[2] ^ k]
        sum_ref[0:1, :] = column_sum(back * normal_rows)
        sum_ref[1:2, :] = column_sum(back)

    return pl.pallas_call(
        kernel,
        in_specs=[SMEM] + [WHOLE] * 5 + [ANY] * count,
        out_specs=[WHOLE] * (parts + 1),
        out_shape=[jax.ShapeDtypeStruct((rows, CELL), BF16)] * parts + [jax.ShapeDtypeStruct((8, D), F32)],
        scratch_shapes=[
            pltpu.VMEM((3, D, D), BF16),
            pltpu.VMEM((parts, rows, CELL), BF16),
            pltpu.SemaphoreType.DMA((3,)),
        ],
        compiler_params=pltpu.CompilerParams(vmem_limit_bytes=LIMIT),
        cost_estimate=cost(6 * rows * D * D, 6 * D * D + 14 * rows * D),
        name="finish",
    )(bundles.place, vectors, inputs, middle_grad, *grads, *bundles.arrays)


def unpack_projections(place, own, other):
    def kernel(place, a_ref, b_ref, *refs):
        outs, buf = refs[:4], refs[4]
        core = place[0] & 1
        buf[core] = a_ref[...]
        buf[1 - core] = b_ref[...]
        for share in range(4):
            for half in range(2):
                cell = buf[share % 2, share // 2, half]
                at = slice(half * CELL, (half + 1) * CELL)
                if share < 3:
                    outs[share][:, at] = cell.astype(F32)
                else:
                    outs[share][at, :] = cell.astype(F32).T

    tall, wide = (jax.ShapeDtypeStruct(s, F32) for s in ((2 * CELL, CELL), (CELL, 2 * CELL)))
    return pl.pallas_call(
        kernel,
        in_specs=[SMEM, WHOLE, WHOLE],
        out_specs=[WHOLE] * 4,
        out_shape=[wide, wide, wide, tall],
        scratch_shapes=[pltpu.VMEM((2, 2, 2, CELL, CELL), BF16)],
        compiler_params=pltpu.CompilerParams(vmem_limit_bytes=LIMIT),
        cost_estimate=cost(0, 3 * 16 * CELL * CELL),
        name="unpack_projections",
    )(place, own, other)


def unpack_feed(place, own, other):
    def kernel(place, a_ref, b_ref, up_ref, down_ref, buf):
        core = place[0] & 1
        buf[core] = a_ref[...]
        buf[1 - core] = b_ref[...]
        for part in range(2):
            for sub in range(2):
                for half in range(2):
                    at = (4 * part + 2 * sub + half) * CELL
                    up_ref[:, at : at + CELL] = buf[sub, part, 0, half].astype(F32)
                    down_ref[at : at + CELL, :] = buf[sub, part, 1, half].astype(F32).T

    return pl.pallas_call(
        kernel,
        in_specs=[SMEM, WHOLE, WHOLE],
        out_specs=[WHOLE] * 2,
        out_shape=[jax.ShapeDtypeStruct((CELL, 8 * CELL), F32), jax.ShapeDtypeStruct((8 * CELL, CELL), F32)],
        scratch_shapes=[pltpu.VMEM((2, 2, 2, 2, CELL, CELL), BF16)],
        compiler_params=pltpu.CompilerParams(vmem_limit_bytes=LIMIT),
        cost_estimate=cost(0, 6 * 16 * CELL * CELL),
        name="unpack_feed",
    )(place, own, other)


def join(pieces, place):
    rows, cols = pieces[0].shape
    parts = len(pieces)

    def kernel(place, *refs):
        xs, out, out_t, buf = refs[:parts], *refs[parts:]
        for k in range(parts):
            buf[place[2] ^ k] = xs[k][...]
        for k in range(parts):
            at = slice(k * cols, (k + 1) * cols)
            out[:, at] = buf[k]
            out_t[at, :] = buf[k].T

    return pl.pallas_call(
        kernel,
        in_specs=[SMEM] + [WHOLE] * parts,
        out_specs=[WHOLE] * 2,
        out_shape=[
            jax.ShapeDtypeStruct((rows, cols * parts), BF16),
            jax.ShapeDtypeStruct((cols * parts, rows), BF16),
        ],
        scratch_shapes=[pltpu.VMEM((parts, rows, cols), BF16)],
        compiler_params=pltpu.CompilerParams(vmem_limit_bytes=LIMIT),
        cost_estimate=cost(0, 6 * rows * cols * parts),
        name="join",
    )(place, *pieces)


def layer_body(*args):
    (
        layer_input,
        output_grad,
        first_gain,
        first_shift,
        query_weight,
        key_weight,
        value_weight,
        query_bias,
        value_bias,
        out_weight,
        out_bias,
        second_gain,
        second_shift,
        up_weight,
        up_bias,
        down_weight,
        down_bias,
    ) = args
    shape = tuple(lax.axis_size(a) for a in AXES)
    fast = shape == (4, 2, 4)
    width = first_gain.shape[0]
    head = query_bias.shape[0]
    feed_width = up_bias.shape[0]
    index = [lax.axis_index(a) for a in AXES]
    place = jnp.stack(index if fast else [jnp.int32(0)] * 3).astype(jnp.int32)

    small = [first_gain, first_shift, out_bias, second_gain, second_shift, down_bias, query_bias, value_bias, up_bias]
    if fast:
        by_columns = lambda w: w.reshape(CELL, 2, CELL).transpose(1, 0, 2)
        by_rows = lambda w: w.reshape(2, CELL, CELL)
        own = jnp.stack(
            [by_columns(query_weight), by_columns(key_weight), by_columns(value_weight), by_rows(out_weight)]
        )
        get_j = Gather(own, place)
        get_j.z(2)
        small, x_block, ups, downs, grad_block = pin(
            [get_j], small, layer_input, up_weight, down_weight, output_grad
        )
        ups = ups.reshape(CELL, 2, 2, 2, CELL).transpose(1, 2, 3, 0, 4)
        downs = downs.reshape(2, 2, 2, CELL, CELL)
        get_a, get_b = (Gather(jnp.concatenate([ups[i], downs[i]]), place) for i in range(2))
        get_j.z(1)
        pieces = exchange(pin([get_j], *part_rows(place, x_block)))
        get_j.xy(0)
        pin([get_j, get_a])
        get_a.z(2)
        get_j.xy(1)
        pieces = list(pin([get_j], *pieces))
        get_j.core()
        joined = get_j.bundles()

    wide = spread_vector(jnp.concatenate(small[:6]), "gy").reshape(-1, 6, width).transpose(1, 0, 2).reshape(6, D)
    tall = spread_vector(jnp.concatenate(small[6:]), "gx")
    vectors = jnp.stack(
        [
            wide[0],
            wide[1],
            tall[:, :head].reshape(-1),
            tall[:, head : 2 * head].reshape(-1),
            wide[2],
            wide[3],
            wide[4],
            wide[5],
        ]
    )
    bias_up = tall[:, 2 * head :].reshape(2, 2, D).transpose(1, 0, 2).reshape(2, 1, 2 * D)

    if not fast:
        rows = lax.all_to_all(layer_input, "gy", split_axis=0, concat_axis=1, tiled=True)
        pieces = [rows[:, k * CELL : (k + 1) * CELL] for k in range(4)]
        rows = lax.all_to_all(output_grad, "gy", split_axis=0, concat_axis=1, tiled=True)
        grad_pieces = [rows[:, k * CELL : (k + 1) * CELL] for k in range(4)]
        joined = whole_bundles(
            jnp.stack(
                [projection_cells(whole_weight(w, "gy", "gx")) for w in (query_weight, key_weight, value_weight)]
                + [out_cells(whole_weight(out_weight, "gx", "gy"))]
            ),
            place,
        )
        ups = up_cells(whole_weight(up_weight, "gy", "gx"))
        downs = down_cells(whole_weight(down_weight, "gx", "gy"))
        both = [jnp.concatenate([ups[i], downs[i]]) for i in range(2)]
        fed = [[whole_bundles(c[low::2], place, low) for low in range(2)] for c in both]

    if fast:
        pieces = pin([get_a], *pieces)
        get_a.z(1)
    qkv, inputs, normed_t = project(pieces, vectors, joined)
    if fast:
        qkv = pin([get_a], qkv)
        get_a.xy(0)
        get_b.z(2)
    mixture_0, lse_0 = attend(qkv, 0, 4)
    if fast:
        qkv, mixture_0 = pin([get_a, get_b], qkv, mixture_0)
        get_a.xy(1)
        get_b.z(1)
    mixture_1, lse_1 = attend(qkv, 4, 8)
    if fast:
        mixture_1, grad_block = pin([get_b], mixture_1, grad_block)
        grad_pieces = exchange(part_rows(place, grad_block))
    mixtures, lses = (mixture_0, mixture_1), (lse_0, lse_1)
    middle, normed_two, normed_two_t = mix_out(mixtures, inputs, vectors, joined)
    if fast:
        normed_two, grad_pieces = pin([get_a], normed_two, list(grad_pieces))
        get_b.xy(0)
        get_a.core()
        fed = [[get_a.bundles(slice(0, 4)), get_a.bundles(slice(4, 8))]]
    cotangent, cotangent_t = join(grad_pieces, place)
    activations = (normed_two, normed_two_t, cotangent, cotangent_t)
    *sums, mine_a, bias_a0 = feed(*activations, bias_up[0], fed[0][0], None, False)
    if fast:
        sums = pin([get_b], sums)
        get_b.xy(1)
    *sums, theirs_a, bias_a1 = feed(*activations, bias_up[0], fed[0][1], sums, True)
    if fast:
        sums = pin([get_b], sums)
        get_b.core()
        fed.append([get_b.bundles(slice(0, 4)), get_b.bundles(slice(4, 8))])
        put_a = Scatter(place, theirs_a)
        put_a.core()
    *sums, mine_b, bias_b0 = feed(*activations, bias_up[1], fed[1][0], sums, False)
    if fast:
        sums, mine_a = pin([put_a, get_b], sums, mine_a)
        fed[1][1] = get_b.bundles(slice(4, 8))
        put_a.split(mine_a)
        sums = pin([put_a], sums)
        put_a.xy(0)
    *sums, theirs_b, bias_b1 = feed(*activations, bias_up[1], fed[1][1], sums, True)
    if fast:
        put_b = Scatter(place, theirs_b)
        put_b.core()
    *results, middle_grad, branch_t, mixture_grad, sums_two = turn(middle, cotangent, *sums, vectors, joined)
    if fast:
        mixture_grad, mine_b = pin([put_a, put_b], mixture_grad, mine_b)
        put_b.split(mine_b)
        put_b_first = pin([put_b], mixture_grad)
        mixture_grad = put_b_first
        put_a.xy(1)
        put_b.xy(0)
        results = exchange(results)
    grads_0, heads_0 = attend_back(qkv, mixture_0, lse_0, mixture_grad, 0, 4)
    if fast:
        mixture_grad, grads_0 = pin([put_a, put_b], mixture_grad, grads_0)
        put_b.xy(1)
    grads_1, heads_1 = attend_back(qkv, mixture_1, lse_1, mixture_grad, 4, 8)
    grads = (grads_0, grads_1)
    if fast:
        grads, results = pin([put_b], grads, results)
        put_f = merged(put_a, put_b)
        put_f.z(1)
    theirs_c = weigh(place, normed_t, branch_t, grads, mixtures, True)
    if fast:
        put_c = Scatter(place, theirs_c)
        put_c.core()
        grads, theirs_c = pin([], grads, theirs_c)
    mine_c = weigh(place, normed_t, branch_t, grads, mixtures, False)
    if fast:
        mine_c, middle_grad = pin([put_c, put_f], mine_c, middle_grad)
        put_c.split(mine_c)
        middle_grad = pin([put_c], middle_grad)
        put_c.xy(0)
        put_f.z(2)
    *input_grads, sums_one = finish(inputs, middle_grad, grads, vectors, joined)

    flat_bias = lambda first, second: jnp.stack([first[:, 0], second[:, 0]], axis=1)
    if fast:
        core = index[0] & 1
        order = lambda own, other: flat_bias(jnp.where(core == 0, own, other), jnp.where(core == 0, other, own))
    else:
        order = flat_bias
    bias_up_grad = jnp.stack([order(bias_a0, bias_a1), order(bias_b0, bias_b1)], axis=1).reshape(4, D)
    sums_heads = jnp.concatenate([heads_0[:2], heads_1[:2]], axis=1)
    totals = jnp.concatenate([sums_one[:2], sums_two[:4], sums_heads, bias_up_grad])
    if fast:
        input_grads, results, totals = pin([put_f, put_c], input_grads, list(results), totals)
        put_c.xy(1)
        input_grads = exchange(input_grads)
        put_f.spread(2)
        totals = totals + swap(totals, "dp", 1)
        result = unite_rows(place, results)
        totals, result = pin([put_c, put_f], totals, result)
        put_c.z(1)
        put_f.spread(1)
        totals = totals + swap(totals, "gx", 1)
        totals, input_grads = pin([put_c, put_f], totals, input_grads)
        put_c.z(2)
        up_grad, down_grad = unpack_feed(place, put_f.arrays[0], put_f.arrays[1])
        input_grad = unite_rows(place, input_grads)
        totals = totals + swap(totals, "dp", 2)
        totals, input_grad, up_grad, down_grad = pin([put_c], totals, input_grad, up_grad, down_grad)
        put_c.spread(2)
        totals = totals + swap(totals, "gy", 1)
        totals = pin([put_c], totals)
        put_c.spread(1)
        totals = totals + swap(totals, "gy", 2)
        query_grad, key_grad, value_grad, out_grad = unpack_projections(
            place, put_c.arrays[0][0], put_c.arrays[1][0]
        )
    else:
        back = lambda parts: lax.all_to_all(
            jnp.concatenate(parts, axis=1), "gy", split_axis=1, concat_axis=0, tiled=True
        )
        result, input_grad = back(results), back(input_grads)
        shares = whole_shares(mine_c, theirs_c).astype(F32)
        query_grad, key_grad, value_grad = (
            weight_block(shares[i].transpose(2, 3, 1, 0, 4).reshape(D, D), "gy", "gx") for i in range(3)
        )
        out_grad = weight_block(shares[3].transpose(1, 0, 4, 2, 3).reshape(D, D), "gx", "gy")
        shares = jnp.stack([whole_shares(mine_a, theirs_a), whole_shares(mine_b, theirs_b)]).astype(F32)
        up_grad = weight_block(shares[:, :2].transpose(4, 5, 3, 0, 1, 2, 6).reshape(D, -1), "gy", "gx")
        down_grad = weight_block(shares[:, 2:].transpose(3, 0, 1, 2, 6, 4, 5).reshape(-1, D), "gx", "gy")
        totals = lax.psum(totals, AXES)

    cut = lambda row: lax.dynamic_slice_in_dim(totals[row], index[2] * width, width)
    cut_head = lambda row: lax.dynamic_slice_in_dim(totals[row], index[1] * head, head)
    up_bias_grad = lax.dynamic_slice_in_dim(totals[8:12].reshape(-1), index[1] * feed_width, feed_width)
    return (
        result,
        input_grad,
        cut(0),
        cut(1),
        query_grad,
        key_grad,
        value_grad,
        cut_head(6),
        cut_head(7),
        out_grad,
        cut(2),
        cut(3),
        cut(4),
        up_grad,
        up_bias_grad,
        down_grad,
        cut(5),
    )


def solution(mesh):
    tokens = P(("dp", "gx"), "gy")
    wide, tall = P("gy"), P("gx")
    down_rows, across = P("gy", "gx"), P("gx", "gy")
    params = (
        wide, wide, down_rows, down_rows, down_rows, tall, tall, across, wide,
        wide, wide, down_rows, tall, across, wide,
    )
    return jax.shard_map(
        layer_body,
        mesh=mesh,
        in_specs=(tokens, tokens) + params,
        out_specs=(tokens, tokens) + params,
        check_vma=False,
    )
```

```python
import jax
import jax.numpy as jnp
from jax import lax
from jax.experimental import pallas as pl
from jax.experimental.pallas import tpu as pltpu
from jax.sharding import PartitionSpec as P

D = 1024
HEAD_DIM = 64
SEQ = 577
EPSILON = 1e-06
F32 = jnp.float32
BF16 = jnp.bfloat16

CELL = 256
NT = (((1,), (1,)), ((), ()))
TN = (((0,), (0,)), ((), ()))
ANY = pl.BlockSpec(memory_space=pl.ANY)
WHOLE = pl.BlockSpec(memory_space=pltpu.VMEM)
SMEM = pl.BlockSpec(memory_space=pltpu.SMEM)
LIMIT = 60 * 1024 * 1024
FEED_LIMIT = 60 * 1024 * 1024


def dot(left, right, dims=(((1,), (0,)), ((), ()))):
    return lax.dot_general(left, right, dims, preferred_element_type=F32)


def cost(flops, moved, transcendentals=0):
    return pl.CostEstimate(flops=8 * flops, bytes_accessed=moved, transcendentals=0)


AXES = ("dp", "gx", "gy")


def swap(value, axis, step):
    return lax.ppermute(value, axis, [(i, i ^ step) for i in range(lax.axis_size(axis))])


def shifted(offsets, axis, step):
    place = AXES.index(axis)
    return [o[:place] + (o[place] ^ step,) + o[place + 1 :] for o in offsets]


def doubled(pieces, offsets, axis, step):
    return (
        jnp.concatenate([pieces, swap(pieces, axis, step)], axis=0),
        offsets + shifted(offsets, axis, step),
    )


class Gather:
    orders = ((("gx", 1), ("dp", 2)), (("dp", 2), ("gx", 1)))

    def __init__(self, piece, place):
        self.place = place
        self.arrays = [piece]
        self.offsets = [[(0, 0, 0)]]

    def z(self, step):
        got, offsets = doubled(self.arrays[0], self.offsets[0], "gy", step)
        self.arrays, self.offsets = [got], [offsets]

    def xy(self, turn):
        if turn == 0:
            self.arrays = [self.arrays[0][:, half] for half in range(2)]
            self.offsets = self.offsets * 2
            for half in range(2):
                self.arrays[half], self.offsets[half] = doubled(
                    self.arrays[half], self.offsets[half], *self.orders[half][turn]
                )
        else:
            self.arrays = self.arrays + [swap(self.arrays[half], *self.orders[half][turn]) for half in range(2)]
            self.offsets = self.offsets + [shifted(self.offsets[half], *self.orders[half][turn]) for half in range(2)]

    def core(self):
        self.arrays = self.arrays + [swap(a, "dp", 1) for a in self.arrays]
        self.offsets = self.offsets + [shifted(o, "dp", 1) for o in self.offsets]

    def bundles(self):
        return Bundles(self.place, [(a, o, i % 2) for i, (a, o) in enumerate(zip(self.arrays, self.offsets))])


def fold(value, dim, bit, axis, step):
    kept = lax.dynamic_index_in_dim(value, bit, dim, keepdims=False)
    sent = lax.dynamic_index_in_dim(value, 1 - bit, dim, keepdims=False)
    return (kept.astype(F32) + swap(sent, axis, step).astype(F32)).astype(BF16)


def halve_sum(value, bit, axis, step):
    kept = lax.dynamic_index_in_dim(value, bit, 0, keepdims=False)
    sent = lax.dynamic_index_in_dim(value, 1 - bit, 0, keepdims=False)
    return kept + swap(sent, axis, step)


class Scatter:
    def __init__(self, place, theirs):
        self.place = place
        self.share, self.x_at, self.z_at = (lax.axis_index(a) for a in AXES)
        self.arrays = [theirs]

    def core(self):
        self.arrays = [swap(self.arrays[0], "dp", 1)]

    def split(self, mine):
        self.arrays = list(add_split(self.place, mine, self.arrays[0]))

    def xy(self, turn):
        high = self.share >> 1
        if turn == 0:
            kept_a, sent_a, kept_b, sent_b = self.arrays
            got_a, got_b = swap(sent_a, "dp", 2), swap(sent_b, "gx", 1)
            add = lambda u, v: (u.astype(F32) + v.astype(F32)).astype(BF16)
            self.arrays = [add(kept_a, got_a), add(kept_b, got_b)]
        else:
            first, second = self.arrays
            first, second = fold(first, 0, self.x_at, "gx", 1), fold(second, 0, high, "dp", 2)
            self.arrays = [jnp.stack([first, second]).reshape(1, 2, 2, 2, CELL, CELL)]

    def z(self, step):
        dim, bit = (3, self.z_at & 1) if step == 1 else (2, self.z_at >> 1)
        self.arrays = [fold(self.arrays[0], dim, bit, "gy", step)]

    def spread(self, step):
        both = self.arrays[0]
        other = swap(both, "dp", step)
        if step == 2:
            bit = self.share >> 1
            self.arrays = [jnp.stack([jnp.where(bit == 0, both, other), jnp.where(bit == 0, other, both)], axis=1)]
        else:
            self.arrays = [both, other]


def add_split(place, mine, got):
    block = (1, 1, 1, 4, CELL, CELL)
    flip = lambda bit, sent: 1 - bit if sent else bit
    over_dp = lambda sent: lambda j, p: (flip(p[0] >> 1, sent), 0, j, 0, 0, 0)
    over_gx = lambda sent: lambda j, p: (j, 1, flip(p[1], sent), 0, 0, 0)
    maps = [over_dp(0), over_dp(1), over_gx(0), over_gx(1)]

    def kernel(place, *refs):
        for i in range(4):
            refs[8 + i][0] = (refs[i][0, 0, 0].astype(F32) + refs[4 + i][0, 0, 0].astype(F32)).astype(BF16)

    return pl.pallas_call(
        kernel,
        grid_spec=pltpu.PrefetchScalarGridSpec(
            num_scalar_prefetch=1,
            grid=(2,),
            in_specs=[pl.BlockSpec(block, f) for f in maps] * 2,
            out_specs=[pl.BlockSpec((1, 4, CELL, CELL), lambda j, p: (j, 0, 0, 0))] * 4,
        ),
        out_shape=[jax.ShapeDtypeStruct((2, 4, CELL, CELL), BF16)] * 4,
        compiler_params=pltpu.CompilerParams(vmem_limit_bytes=24 * 1024 * 1024),
        cost_estimate=cost(0, 2 * 3 * 32 * CELL * CELL),
        name="add_split",
    )(place, mine, mine, mine, mine, got, got, got, got)


def pin(chains, *values):
    arrays = [c.arrays for c in chains]
    values, arrays = lax.optimization_barrier((values, arrays))
    for c, held in zip(chains, arrays):
        c.arrays = list(held)
    return values[0] if len(values) == 1 else values


def spread_vector(vector, axis):
    size = lax.axis_size(axis)
    pieces, offsets = vector[None], [0]
    step = size >> 1
    while step:
        pieces = jnp.concatenate([pieces, swap(pieces, axis, step)], axis=0)
        offsets = offsets + [o ^ step for o in offsets]
        step >>= 1
    index = lax.axis_index(axis)
    wanted = jnp.arange(size)[:, None]
    total = jnp.zeros((size, vector.shape[0]), F32)
    for i, offset in enumerate(offsets):
        total = total + jnp.where(wanted == (index ^ offset), pieces[i][None].astype(F32), 0.0)
    return total


def part_rows(block):
    parts = 4
    rows, cols = block.shape[0] // parts, block.shape[1]

    def kernel(x_ref, out):
        for z in range(parts):
            out[z] = x_ref[z * rows : (z + 1) * rows, :]

    return pl.pallas_call(
        kernel,
        in_specs=[WHOLE],
        out_specs=WHOLE,
        out_shape=jax.ShapeDtypeStruct((parts, rows, cols), BF16),
        compiler_params=pltpu.CompilerParams(vmem_limit_bytes=16 * 1024 * 1024),
        cost_estimate=cost(0, 4 * block.size),
        name="part_rows",
    )(block)


def unite_rows(block):
    parts, rows, cols = block.shape

    def kernel(x_ref, out):
        for z in range(parts):
            out[z * rows : (z + 1) * rows, :] = x_ref[z]

    return pl.pallas_call(
        kernel,
        in_specs=[WHOLE],
        out_specs=WHOLE,
        out_shape=jax.ShapeDtypeStruct((parts * rows, cols), BF16),
        compiler_params=pltpu.CompilerParams(vmem_limit_bytes=16 * 1024 * 1024),
        cost_estimate=cost(0, 4 * block.size),
        name="unite_rows",
    )(block)


def exchange(block):
    return lax.all_to_all(block, "gy", split_axis=0, concat_axis=0, tiled=True)


def pack(place, weights, small):
    def kernel(place, q, k, v, o, *refs):
        vectors, out, sem = refs[: len(small)], refs[-2], refs[-1]
        for share, ref in enumerate((q, k, v, o)):

            @pl.when(place[0] == share)
            def _():
                for half in range(2):
                    at = pl.ds(half * CELL, CELL)
                    source = ref.at[:, at] if share < 3 else ref.at[at, :]
                    pltpu.make_async_copy(source, out.at[0, half, 0:CELL], sem.at[half]).start()

        rows = [r[...].reshape(-1, CELL).astype(F32) for r in vectors]
        blank = jnp.zeros((6, CELL), F32)
        out[0, 0, CELL : CELL + 16, :] = jnp.concatenate(rows[:8] + [blank], axis=0).astype(BF16)
        out[0, 1, CELL : CELL + 16, :] = jnp.concatenate([rows[8], blank, blank[:2]], axis=0).astype(BF16)
        for half in range(2):
            cell = out.at[0, half, 0:CELL]
            pltpu.make_async_copy(cell, cell, sem.at[half]).wait()

    return pl.pallas_call(
        kernel,
        in_specs=[SMEM] + [ANY] * 4 + [WHOLE] * len(small),
        out_specs=WHOLE,
        out_shape=jax.ShapeDtypeStruct((1, 2, CELL + 16, CELL), BF16),
        scratch_shapes=[pltpu.SemaphoreType.DMA((2,))],
        compiler_params=pltpu.CompilerParams(vmem_limit_bytes=LIMIT),
        cost_estimate=cost(0, 8 * CELL * CELL),
        name="pack",
    )(place, *weights, *small)


def whole_weight(block, rows_axis, cols_axis):
    return lax.all_gather(lax.all_gather(block, rows_axis, axis=0, tiled=True), cols_axis, axis=1, tiled=True)


def weight_block(grad, rows_axis, cols_axis):
    part = lax.psum_scatter(grad, rows_axis, scatter_dimension=0, tiled=True)
    return lax.psum(lax.psum_scatter(part, cols_axis, scatter_dimension=1, tiled=True), "dp")


def projection_cells(weight):
    return weight.reshape(4, CELL, 2, 2, CELL).transpose(3, 2, 0, 1, 4)


def out_cells(weight):
    return weight.reshape(2, 2, CELL, 4, CELL).transpose(1, 0, 3, 2, 4)


def up_cells(weight):
    return weight.reshape(4, CELL, 2, 2, 2, 2, CELL).transpose(3, 4, 5, 2, 0, 1, 6)


def down_cells(weight):
    return weight.reshape(2, 2, 2, 2, CELL, 4, CELL).transpose(1, 2, 3, 0, 5, 4, 6)


def whole_bundles(cells, place):
    offsets = [(d, x, z) for d in range(4) for x in range(2) for z in range(4)]
    return Bundles(place, [(cells[:, half].reshape(-1, CELL, CELL), offsets, half) for half in range(2)])


def split_bundles(cells, place):
    parts = []
    for low in range(2):
        offsets = [(d, x, z) for d in (low, low + 2) for x in range(2) for z in range(4)]
        parts += [(cells[low::2, half].reshape(-1, CELL, CELL), offsets, half) for half in range(2)]
    return Bundles(place, parts)


def whole_shares(mine, theirs):
    return jnp.stack([mine, theirs], axis=1).reshape((4,) + mine.shape[1:])


class Bundles:
    def __init__(self, place, parts):
        self.place = place
        self.arrays = [p[0] for p in parts]
        self.meta = [(p[1], p[2]) for p in parts]

    def start(self, place_ref, refs, put):
        for ref, meta in zip(refs, self.meta):
            self.start_one(place_ref, ref, meta, put)

    @staticmethod
    def start_one(place_ref, ref, meta, put):
        offsets, half = meta
        for i, (od, ox, oz) in enumerate(offsets):
            put(ref.at[i, 0:CELL], place_ref[0] ^ od, half, place_ref[1] ^ ox, place_ref[2] ^ oz)


def window(ref, row, col):
    return ref.at[pl.ds(pl.multiple_of(row, CELL), CELL), pl.ds(pl.multiple_of(col, CELL), CELL)]


def put_projections(weights, sems):
    def put(source, share, half, x, z):
        @pl.when(share < 3)
        def _():
            dest = window(weights.at[share], z * CELL, (2 * x + half) * CELL)
            pltpu.make_async_copy(source, dest, sems.at[share]).start()

    return put


def put_out(weight, sem):
    def put(source, share, half, x, z):
        @pl.when(share == 3)
        def _():
            pltpu.make_async_copy(source, window(weight, (2 * x + half) * CELL, z * CELL), sem).start()

    return put


def put_feed(up, down, sems, core):
    def put(source, share, half, x, z):
        at = (2 * x + half) * CELL
        own = 1 - ((share ^ core) & 1)

        @pl.when(share < 2)
        def _():
            pltpu.make_async_copy(source, window(up.at[own], z * CELL, at), sems.at[own, 0]).start()

        @pl.when(share >= 2)
        def _():
            pltpu.make_async_copy(source, window(down.at[own], at, z * CELL), sems.at[own, 1]).start()

    return put


def wait_all(ref, sem):
    pltpu.make_async_copy(ref, ref, sem).wait()


def normal(values):
    center = values - jnp.mean(values, axis=1, keepdims=True)
    inverse = lax.rsqrt(jnp.mean(center * center, axis=1, keepdims=True) + EPSILON)
    return center * inverse, inverse


def back_norm(grad, normal_rows, inverse, gain):
    scaled = grad * gain
    mean_one = jnp.mean(scaled, axis=1, keepdims=True)
    mean_two = jnp.mean(scaled * normal_rows, axis=1, keepdims=True)
    return inverse * (scaled - mean_one - normal_rows * mean_two)


def column_sum(values):
    return jnp.sum(values, axis=0, keepdims=True)


def project(x_parts, vectors, bundles):
    parts, rows, cols = x_parts.shape
    count = len(bundles.arrays)
    given = vectors is not None

    def kernel(place, x_parts, *refs):
        if given:
            vec, *refs = refs
        sources = refs[:count]
        q_ref, x_ref, nt_ref, *refs = refs[count:]
        if not given:
            vec, up_ref, vbuf, vsem, *refs = refs
        weights, n_ref, sems = refs
        step = pl.program_id(0)

        @pl.when(step == 0)
        def _():
            if not given:
                for ref, (offsets, half) in zip(sources, bundles.meta):
                    for i, (od, ox, oz) in enumerate(offsets):
                        if od == 0:
                            dest = vbuf.at[half, place[1] ^ ox, place[2] ^ oz]
                            pltpu.make_async_copy(ref.at[i, CELL : CELL + 16], dest, vsem).start()
            bundles.start(place, sources, put_projections(weights, sems))
            if not given:
                wait_all(vbuf, vsem)
                tall = lambda row: [vbuf[0, x, 0, row + i : row + i + 1, :] for x in range(2) for i in range(2)]
                wide = lambda row: [vbuf[0, 0, z, row : row + 1, :] for z in range(4)]
                pieces = [wide(0), wide(1), tall(6), tall(8), wide(2), wide(3), wide(4), wide(5)]
                for i, cut in enumerate(pieces):
                    vec[i : i + 1, :] = jnp.concatenate(cut, axis=1).astype(F32)
                for part in range(2):
                    cut = [vbuf[1, x, 0, 4 * part + i : 4 * part + i + 1, :] for x in range(2) for i in range(4)]
                    up_ref[part] = jnp.concatenate(cut, axis=1).astype(F32)
            x = jnp.concatenate([x_parts[z] for z in range(parts)], axis=1)
            x_ref[...] = x
            normal_rows, _ = normal(x.astype(F32))
            normed = (normal_rows * vec[0:1, :] + vec[1:2, :]).astype(BF16)
            n_ref[...] = normed
            nt_ref[...] = normed.T

        for share in range(3):

            @pl.when(step == share)
            def _():
                wait_all(weights.at[share], sems.at[share])
                total = dot(n_ref[...], weights[share])
                if share != 1:
                    total = total + vec[2 + share // 2 : 3 + share // 2, :]
                q_ref[0] = total.astype(BF16)

    extra = [] if given else [jax.ShapeDtypeStruct((8, D), F32), jax.ShapeDtypeStruct((2, 1, 2 * D), F32)]
    outs = pl.pallas_call(
        kernel,
        grid=(3,),
        in_specs=[SMEM, WHOLE] + [WHOLE] * given + [ANY] * count,
        out_specs=[pl.BlockSpec((1, rows, D), lambda s: (s, 0, 0)), WHOLE, WHOLE] + [WHOLE] * len(extra),
        out_shape=[
            jax.ShapeDtypeStruct((3, rows, D), BF16),
            jax.ShapeDtypeStruct((rows, D), BF16),
            jax.ShapeDtypeStruct((D, rows), BF16),
        ]
        + extra,
        scratch_shapes=([] if given else [pltpu.VMEM((2, 2, 4, 16, CELL), BF16), pltpu.SemaphoreType.DMA])
        + [
            pltpu.VMEM((3, D, D), BF16),
            pltpu.VMEM((rows, D), BF16),
            pltpu.SemaphoreType.DMA((3,)),
        ],
        compiler_params=pltpu.CompilerParams(vmem_limit_bytes=LIMIT),
        cost_estimate=cost(6 * rows * D * D, 6 * D * D + 12 * rows * D),
        name="project",
    )(bundles.place, x_parts, *([vectors] if given else []), *bundles.arrays)
    return outs if not given else (*outs, vectors, None)


def attend(qkv, begin, end):
    rows = qkv.shape[1]
    pairs = end - begin

    def kernel(q_ref, k_ref, v_ref, o_ref, lse_ref, buf):
        q, k, v = q_ref[0], k_ref[0], v_ref[0]
        first = lax.broadcasted_iota(jnp.int32, (1, 128), 1) < 64
        scale = HEAD_DIM**-0.5
        outs = []
        for h in range(2):
            mine = first if h == 0 else jnp.logical_not(first)
            qh = jnp.where(mine, q.astype(F32) * scale, 0.0).astype(BF16)
            s = dot(qh, k, NT)
            top = jnp.max(s, axis=1, keepdims=True)
            p = jnp.exp(s - top)
            total = jnp.sum(p, axis=1, keepdims=True)
            outs.append(dot(p.astype(BF16), v) / total)
            buf[0:rows, h : h + 1] = top + jnp.log(total)
        o_ref[...] = jnp.where(first, outs[0], outs[1]).astype(BF16)
        lse_ref[0] = buf[...].T[0:8, 0:rows]

    spec = lambda i: pl.BlockSpec((1, rows, 128), lambda s, i=i: (i, 0, s + begin))
    return pl.pallas_call(
        kernel,
        grid=(pairs,),
        in_specs=[spec(0), spec(1), spec(2)],
        out_specs=[pl.BlockSpec((rows, 128), lambda s: (0, s)), pl.BlockSpec((1, 8, rows), lambda s: (s, 0, 0))],
        out_shape=[
            jax.ShapeDtypeStruct((rows, pairs * 128), BF16),
            jax.ShapeDtypeStruct((pairs, 8, rows), F32),
        ],
        scratch_shapes=[pltpu.VMEM((640, 128), F32)],
        compiler_params=pltpu.CompilerParams(vmem_limit_bytes=LIMIT),
        cost_estimate=cost(2048 * pairs * rows * rows, 1024 * pairs * rows, 2 * pairs * rows * rows),
        name="attend",
    )(qkv, qkv, qkv)


def attend_back(qkv, mixture, lse, mixture_grad, begin, end):
    rows = qkv.shape[1]
    pairs = end - begin

    def kernel(q_ref, k_ref, v_ref, o_ref, lse_ref, do_ref, g_ref, b_ref):
        q, k, v, grad = q_ref[0], k_ref[0], v_ref[0], do_ref[...]
        first = lax.broadcasted_iota(jnp.int32, (1, 128), 1) < 64
        scale = HEAD_DIM**-0.5
        pick = lax.broadcasted_iota(jnp.int32, (8, 128), 0) == lax.broadcasted_iota(jnp.int32, (8, 128), 1) // 64
        product = grad.astype(F32) * o_ref[...].astype(F32)
        delta = lax.dot_general(
            jnp.where(pick, 1.0, 0.0), product, NT, precision=lax.Precision.HIGHEST, preferred_element_type=F32
        )
        dqs, dks, dvs = [], [], []
        for h in range(2):
            mine = first if h == 0 else jnp.logical_not(first)
            qh = jnp.where(mine, q.astype(F32) * scale, 0.0).astype(BF16)
            gh = jnp.where(mine, grad, jnp.zeros_like(grad))
            p = jnp.exp(dot(k, qh, NT) - lse_ref[0, h : h + 1, :])
            dp = dot(v, gh, NT)
            ds = (p * (dp - delta[h : h + 1, :])).astype(BF16)
            dvs.append(dot(p.astype(BF16), grad))
            dks.append(dot(ds, q))
            dqs.append(dot(k, ds, TN))
        dq = (jnp.concatenate([dqs[0][:64], dqs[1][64:]], axis=0) * scale).T.astype(BF16)
        dk = (jnp.where(first, dks[0], dks[1]) * scale).astype(BF16)
        dv = jnp.where(first, dvs[0], dvs[1]).astype(BF16)
        g_ref[0], g_ref[1], g_ref[2] = dq, dk, dv
        b_ref[0:1, :] = column_sum(dq.astype(F32))
        b_ref[1:2, :] = column_sum(dv.astype(F32))

    spec = lambda i: pl.BlockSpec((1, rows, 128), lambda s, i=i: (i, 0, s + begin))
    flat = pl.BlockSpec((rows, 128), lambda s: (0, s))
    wide = pl.BlockSpec((rows, 128), lambda s: (0, s + begin))
    return pl.pallas_call(
        kernel,
        grid=(pairs,),
        in_specs=[spec(0), spec(1), spec(2), flat, pl.BlockSpec((1, 8, rows), lambda s: (s, 0, 0)), wide],
        out_specs=[pl.BlockSpec((3, rows, 128), lambda s: (0, 0, s)), pl.BlockSpec((8, 128), lambda s: (0, s))],
        out_shape=[
            jax.ShapeDtypeStruct((3, rows, pairs * 128), BF16),
            jax.ShapeDtypeStruct((8, pairs * 128), F32),
        ],
        compiler_params=pltpu.CompilerParams(vmem_limit_bytes=LIMIT),
        cost_estimate=cost(6000 * pairs * rows * rows, 2048 * pairs * rows, 2 * pairs * rows * rows),
        name="attend_back",
    )(qkv, qkv, qkv, mixture, lse, mixture_grad)


def mix_out(mixtures, inputs, vectors, bundles):
    rows = inputs.shape[0]
    count = len(bundles.arrays)

    def kernel(place, vec, m_ref, o_ref, x_ref, *refs):
        sources = refs[:count]
        mid_ref, n_ref, nt_ref, weight, sem = refs[count:]
        bundles.start(place, sources, put_out(weight, sem))
        wait_all(weight, sem)
        mixture = jnp.concatenate([m_ref[...], o_ref[...]], axis=1)
        middle = x_ref[...].astype(F32) + (dot(mixture, weight[...]) + vec[4:5, :])
        mid_ref[...] = middle
        normal_rows, _ = normal(middle)
        normed = (normal_rows * vec[5:6, :] + vec[6:7, :]).astype(BF16)
        n_ref[...] = normed
        nt_ref[...] = normed.T

    return pl.pallas_call(
        kernel,
        in_specs=[SMEM] + [WHOLE] * 4 + [ANY] * count,
        out_specs=[WHOLE] * 3,
        out_shape=[
            jax.ShapeDtypeStruct((rows, D), F32),
            jax.ShapeDtypeStruct((rows, D), BF16),
            jax.ShapeDtypeStruct((D, rows), BF16),
        ],
        scratch_shapes=[pltpu.VMEM((D, D), BF16), pltpu.SemaphoreType.DMA],
        compiler_params=pltpu.CompilerParams(vmem_limit_bytes=LIMIT),
        cost_estimate=cost(2 * rows * D * D, 2 * D * D + 10 * rows * D),
        name="mix_out",
    )(bundles.place, vectors, *mixtures, inputs, *bundles.arrays)


def gelu_pair(h):
    below = 0.5 * (1.0 + lax.erf(h * 0.7071067811865476))
    bell = jnp.exp(h * h * -0.5) * 0.3989422804014327
    return h * below, below + h * bell


def feed(acts, up_bias, bundles, partials):
    rows = acts[0].shape[0]
    tile = 2 * CELL
    count = len(bundles.arrays)
    olds = [] if partials is None else list(partials)
    carried = len(olds)

    def kernel(place, bias, n_ref, nt_ref, g_ref, gt_ref, *refs):
        olds, sources = refs[:carried], refs[carried : carried + count]
        out_acc, back_acc, mine, theirs, bias_ref, up, down, sems = refs[carried + count :]
        step = pl.program_id(0)
        own = step // 2
        x = lax.rem(step, 2)
        core = place[0] & 1
        sub = jnp.where(step < 2, 1 - core, core)

        @pl.when(step == 0)
        def _():
            order = list(range(count // 2, count)) + list(range(count // 2))
            put = put_feed(up, down, sems, core)
            for i in order:
                Bundles.start_one(place, sources[i], bundles.meta[i], put)
            for acc, old in zip((out_acc, back_acc), olds):
                acc[...] = old[...]
            if not carried:
                out_acc[...] = jnp.zeros_like(out_acc)
                back_acc[...] = jnp.zeros_like(back_acc)

        for i in range(2):

            @pl.when(step == 2 * i)
            def _():
                wait_all(up.at[i], sems.at[i, 0])
                wait_all(down.at[i], sems.at[i, 1])

        at = pl.multiple_of(x * tile, tile)
        bias_at = pl.multiple_of((2 * x + sub) * tile, tile)
        up_tile = up[own, :, pl.ds(at, tile)]
        down_tile = down[own, pl.ds(at, tile), :]
        pre = dot(n_ref[...], up_tile) + bias[0:1, pl.ds(bias_at, tile)]
        hidden, slope = gelu_pair(pre)
        hidden = hidden.astype(BF16)
        out_acc[...] += dot(hidden, down_tile)
        pre_grad = (dot(g_ref[...], down_tile, NT) * slope).astype(BF16)
        back_acc[...] += dot(pre_grad, up_tile, NT)
        bias_ref[0, 0] = column_sum(pre_grad.astype(F32))
        up_grad, down_grad = dot(nt_ref[...], pre_grad).astype(BF16), dot(gt_ref[...], hidden).astype(BF16)

        def leave(cells):
            for i, grad in enumerate((up_grad, down_grad)):
                for half in range(2):
                    for z in range(4):
                        cell = grad[z * CELL : (z + 1) * CELL, half * CELL : (half + 1) * CELL]
                        cells[i, half, 0, z] = cell

        @pl.when(step < 2)
        def _():
            leave(theirs)

        @pl.when(step >= 2)
        def _():
            leave(mine)

    acc = jax.ShapeDtypeStruct((rows, D), F32)
    full = lambda shape: pl.BlockSpec(shape, lambda s, p: (0,) * len(shape))
    block = (2, 2, 1, 4, CELL, CELL)
    cells = jax.ShapeDtypeStruct((2, 2, 2, 4, CELL, CELL), BF16)
    ins = [up_bias, *acts, *olds]
    low = lambda s, p: jnp.where(s < 2, 1 - (p[0] & 1), p[0] & 1)
    return pl.pallas_call(
        kernel,
        grid_spec=pltpu.PrefetchScalarGridSpec(
            num_scalar_prefetch=1,
            grid=(4,),
            in_specs=[full(v.shape) for v in ins] + [ANY] * count,
            out_specs=[
                full((rows, D)),
                full((rows, D)),
                pl.BlockSpec(block, lambda s, p: (0, 0, jnp.maximum(s - 2, 0), 0, 0, 0)),
                pl.BlockSpec(block, lambda s, p: (0, 0, jnp.minimum(s, 1), 0, 0, 0)),
                pl.BlockSpec((1, 1, 1, tile), lambda s, p: (lax.rem(s, 2), low(s, p), 0, 0)),
            ],
            scratch_shapes=[
                pltpu.VMEM((2, D, 2 * tile), BF16),
                pltpu.VMEM((2, 2 * tile, D), BF16),
                pltpu.SemaphoreType.DMA((2, 2)),
            ],
        ),
        out_shape=[acc, acc, cells, cells, jax.ShapeDtypeStruct((2, 2, 1, tile), F32)],
        compiler_params=pltpu.CompilerParams(vmem_limit_bytes=FEED_LIMIT),
        cost_estimate=cost(48 * rows * D * tile, 32 * D * tile + 28 * rows * D, 8 * rows * tile),
        name="feed",
    )(bundles.place, *ins, *bundles.arrays)


def turn(middle, cotangent, out_sum, back_sum, vectors, bundles):
    rows = middle.shape[0]
    count = len(bundles.arrays)
    parts = 4

    def kernel(place, vec, mid_ref, g_ref, out_ref, back_ref, *refs):
        sources = refs[:count]
        pieces, grad_ref, branch_t, mix_ref, sum_ref, weight, sem = refs[count:]
        bundles.start(place, sources, put_out(weight, sem))
        middle = mid_ref[...]
        result = (middle + (out_ref[...] + vec[7:8, :])).astype(BF16)
        for k in range(parts):
            pieces[k] = result[:, k * CELL : (k + 1) * CELL]
        normal_rows, inverse = normal(middle)
        back = back_ref[...]
        grads = g_ref[...].astype(F32)
        middle_grad = grads + back_norm(back, normal_rows, inverse, vec[5:6, :])
        grad_ref[...] = middle_grad
        branch = middle_grad.astype(BF16)
        branch_t[...] = branch.T
        sum_ref[0:1, :] = column_sum(branch.astype(F32))
        sum_ref[1:2, :] = column_sum(back * normal_rows)
        sum_ref[2:3, :] = column_sum(back)
        sum_ref[3:4, :] = column_sum(grads)
        wait_all(weight, sem)
        mix_ref[...] = dot(branch, weight[...], NT).astype(BF16)

    full = jax.ShapeDtypeStruct((rows, D), BF16)
    return pl.pallas_call(
        kernel,
        in_specs=[SMEM] + [WHOLE] * 5 + [ANY] * count,
        out_specs=[WHOLE] * 5,
        out_shape=[
            jax.ShapeDtypeStruct((parts, rows, CELL), BF16),
            jax.ShapeDtypeStruct((rows, D), F32),
            jax.ShapeDtypeStruct((D, rows), BF16),
            full,
            jax.ShapeDtypeStruct((8, D), F32),
        ],
        scratch_shapes=[
            pltpu.VMEM((D, D), BF16),
            pltpu.SemaphoreType.DMA,
        ],
        compiler_params=pltpu.CompilerParams(vmem_limit_bytes=LIMIT),
        cost_estimate=cost(2 * rows * D * D, 2 * D * D + 24 * rows * D),
        name="turn",
    )(bundles.place, vectors, middle, cotangent, out_sum, back_sum, *bundles.arrays)


def weigh(place, normed_t, branch_t, grads, mixtures, other):
    rows = normed_t.shape[1]

    def kernel(place, n_t, b_t, g0, g1, m0, m1, cells):
        core = place[0] & 1
        share = 2 * pl.program_id(0) + (1 - core if other else core)

        def fill(left, right):
            for x in range(2):
                for half in range(2):
                    grad = dot(left, right(x, half * CELL)).astype(BF16)
                    cells[0, half, x] = grad.reshape(4, CELL, CELL)

        for k in range(3):

            @pl.when(share == k)
            def _():
                fill(n_t[...], lambda x, at: (g0, g1)[x][k, :, at : at + CELL])

        @pl.when(share == 3)
        def _():
            fill(b_t[...], lambda x, at: (m0, m1)[x][:, at : at + CELL])

    return pl.pallas_call(
        kernel,
        grid=(2,),
        in_specs=[SMEM] + [WHOLE] * 6,
        out_specs=pl.BlockSpec((1, 2, 2, 4, CELL, CELL), lambda s: (s, 0, 0, 0, 0, 0)),
        out_shape=jax.ShapeDtypeStruct((2, 2, 2, 4, CELL, CELL), BF16),
        compiler_params=pltpu.CompilerParams(vmem_limit_bytes=LIMIT),
        cost_estimate=cost(4 * rows * D * D, 4 * D * D + 12 * rows * D),
        name="weigh",
    )(place, normed_t, branch_t, *grads, *mixtures)


def finish(inputs, middle_grad, grads, vectors, bundles):
    rows = inputs.shape[0]
    count = len(bundles.arrays)
    parts = 4

    def kernel(place, vec, x_ref, mid_ref, g0, g1, *refs):
        sources = refs[:count]
        pieces, sum_ref, weights, sems = refs[count:]
        bundles.start(place, sources, put_projections(weights, sems))
        normal_rows, inverse = normal(x_ref[...].astype(F32))
        back = None
        for k in range(3):
            wait_all(weights.at[k], sems.at[k])
            term = dot(jnp.concatenate([g0[k], g1[k]], axis=1), weights[k], NT)
            back = term if back is None else back + term
        result = (mid_ref[...] + back_norm(back, normal_rows, inverse, vec[0:1, :])).astype(BF16)
        for k in range(parts):
            pieces[k] = result[:, k * CELL : (k + 1) * CELL]
        sum_ref[0:1, :] = column_sum(back * normal_rows)
        sum_ref[1:2, :] = column_sum(back)

    return pl.pallas_call(
        kernel,
        in_specs=[SMEM] + [WHOLE] * 5 + [ANY] * count,
        out_specs=[WHOLE] * 2,
        out_shape=[jax.ShapeDtypeStruct((parts, rows, CELL), BF16), jax.ShapeDtypeStruct((8, D), F32)],
        scratch_shapes=[pltpu.VMEM((3, D, D), BF16), pltpu.SemaphoreType.DMA((3,))],
        compiler_params=pltpu.CompilerParams(vmem_limit_bytes=LIMIT),
        cost_estimate=cost(6 * rows * D * D, 6 * D * D + 14 * rows * D),
        name="finish",
    )(bundles.place, vectors, inputs, middle_grad, *grads, *bundles.arrays)


def unpack_projections(place, own, other):
    def kernel(place, a_ref, b_ref, *refs):
        outs, buf = refs[:4], refs[4]
        core = place[0] & 1
        buf[core] = a_ref[...]
        buf[1 - core] = b_ref[...]
        for share in range(4):
            for half in range(2):
                cell = buf[share % 2, share // 2, half]
                at = slice(half * CELL, (half + 1) * CELL)
                if share < 3:
                    outs[share][:, at] = cell.astype(F32)
                else:
                    outs[share][at, :] = cell.astype(F32).T

    tall, wide = (jax.ShapeDtypeStruct(s, F32) for s in ((2 * CELL, CELL), (CELL, 2 * CELL)))
    return pl.pallas_call(
        kernel,
        in_specs=[SMEM, WHOLE, WHOLE],
        out_specs=[WHOLE] * 4,
        out_shape=[wide, wide, wide, tall],
        scratch_shapes=[pltpu.VMEM((2, 2, 2, CELL, CELL), BF16)],
        compiler_params=pltpu.CompilerParams(vmem_limit_bytes=LIMIT),
        cost_estimate=cost(0, 3 * 16 * CELL * CELL),
        name="unpack_projections",
    )(place, own, other)


def unpack_feed(place, own, other):
    def kernel(place, a_ref, b_ref, up_ref, down_ref, buf):
        core = place[0] & 1
        buf[core] = a_ref[...]
        buf[1 - core] = b_ref[...]
        for part in range(2):
            for sub in range(2):
                for half in range(2):
                    at = (4 * part + 2 * sub + half) * CELL
                    up_ref[:, at : at + CELL] = buf[sub, part, 0, half].astype(F32)
                    down_ref[at : at + CELL, :] = buf[sub, part, 1, half].astype(F32).T

    return pl.pallas_call(
        kernel,
        in_specs=[SMEM, WHOLE, WHOLE],
        out_specs=[WHOLE] * 2,
        out_shape=[jax.ShapeDtypeStruct((CELL, 8 * CELL), F32), jax.ShapeDtypeStruct((8 * CELL, CELL), F32)],
        scratch_shapes=[pltpu.VMEM((2, 2, 2, 2, CELL, CELL), BF16)],
        compiler_params=pltpu.CompilerParams(vmem_limit_bytes=LIMIT),
        cost_estimate=cost(0, 6 * 16 * CELL * CELL),
        name="unpack_feed",
    )(place, own, other)


def join(x_parts):
    parts, rows, cols = x_parts.shape

    def kernel(x_ref, out, out_t):
        for k in range(parts):
            at = slice(k * cols, (k + 1) * cols)
            out[:, at] = x_ref[k]
            out_t[at, :] = x_ref[k].T

    return pl.pallas_call(
        kernel,
        in_specs=[WHOLE],
        out_specs=[WHOLE] * 2,
        out_shape=[
            jax.ShapeDtypeStruct((rows, cols * parts), BF16),
            jax.ShapeDtypeStruct((cols * parts, rows), BF16),
        ],
        compiler_params=pltpu.CompilerParams(vmem_limit_bytes=24 * 1024 * 1024),
        cost_estimate=cost(0, 6 * rows * cols * parts),
        name="join",
    )(x_parts)


def layer_body(*args):
    (
        layer_input,
        output_grad,
        first_gain,
        first_shift,
        query_weight,
        key_weight,
        value_weight,
        query_bias,
        value_bias,
        out_weight,
        out_bias,
        second_gain,
        second_shift,
        up_weight,
        up_bias,
        down_weight,
        down_bias,
    ) = args
    shape = tuple(lax.axis_size(a) for a in AXES)
    fast = shape == (4, 2, 4)
    width = first_gain.shape[0]
    head = query_bias.shape[0]
    feed_width = up_bias.shape[0]
    index = [lax.axis_index(a) for a in AXES]
    place = jnp.stack(index if fast else [jnp.int32(0)] * 3).astype(jnp.int32)

    small = [first_gain, first_shift, out_bias, second_gain, second_shift, down_bias, query_bias, value_bias, up_bias]
    if fast:
        get_j = Gather(pack(place, (query_weight, key_weight, value_weight, out_weight), small), place)
        get_j.z(2)
        x_block, ups, downs = pin([], layer_input, up_weight, down_weight)
        x_copies = part_rows(x_block)
        ups = ups.reshape(CELL, 2, 2, 2, CELL).transpose(2, 1, 3, 0, 4)
        downs = downs.reshape(2, 2, 2, CELL, CELL).transpose(1, 0, 2, 3, 4)
        feeds = lax.dynamic_index_in_dim(jnp.concatenate([ups, downs]), index[0], 0, keepdims=False)
        get_j.z(1)
        x_parts = exchange(pin([get_j], x_copies))
        get_j.xy(0)
        get_j.xy(1)
        x_parts, feeds = pin([], x_parts, feeds)
        get_a, get_b = (Gather(feeds[i : i + 1], place) for i in range(2))
        get_a.z(2)
        get_j.core()
        joined = get_j.bundles()
        vectors = None
        get_a.z(1)
        x_parts, output_grad = pin([get_a, get_b], x_parts, output_grad)
        get_a.xy(0)
        get_b.z(2)
    else:
        wide = spread_vector(jnp.concatenate(small[:6]), "gy").reshape(-1, 6, width)
        wide = wide.transpose(1, 0, 2).reshape(6, D)
        tall = spread_vector(jnp.concatenate(small[6:]), "gx")
        vectors = jnp.stack(
            [
                wide[0],
                wide[1],
                tall[:, :head].reshape(-1),
                tall[:, head : 2 * head].reshape(-1),
                wide[2],
                wide[3],
                wide[4],
                wide[5],
            ]
        )
        bias_up = tall[:, 2 * head :].reshape(2, 2, D).transpose(1, 0, 2).reshape(2, 1, 2 * D)
        by_parts = lambda rows: rows.reshape(rows.shape[0], 4, CELL).transpose(1, 0, 2)
        x_parts = by_parts(lax.all_to_all(layer_input, "gy", split_axis=0, concat_axis=1, tiled=True))
        grad_parts = by_parts(lax.all_to_all(output_grad, "gy", split_axis=0, concat_axis=1, tiled=True))
        joined = whole_bundles(
            jnp.stack(
                [projection_cells(whole_weight(w, "gy", "gx")) for w in (query_weight, key_weight, value_weight)]
                + [out_cells(whole_weight(out_weight, "gx", "gy"))]
            ),
            place,
        )
        ups = up_cells(whole_weight(up_weight, "gy", "gx"))
        downs = down_cells(whole_weight(down_weight, "gx", "gy"))
        both = [jnp.concatenate([ups[i], downs[i]]) for i in range(2)]
        fed = [split_bundles(c, place) for c in both]

    qkv, inputs, normed_t, vectors, bias_given = project(x_parts, vectors, joined)
    if fast:
        bias_up = bias_given
        qkv = pin([get_a, get_b], qkv)
        get_a.xy(1)
        get_b.z(1)
    mixture_0, lse_0 = attend(qkv, 0, 4)
    if fast:
        qkv, mixture_0, output_grad = pin([get_b], qkv, mixture_0, output_grad)
        grad_parts = exchange(part_rows(output_grad))
    mixture_1, lse_1 = attend(qkv, 4, 8)
    mixtures = (mixture_0, mixture_1)
    if fast:
        mixtures = pin([get_a, get_b], mixtures)
        get_b.xy(0)
        get_a.core()
        fed = [get_a.bundles()]
    middle, normed_two, normed_two_t = mix_out(mixtures, inputs, vectors, joined)
    cotangent, cotangent_t = join(grad_parts)
    if fast:
        normed_two = pin([get_b], normed_two)
        get_b.xy(1)
    acts = (normed_two, normed_two_t, cotangent, cotangent_t)
    *sums, mine_a, theirs_a, bias_a = feed(acts, bias_up[0], fed[0], None)
    if fast:
        sums, theirs_a = pin([get_b], sums, theirs_a)
        get_b.core()
        fed.append(get_b.bundles())
        put_a = Scatter(place, theirs_a)
        put_a.core()
    *sums, mine_b, theirs_b, bias_b = feed(acts, bias_up[1], fed[1], sums)
    if fast:
        put_b = Scatter(place, theirs_b)
        put_b.core()
        sums, mine_a = pin([put_a], sums, mine_a)
        put_a.split(mine_a)
        sums = pin([put_a], sums)
        put_a.xy(0)
    results, middle_grad, branch_t, mixture_grad, sums_two = turn(middle, cotangent, *sums, vectors, joined)
    if fast:
        mine_b, mixture_grad, results = pin([put_b], mine_b, mixture_grad, results)
        put_b.split(mine_b)
        mixture_grad = pin([put_b], mixture_grad)
        results = exchange(results)
    grads_0, heads_0 = attend_back(qkv, mixtures[0], lse_0, mixture_grad, 0, 4)
    if fast:
        mixture_grad, grads_0 = pin([put_a], mixture_grad, grads_0)
        put_a.xy(1)
        put_b.xy(0)
    grads_1, heads_1 = attend_back(qkv, mixtures[1], lse_1, mixture_grad, 4, 8)
    grads = (grads_0, grads_1)
    if fast:
        grads, results = pin([put_a], grads, results)
        put_a.z(1)
    theirs_c = weigh(place, normed_t, branch_t, grads, mixtures, True)
    if fast:
        put_c = Scatter(place, theirs_c)
        put_c.core()
        grads, theirs_c = pin([put_b], grads, theirs_c)
        put_b.xy(1)
    mine_c = weigh(place, normed_t, branch_t, grads, mixtures, False)
    if fast:
        mine_c, middle_grad = pin([put_a, put_b, put_c], mine_c, middle_grad)
        put_c.split(mine_c)
        middle_grad = pin([put_c], middle_grad)
        put_c.xy(0)
        put_a.z(2)
        put_b.z(1)
    input_grads, sums_one = finish(inputs, middle_grad, grads, vectors, joined)

    bias_up_grad = jnp.stack([bias_a, bias_b]).transpose(1, 0, 2, 3, 4).reshape(2, -1)
    sums_heads = jnp.concatenate([heads_0[:2], heads_1[:2]], axis=1)
    wide_sums = jnp.concatenate([sums_one[:2], sums_two[:4]])
    if fast:
        by_z = wide_sums.reshape(6, 1, 4, CELL).transpose(1, 2, 0, 3).reshape(1, 4, 6 * CELL)
        by_x = jnp.concatenate(
            [sums_heads.reshape(2, 2, head).transpose(1, 0, 2).reshape(2, 2 * head), bias_up_grad], axis=1
        )
        totals = jnp.concatenate(
            [jnp.broadcast_to(by_z, (2, 4, 6 * CELL)), jnp.broadcast_to(by_x[:, None], (2, 4, by_x.shape[1]))], axis=2
        )
        input_grads, totals = pin([put_c, put_b], input_grads, totals)
        put_c.xy(1)
        input_grads = exchange(input_grads)
        put_b.z(2)
        put_f = Scatter(place, None)
        put_f.arrays = [jnp.concatenate([put_a.arrays[0], put_b.arrays[0]])]
        put_f.spread(2)
        totals = halve_sum(totals, index[1], "gx", 1)
        totals = halve_sum(totals.reshape(2, 2, -1), index[2] >> 1, "gy", 2)
        result = results
        put_c.z(1)
        put_f.spread(1)
        totals = halve_sum(totals, index[2] & 1, "gy", 1)
        result = unite_rows(result)
        put_c.z(2)
        totals = totals + swap(totals, "dp", 1)
        up_grad, down_grad = unpack_feed(place, put_f.arrays[0], put_f.arrays[1])
        put_c.spread(2)
        totals = totals + swap(totals, "dp", 2)
        input_grad = unite_rows(input_grads)
        put_c.spread(1)
        query_grad, key_grad, value_grad, out_grad = unpack_projections(
            place, put_c.arrays[0][0], put_c.arrays[1][0]
        )
        wide_grads = [totals[i * CELL : (i + 1) * CELL] for i in range(6)]
        head_grads = [totals[6 * CELL + i * head : 6 * CELL + (i + 1) * head] for i in range(2)]
        up_bias_grad = totals[6 * CELL + 2 * head :]
    else:
        back = lambda parts: lax.all_to_all(
            parts.transpose(1, 0, 2).reshape(parts.shape[1], D), "gy", split_axis=1, concat_axis=0, tiled=True
        )
        result, input_grad = back(results), back(input_grads)
        shares = whole_shares(mine_c, theirs_c).astype(F32)
        query_grad, key_grad, value_grad = (
            weight_block(shares[i].transpose(2, 3, 1, 0, 4).reshape(D, D), "gy", "gx") for i in range(3)
        )
        out_grad = weight_block(shares[3].transpose(1, 0, 4, 2, 3).reshape(D, D), "gx", "gy")
        shares = jnp.stack([whole_shares(mine_a, theirs_a), whole_shares(mine_b, theirs_b)]).astype(F32)
        up_grad = weight_block(shares[:, :2].transpose(4, 5, 3, 0, 1, 2, 6).reshape(D, -1), "gy", "gx")
        down_grad = weight_block(shares[:, 2:].transpose(3, 0, 1, 2, 6, 4, 5).reshape(-1, D), "gx", "gy")
        wide_sums, sums_heads, bias_up_grad = lax.psum((wide_sums, sums_heads, bias_up_grad), AXES)
        wide_grads = [lax.dynamic_slice_in_dim(wide_sums[i], index[2] * width, width) for i in range(6)]
        head_grads = [lax.dynamic_slice_in_dim(sums_heads[i], index[1] * head, head) for i in range(2)]
        up_bias_grad = lax.dynamic_slice_in_dim(bias_up_grad.reshape(-1), index[1] * feed_width, feed_width)

    return (
        result,
        input_grad,
        wide_grads[0],
        wide_grads[1],
        query_grad,
        key_grad,
        value_grad,
        head_grads[0],
        head_grads[1],
        out_grad,
        wide_grads[2],
        wide_grads[3],
        wide_grads[4],
        up_grad,
        up_bias_grad,
        down_grad,
        wide_grads[5],
    )


def solution(mesh):
    tokens = P(("dp", "gx"), "gy")
    wide, tall = P("gy"), P("gx")
    down_rows, across = P("gy", "gx"), P("gx", "gy")
    params = (
        wide, wide, down_rows, down_rows, down_rows, tall, tall, across, wide,
        wide, wide, down_rows, tall, across, wide,
    )
    return jax.shard_map(
        layer_body,
        mesh=mesh,
        in_specs=(tokens, tokens) + params,
        out_specs=(tokens, tokens) + params,
        check_vma=False,
    )
```

```python
import jax
import jax.numpy as jnp
from jax import lax
from jax.experimental import pallas as pl
from jax.experimental.pallas import tpu as pltpu
from jax.sharding import PartitionSpec as P

D = 1024
HEAD_DIM = 64
SEQ = 577
EPSILON = 1e-06
F32 = jnp.float32
BF16 = jnp.bfloat16

CELL = 256
NT = (((1,), (1,)), ((), ()))
TN = (((0,), (0,)), ((), ()))
ANY = pl.BlockSpec(memory_space=pl.ANY)
WHOLE = pl.BlockSpec(memory_space=pltpu.VMEM)
SMEM = pl.BlockSpec(memory_space=pltpu.SMEM)
LIMIT = 60 * 1024 * 1024
FEED_LIMIT = 60 * 1024 * 1024


def dot(left, right, dims=(((1,), (0,)), ((), ()))):
    return lax.dot_general(left, right, dims, preferred_element_type=F32)


def cost(flops, moved, transcendentals=0):
    return pl.CostEstimate(flops=8 * flops, bytes_accessed=moved, transcendentals=0)


AXES = ("dp", "gx", "gy")


def swap(value, axis, step):
    return lax.ppermute(value, axis, [(i, i ^ step) for i in range(lax.axis_size(axis))])


def shifted(offsets, axis, step):
    place = AXES.index(axis)
    return [o[:place] + (o[place] ^ step,) + o[place + 1 :] for o in offsets]


def doubled(pieces, offsets, axis, step):
    return (
        jnp.concatenate([pieces, swap(pieces, axis, step)], axis=0),
        offsets + shifted(offsets, axis, step),
    )


class Gather:
    orders = ((("gx", 1), ("dp", 2)), (("dp", 2), ("gx", 1)))

    def __init__(self, piece, place):
        self.place = place
        self.arrays = [piece]
        self.offsets = [[(0, 0, 0)]]

    def z(self, step):
        got, offsets = doubled(self.arrays[0], self.offsets[0], "gy", step)
        self.arrays, self.offsets = [got], [offsets]

    def xy(self, turn):
        if turn == 0:
            self.arrays = [self.arrays[0][:, half] for half in range(2)]
            self.offsets = self.offsets * 2
            for half in range(2):
                self.arrays[half], self.offsets[half] = doubled(
                    self.arrays[half], self.offsets[half], *self.orders[half][turn]
                )
        else:
            self.arrays = self.arrays + [swap(self.arrays[half], *self.orders[half][turn]) for half in range(2)]
            self.offsets = self.offsets + [shifted(self.offsets[half], *self.orders[half][turn]) for half in range(2)]

    def core(self):
        self.arrays = self.arrays + [swap(a, "dp", 1) for a in self.arrays]
        self.offsets = self.offsets + [shifted(o, "dp", 1) for o in self.offsets]

    def bundles(self):
        return Bundles(self.place, [(a, o, i % 2) for i, (a, o) in enumerate(zip(self.arrays, self.offsets))])


def fold(value, dim, bit, axis, step):
    kept = lax.dynamic_index_in_dim(value, bit, dim, keepdims=False)
    sent = lax.dynamic_index_in_dim(value, 1 - bit, dim, keepdims=False)
    return (kept.astype(F32) + swap(sent, axis, step).astype(F32)).astype(BF16)


def halve_sum(value, bit, axis, step):
    kept = lax.dynamic_index_in_dim(value, bit, 0, keepdims=False)
    sent = lax.dynamic_index_in_dim(value, 1 - bit, 0, keepdims=False)
    return kept + swap(sent, axis, step)


class Scatter:
    def __init__(self, place, theirs):
        self.place = place
        self.share, self.x_at, self.z_at = (lax.axis_index(a) for a in AXES)
        self.arrays = [theirs]

    def core(self):
        self.arrays = [swap(self.arrays[0], "dp", 1)]

    def split(self, mine):
        self.arrays = list(add_split(self.place, mine, self.arrays[0]))

    def xy(self, turn):
        high = self.share >> 1
        if turn == 0:
            kept_a, sent_a, kept_b, sent_b = self.arrays
            got_a, got_b = swap(sent_a, "dp", 2), swap(sent_b, "gx", 1)
            add = lambda u, v: (u.astype(F32) + v.astype(F32)).astype(BF16)
            self.arrays = [add(kept_a, got_a), add(kept_b, got_b)]
        else:
            first, second = self.arrays
            first, second = fold(first, 0, self.x_at, "gx", 1), fold(second, 0, high, "dp", 2)
            self.arrays = [jnp.stack([first, second]).reshape(1, 2, 2, 2, CELL, CELL)]

    def z(self, step):
        dim, bit = (3, self.z_at & 1) if step == 1 else (2, self.z_at >> 1)
        self.arrays = [fold(self.arrays[0], dim, bit, "gy", step)]

    def spread(self, step):
        both = self.arrays[0]
        other = swap(both, "dp", step)
        if step == 2:
            bit = self.share >> 1
            self.arrays = [jnp.stack([jnp.where(bit == 0, both, other), jnp.where(bit == 0, other, both)], axis=1)]
        else:
            self.arrays = [both, other]


def add_split(place, mine, got):
    block = (1, 1, 1, 4, CELL, CELL)
    flip = lambda bit, sent: 1 - bit if sent else bit
    over_dp = lambda sent: lambda j, p: (flip(p[0] >> 1, sent), 0, j, 0, 0, 0)
    over_gx = lambda sent: lambda j, p: (j, 1, flip(p[1], sent), 0, 0, 0)
    maps = [over_dp(0), over_dp(1), over_gx(0), over_gx(1)]

    def kernel(place, *refs):
        for i in range(4):
            refs[8 + i][0] = (refs[i][0, 0, 0].astype(F32) + refs[4 + i][0, 0, 0].astype(F32)).astype(BF16)

    return pl.pallas_call(
        kernel,
        grid_spec=pltpu.PrefetchScalarGridSpec(
            num_scalar_prefetch=1,
            grid=(2,),
            in_specs=[pl.BlockSpec(block, f) for f in maps] * 2,
            out_specs=[pl.BlockSpec((1, 4, CELL, CELL), lambda j, p: (j, 0, 0, 0))] * 4,
        ),
        out_shape=[jax.ShapeDtypeStruct((2, 4, CELL, CELL), BF16)] * 4,
        compiler_params=pltpu.CompilerParams(vmem_limit_bytes=24 * 1024 * 1024),
        cost_estimate=cost(0, 2 * 3 * 32 * CELL * CELL),
        name="add_split",
    )(place, mine, mine, mine, mine, got, got, got, got)


def pin(chains, *values):
    arrays = [c.arrays for c in chains]
    values, arrays = lax.optimization_barrier((values, arrays))
    for c, held in zip(chains, arrays):
        c.arrays = list(held)
    return values[0] if len(values) == 1 else values


def spread_vector(vector, axis):
    size = lax.axis_size(axis)
    pieces, offsets = vector[None], [0]
    step = size >> 1
    while step:
        pieces = jnp.concatenate([pieces, swap(pieces, axis, step)], axis=0)
        offsets = offsets + [o ^ step for o in offsets]
        step >>= 1
    index = lax.axis_index(axis)
    wanted = jnp.arange(size)[:, None]
    total = jnp.zeros((size, vector.shape[0]), F32)
    for i, offset in enumerate(offsets):
        total = total + jnp.where(wanted == (index ^ offset), pieces[i][None].astype(F32), 0.0)
    return total


def part_rows(block):
    parts = 4
    rows, cols = block.shape[0] // parts, block.shape[1]

    def kernel(x_ref, out):
        for z in range(parts):
            out[z] = x_ref[z * rows : (z + 1) * rows, :]

    return pl.pallas_call(
        kernel,
        in_specs=[WHOLE],
        out_specs=WHOLE,
        out_shape=jax.ShapeDtypeStruct((parts, rows, cols), BF16),
        compiler_params=pltpu.CompilerParams(vmem_limit_bytes=16 * 1024 * 1024),
        cost_estimate=cost(0, 4 * block.size),
        name="part_rows",
    )(block)


def unite_rows(block):
    parts, rows, cols = block.shape

    def kernel(x_ref, out):
        for z in range(parts):
            out[z * rows : (z + 1) * rows, :] = x_ref[z]

    return pl.pallas_call(
        kernel,
        in_specs=[WHOLE],
        out_specs=WHOLE,
        out_shape=jax.ShapeDtypeStruct((parts * rows, cols), BF16),
        compiler_params=pltpu.CompilerParams(vmem_limit_bytes=16 * 1024 * 1024),
        cost_estimate=cost(0, 4 * block.size),
        name="unite_rows",
    )(block)


def exchange(block):
    return lax.all_to_all(block, "gy", split_axis=0, concat_axis=0, tiled=True)


def pack(place, weights, small):
    def kernel(place, q, k, v, o, *refs):
        vectors, out, sem = refs[: len(small)], refs[-2], refs[-1]
        for share, ref in enumerate((q, k, v, o)):

            @pl.when(place[0] == share)
            def _():
                for half in range(2):
                    at = pl.ds(half * CELL, CELL)
                    source = ref.at[:, at] if share < 3 else ref.at[at, :]
                    pltpu.make_async_copy(source, out.at[0, half, 0:CELL], sem.at[half]).start()

        rows = [r[...].reshape(-1, CELL).astype(F32) for r in vectors]
        blank = jnp.zeros((6, CELL), F32)
        out[0, 0, CELL : CELL + 16, :] = jnp.concatenate(rows[:8] + [blank], axis=0).astype(BF16)
        out[0, 1, CELL : CELL + 16, :] = jnp.concatenate([rows[8], blank, blank[:2]], axis=0).astype(BF16)
        for half in range(2):
            cell = out.at[0, half, 0:CELL]
            pltpu.make_async_copy(cell, cell, sem.at[half]).wait()

    return pl.pallas_call(
        kernel,
        in_specs=[SMEM] + [ANY] * 4 + [WHOLE] * len(small),
        out_specs=WHOLE,
        out_shape=jax.ShapeDtypeStruct((1, 2, CELL + 16, CELL), BF16),
        scratch_shapes=[pltpu.SemaphoreType.DMA((2,))],
        compiler_params=pltpu.CompilerParams(vmem_limit_bytes=LIMIT),
        cost_estimate=cost(0, 8 * CELL * CELL),
        name="pack",
    )(place, *weights, *small)


def whole_weight(block, rows_axis, cols_axis):
    return lax.all_gather(lax.all_gather(block, rows_axis, axis=0, tiled=True), cols_axis, axis=1, tiled=True)


def weight_block(grad, rows_axis, cols_axis):
    part = lax.psum_scatter(grad, rows_axis, scatter_dimension=0, tiled=True)
    return lax.psum(lax.psum_scatter(part, cols_axis, scatter_dimension=1, tiled=True), "dp")


def projection_cells(weight):
    return weight.reshape(4, CELL, 2, 2, CELL).transpose(3, 2, 0, 1, 4)


def out_cells(weight):
    return weight.reshape(2, 2, CELL, 4, CELL).transpose(1, 0, 3, 2, 4)


def up_cells(weight):
    return weight.reshape(4, CELL, 2, 2, 2, 2, CELL).transpose(3, 4, 5, 2, 0, 1, 6)


def down_cells(weight):
    return weight.reshape(2, 2, 2, 2, CELL, 4, CELL).transpose(1, 2, 3, 0, 5, 4, 6)


def whole_bundles(cells, place):
    offsets = [(d, x, z) for d in range(4) for x in range(2) for z in range(4)]
    return Bundles(place, [(cells[:, half].reshape(-1, CELL, CELL), offsets, half) for half in range(2)])


def split_bundles(cells, place):
    parts = []
    for low in range(2):
        offsets = [(d, x, z) for d in (low, low + 2) for x in range(2) for z in range(4)]
        parts += [(cells[low::2, half].reshape(-1, CELL, CELL), offsets, half) for half in range(2)]
    return Bundles(place, parts)


def whole_shares(mine, theirs):
    return jnp.stack([mine, theirs], axis=1).reshape((4,) + mine.shape[1:])


class Bundles:
    def __init__(self, place, parts):
        self.place = place
        self.arrays = [p[0] for p in parts]
        self.meta = [(p[1], p[2]) for p in parts]

    def start(self, place_ref, refs, put):
        for ref, meta in zip(refs, self.meta):
            self.start_one(place_ref, ref, meta, put)

    @staticmethod
    def start_one(place_ref, ref, meta, put):
        offsets, half = meta
        for i, (od, ox, oz) in enumerate(offsets):
            put(ref.at[i, 0:CELL], place_ref[0] ^ od, half, place_ref[1] ^ ox, place_ref[2] ^ oz)


def window(ref, row, col):
    return ref.at[pl.ds(pl.multiple_of(row, CELL), CELL), pl.ds(pl.multiple_of(col, CELL), CELL)]


def put_projections(weights, sems):
    def put(source, share, half, x, z):
        @pl.when(share < 3)
        def _():
            dest = window(weights.at[share], z * CELL, (2 * x + half) * CELL)
            pltpu.make_async_copy(source, dest, sems.at[share]).start()

    return put


def put_out(weight, sem):
    def put(source, share, half, x, z):
        @pl.when(share == 3)
        def _():
            pltpu.make_async_copy(source, window(weight, (2 * x + half) * CELL, z * CELL), sem).start()

    return put


def put_feed(up, down, sems, core):
    def put(source, share, half, x, z):
        at = (2 * x + half) * CELL
        own = 1 - ((share ^ core) & 1)

        @pl.when(share < 2)
        def _():
            pltpu.make_async_copy(source, window(up.at[own], z * CELL, at), sems.at[own, 0]).start()

        @pl.when(share >= 2)
        def _():
            pltpu.make_async_copy(source, window(down.at[own], at, z * CELL), sems.at[own, 1]).start()

    return put


def wait_all(ref, sem):
    pltpu.make_async_copy(ref, ref, sem).wait()


def normal(values):
    center = values - jnp.mean(values, axis=1, keepdims=True)
    inverse = lax.rsqrt(jnp.mean(center * center, axis=1, keepdims=True) + EPSILON)
    return center * inverse, inverse


def back_norm(grad, normal_rows, inverse, gain):
    scaled = grad * gain
    mean_one = jnp.mean(scaled, axis=1, keepdims=True)
    mean_two = jnp.mean(scaled * normal_rows, axis=1, keepdims=True)
    return inverse * (scaled - mean_one - normal_rows * mean_two)


def column_sum(values):
    return jnp.sum(values, axis=0, keepdims=True)


def project(x_parts, vectors, bundles):
    parts, rows, cols = x_parts.shape
    count = len(bundles.arrays)
    given = vectors is not None

    def kernel(place, x_parts, *refs):
        if given:
            vec, *refs = refs
        sources = refs[:count]
        q_ref, x_ref, nt_ref, *refs = refs[count:]
        if not given:
            vec, up_ref, vbuf, vsem, *refs = refs
        weights, n_ref, sems = refs
        step = pl.program_id(0)

        @pl.when(step == 0)
        def _():
            if not given:
                for ref, (offsets, half) in zip(sources, bundles.meta):
                    for i, (od, ox, oz) in enumerate(offsets):
                        if od == 0:
                            dest = vbuf.at[half, place[1] ^ ox, place[2] ^ oz]
                            pltpu.make_async_copy(ref.at[i, CELL : CELL + 16], dest, vsem).start()
            bundles.start(place, sources, put_projections(weights, sems))
            if not given:
                wait_all(vbuf, vsem)
                tall = lambda row: [vbuf[0, x, 0, row + i : row + i + 1, :] for x in range(2) for i in range(2)]
                wide = lambda row: [vbuf[0, 0, z, row : row + 1, :] for z in range(4)]
                pieces = [wide(0), wide(1), tall(6), tall(8), wide(2), wide(3), wide(4), wide(5)]
                for i, cut in enumerate(pieces):
                    vec[i : i + 1, :] = jnp.concatenate(cut, axis=1).astype(F32)
                for part in range(2):
                    cut = [vbuf[1, x, 0, 4 * part + i : 4 * part + i + 1, :] for x in range(2) for i in range(4)]
                    up_ref[part] = jnp.concatenate(cut, axis=1).astype(F32)
            x = jnp.concatenate([x_parts[z] for z in range(parts)], axis=1)
            x_ref[...] = x
            normal_rows, _ = normal(x.astype(F32))
            normed = (normal_rows * vec[0:1, :] + vec[1:2, :]).astype(BF16)
            n_ref[...] = normed
            nt_ref[...] = normed.T

        for share in range(3):

            @pl.when(step == share)
            def _():
                wait_all(weights.at[share], sems.at[share])
                total = dot(n_ref[...], weights[share])
                if share != 1:
                    total = total + vec[2 + share // 2 : 3 + share // 2, :]
                q_ref[0] = total.astype(BF16)

    extra = [] if given else [jax.ShapeDtypeStruct((8, D), F32), jax.ShapeDtypeStruct((2, 1, 2 * D), F32)]
    outs = pl.pallas_call(
        kernel,
        grid=(3,),
        in_specs=[SMEM, WHOLE] + [WHOLE] * given + [ANY] * count,
        out_specs=[pl.BlockSpec((1, rows, D), lambda s: (s, 0, 0)), WHOLE, WHOLE] + [WHOLE] * len(extra),
        out_shape=[
            jax.ShapeDtypeStruct((3, rows, D), BF16),
            jax.ShapeDtypeStruct((rows, D), BF16),
            jax.ShapeDtypeStruct((D, rows), BF16),
        ]
        + extra,
        scratch_shapes=([] if given else [pltpu.VMEM((2, 2, 4, 16, CELL), BF16), pltpu.SemaphoreType.DMA])
        + [
            pltpu.VMEM((3, D, D), BF16),
            pltpu.VMEM((rows, D), BF16),
            pltpu.SemaphoreType.DMA((3,)),
        ],
        compiler_params=pltpu.CompilerParams(vmem_limit_bytes=LIMIT),
        cost_estimate=cost(6 * rows * D * D, 6 * D * D + 12 * rows * D),
        name="project",
    )(bundles.place, x_parts, *([vectors] if given else []), *bundles.arrays)
    return outs if not given else (*outs, vectors, None)


def attend(qkv, begin, end):
    rows = qkv.shape[1]
    pairs = end - begin

    def kernel(q_ref, k_ref, v_ref, o_ref, lse_ref, buf):
        q, k, v = q_ref[0], k_ref[0], v_ref[0]
        first = lax.broadcasted_iota(jnp.int32, (1, 128), 1) < 64
        scale = HEAD_DIM**-0.5
        outs = []
        for h in range(2):
            mine = first if h == 0 else jnp.logical_not(first)
            qh = jnp.where(mine, q.astype(F32) * scale, 0.0).astype(BF16)
            s = dot(qh, k, NT)
            top = jnp.max(s, axis=1, keepdims=True)
            p = jnp.exp(s - top)
            total = jnp.sum(p, axis=1, keepdims=True)
            outs.append(dot(p.astype(BF16), v) / total)
            buf[0:rows, h : h + 1] = top + jnp.log(total)
        o_ref[...] = jnp.where(first, outs[0], outs[1]).astype(BF16)
        lse_ref[0] = buf[...].T[0:8, 0:rows]

    spec = lambda i: pl.BlockSpec((1, rows, 128), lambda s, i=i: (i, 0, s + begin))
    return pl.pallas_call(
        kernel,
        grid=(pairs,),
        in_specs=[spec(0), spec(1), spec(2)],
        out_specs=[pl.BlockSpec((rows, 128), lambda s: (0, s)), pl.BlockSpec((1, 8, rows), lambda s: (s, 0, 0))],
        out_shape=[
            jax.ShapeDtypeStruct((rows, pairs * 128), BF16),
            jax.ShapeDtypeStruct((pairs, 8, rows), F32),
        ],
        scratch_shapes=[pltpu.VMEM((640, 128), F32)],
        compiler_params=pltpu.CompilerParams(vmem_limit_bytes=LIMIT),
        cost_estimate=cost(2048 * pairs * rows * rows, 1024 * pairs * rows, 2 * pairs * rows * rows),
        name="attend",
    )(qkv, qkv, qkv)


def attend_back(qkv, mixture, lse, mixture_grad, begin, end):
    rows = qkv.shape[1]
    pairs = end - begin

    def kernel(q_ref, k_ref, v_ref, o_ref, lse_ref, do_ref, g_ref, b_ref):
        q, k, v, grad = q_ref[0], k_ref[0], v_ref[0], do_ref[...]
        first = lax.broadcasted_iota(jnp.int32, (1, 128), 1) < 64
        scale = HEAD_DIM**-0.5
        pick = lax.broadcasted_iota(jnp.int32, (8, 128), 0) == lax.broadcasted_iota(jnp.int32, (8, 128), 1) // 64
        product = grad.astype(F32) * o_ref[...].astype(F32)
        delta = lax.dot_general(
            jnp.where(pick, 1.0, 0.0), product, NT, precision=lax.Precision.HIGHEST, preferred_element_type=F32
        )
        dqs, dks, dvs = [], [], []
        for h in range(2):
            mine = first if h == 0 else jnp.logical_not(first)
            qh = jnp.where(mine, q.astype(F32) * scale, 0.0).astype(BF16)
            gh = jnp.where(mine, grad, jnp.zeros_like(grad))
            p = jnp.exp(dot(k, qh, NT) - lse_ref[0, h : h + 1, :])
            dp = dot(v, gh, NT)
            ds = (p * (dp - delta[h : h + 1, :])).astype(BF16)
            dvs.append(dot(p.astype(BF16), grad))
            dks.append(dot(ds, q))
            dqs.append(dot(k, ds, TN))
        dq = (jnp.concatenate([dqs[0][:64], dqs[1][64:]], axis=0) * scale).T.astype(BF16)
        dk = (jnp.where(first, dks[0], dks[1]) * scale).astype(BF16)
        dv = jnp.where(first, dvs[0], dvs[1]).astype(BF16)
        g_ref[0], g_ref[1], g_ref[2] = dq, dk, dv
        b_ref[0:1, :] = column_sum(dq.astype(F32))
        b_ref[1:2, :] = column_sum(dv.astype(F32))

    spec = lambda i: pl.BlockSpec((1, rows, 128), lambda s, i=i: (i, 0, s + begin))
    flat = pl.BlockSpec((rows, 128), lambda s: (0, s))
    wide = pl.BlockSpec((rows, 128), lambda s: (0, s + begin))
    return pl.pallas_call(
        kernel,
        grid=(pairs,),
        in_specs=[spec(0), spec(1), spec(2), flat, pl.BlockSpec((1, 8, rows), lambda s: (s, 0, 0)), wide],
        out_specs=[pl.BlockSpec((3, rows, 128), lambda s: (0, 0, s)), pl.BlockSpec((8, 128), lambda s: (0, s))],
        out_shape=[
            jax.ShapeDtypeStruct((3, rows, pairs * 128), BF16),
            jax.ShapeDtypeStruct((8, pairs * 128), F32),
        ],
        compiler_params=pltpu.CompilerParams(vmem_limit_bytes=32 * 1024 * 1024),
        cost_estimate=cost(6000 * pairs * rows * rows, 2048 * pairs * rows, 2 * pairs * rows * rows),
        name="attend_back",
    )(qkv, qkv, qkv, mixture, lse, mixture_grad)


def mix_out(mixtures, inputs, vectors, bundles):
    rows = inputs.shape[0]
    count = len(bundles.arrays)

    def kernel(place, vec, m_ref, o_ref, x_ref, *refs):
        sources = refs[:count]
        mid_ref, n_ref, nt_ref, weight, sem = refs[count:]
        bundles.start(place, sources, put_out(weight, sem))
        wait_all(weight, sem)
        mixture = jnp.concatenate([m_ref[...], o_ref[...]], axis=1)
        middle = x_ref[...].astype(F32) + (dot(mixture, weight[...]) + vec[4:5, :])
        mid_ref[...] = middle
        normal_rows, _ = normal(middle)
        normed = (normal_rows * vec[5:6, :] + vec[6:7, :]).astype(BF16)
        n_ref[...] = normed
        nt_ref[...] = normed.T

    return pl.pallas_call(
        kernel,
        in_specs=[SMEM] + [WHOLE] * 4 + [ANY] * count,
        out_specs=[WHOLE] * 3,
        out_shape=[
            jax.ShapeDtypeStruct((rows, D), F32),
            jax.ShapeDtypeStruct((rows, D), BF16),
            jax.ShapeDtypeStruct((D, rows), BF16),
        ],
        scratch_shapes=[pltpu.VMEM((D, D), BF16), pltpu.SemaphoreType.DMA],
        compiler_params=pltpu.CompilerParams(vmem_limit_bytes=LIMIT),
        cost_estimate=cost(2 * rows * D * D, 2 * D * D + 10 * rows * D),
        name="mix_out",
    )(bundles.place, vectors, *mixtures, inputs, *bundles.arrays)


def gelu_pair(h):
    below = 0.5 * (1.0 + lax.erf(h * 0.7071067811865476))
    bell = jnp.exp(h * h * -0.5) * 0.3989422804014327
    return h * below, below + h * bell


def feed(acts, up_bias, bundles, partials):
    rows = acts[0].shape[0]
    tile = 2 * CELL
    count = len(bundles.arrays)
    olds = [] if partials is None else list(partials)
    carried = len(olds)

    def kernel(place, bias, n_ref, nt_ref, g_ref, gt_ref, *refs):
        olds, sources = refs[:carried], refs[carried : carried + count]
        out_acc, back_acc, mine, theirs, bias_ref, up, down, sems = refs[carried + count :]
        step = pl.program_id(0)
        own = step // 2
        x = lax.rem(step, 2)
        core = place[0] & 1
        sub = jnp.where(step < 2, 1 - core, core)

        @pl.when(step == 0)
        def _():
            order = list(range(count // 2, count)) + list(range(count // 2))
            put = put_feed(up, down, sems, core)
            for i in order:
                Bundles.start_one(place, sources[i], bundles.meta[i], put)
            for acc, old in zip((out_acc, back_acc), olds):
                acc[...] = old[...]
            if not carried:
                out_acc[...] = jnp.zeros_like(out_acc)
                back_acc[...] = jnp.zeros_like(back_acc)

        for i in range(2):

            @pl.when(step == 2 * i)
            def _():
                wait_all(up.at[i], sems.at[i, 0])
                wait_all(down.at[i], sems.at[i, 1])

        at = pl.multiple_of(x * tile, tile)
        bias_at = pl.multiple_of((2 * x + sub) * tile, tile)
        up_tile = up[own, :, pl.ds(at, tile)]
        down_tile = down[own, pl.ds(at, tile), :]
        pre = dot(n_ref[...], up_tile) + bias[0:1, pl.ds(bias_at, tile)]
        hidden, slope = gelu_pair(pre)
        hidden = hidden.astype(BF16)
        out_acc[...] += dot(hidden, down_tile)
        pre_grad = (dot(g_ref[...], down_tile, NT) * slope).astype(BF16)
        back_acc[...] += dot(pre_grad, up_tile, NT)
        bias_ref[0, 0] = column_sum(pre_grad.astype(F32))
        up_grad, down_grad = dot(nt_ref[...], pre_grad).astype(BF16), dot(gt_ref[...], hidden).astype(BF16)

        def leave(cells):
            for i, grad in enumerate((up_grad, down_grad)):
                for half in range(2):
                    for z in range(4):
                        cell = grad[z * CELL : (z + 1) * CELL, half * CELL : (half + 1) * CELL]
                        cells[i, half, 0, z] = cell

        @pl.when(step < 2)
        def _():
            leave(theirs)

        @pl.when(step >= 2)
        def _():
            leave(mine)

    acc = jax.ShapeDtypeStruct((rows, D), F32)
    full = lambda shape: pl.BlockSpec(shape, lambda s, p: (0,) * len(shape))
    block = (2, 2, 1, 4, CELL, CELL)
    cells = jax.ShapeDtypeStruct((2, 2, 2, 4, CELL, CELL), BF16)
    ins = [up_bias, *acts, *olds]
    low = lambda s, p: jnp.where(s < 2, 1 - (p[0] & 1), p[0] & 1)
    return pl.pallas_call(
        kernel,
        grid_spec=pltpu.PrefetchScalarGridSpec(
            num_scalar_prefetch=1,
            grid=(4,),
            in_specs=[full(v.shape) for v in ins] + [ANY] * count,
            out_specs=[
                full((rows, D)),
                full((rows, D)),
                pl.BlockSpec(block, lambda s, p: (0, 0, jnp.maximum(s - 2, 0), 0, 0, 0)),
                pl.BlockSpec(block, lambda s, p: (0, 0, jnp.minimum(s, 1), 0, 0, 0)),
                pl.BlockSpec((1, 1, 1, tile), lambda s, p: (lax.rem(s, 2), low(s, p), 0, 0)),
            ],
            scratch_shapes=[
                pltpu.VMEM((2, D, 2 * tile), BF16),
                pltpu.VMEM((2, 2 * tile, D), BF16),
                pltpu.SemaphoreType.DMA((2, 2)),
            ],
        ),
        out_shape=[acc, acc, cells, cells, jax.ShapeDtypeStruct((2, 2, 1, tile), F32)],
        compiler_params=pltpu.CompilerParams(vmem_limit_bytes=FEED_LIMIT),
        cost_estimate=cost(48 * rows * D * tile, 32 * D * tile + 28 * rows * D, 8 * rows * tile),
        name="feed",
    )(bundles.place, *ins, *bundles.arrays)


def turn(middle, cotangent, out_sum, back_sum, vectors, bundles):
    rows = middle.shape[0]
    count = len(bundles.arrays)
    parts = 4

    def kernel(place, vec, mid_ref, g_ref, out_ref, back_ref, *refs):
        sources = refs[:count]
        pieces, grad_ref, branch_t, mix_ref, sum_ref, weight, sem = refs[count:]
        bundles.start(place, sources, put_out(weight, sem))
        middle = mid_ref[...]
        result = (middle + (out_ref[...] + vec[7:8, :])).astype(BF16)
        for k in range(parts):
            pieces[k] = result[:, k * CELL : (k + 1) * CELL]
        normal_rows, inverse = normal(middle)
        back = back_ref[...]
        grads = g_ref[...].astype(F32)
        middle_grad = grads + back_norm(back, normal_rows, inverse, vec[5:6, :])
        grad_ref[...] = middle_grad
        branch = middle_grad.astype(BF16)
        branch_t[...] = branch.T
        sum_ref[0:1, :] = column_sum(branch.astype(F32))
        sum_ref[1:2, :] = column_sum(back * normal_rows)
        sum_ref[2:3, :] = column_sum(back)
        sum_ref[3:4, :] = column_sum(grads)
        wait_all(weight, sem)
        mix_ref[...] = dot(branch, weight[...], NT).astype(BF16)

    full = jax.ShapeDtypeStruct((rows, D), BF16)
    return pl.pallas_call(
        kernel,
        in_specs=[SMEM] + [WHOLE] * 5 + [ANY] * count,
        out_specs=[WHOLE] * 5,
        out_shape=[
            jax.ShapeDtypeStruct((parts, rows, CELL), BF16),
            jax.ShapeDtypeStruct((rows, D), F32),
            jax.ShapeDtypeStruct((D, rows), BF16),
            full,
            jax.ShapeDtypeStruct((8, D), F32),
        ],
        scratch_shapes=[
            pltpu.VMEM((D, D), BF16),
            pltpu.SemaphoreType.DMA,
        ],
        compiler_params=pltpu.CompilerParams(vmem_limit_bytes=LIMIT),
        cost_estimate=cost(2 * rows * D * D, 2 * D * D + 24 * rows * D),
        name="turn",
    )(bundles.place, vectors, middle, cotangent, out_sum, back_sum, *bundles.arrays)


def weigh(place, normed_t, branch_t, grads, mixtures, other):
    rows = normed_t.shape[1]

    def kernel(place, n_t, b_t, g0, g1, m0, m1, cells):
        core = place[0] & 1
        share = 2 * pl.program_id(0) + (1 - core if other else core)

        def fill(left, right):
            for x in range(2):
                for half in range(2):
                    grad = dot(left, right(x, half * CELL)).astype(BF16)
                    cells[0, half, x] = grad.reshape(4, CELL, CELL)

        for k in range(3):

            @pl.when(share == k)
            def _():
                fill(n_t[...], lambda x, at: (g0, g1)[x][k, :, at : at + CELL])

        @pl.when(share == 3)
        def _():
            fill(b_t[...], lambda x, at: (m0, m1)[x][:, at : at + CELL])

    return pl.pallas_call(
        kernel,
        grid=(2,),
        in_specs=[SMEM] + [WHOLE] * 6,
        out_specs=pl.BlockSpec((1, 2, 2, 4, CELL, CELL), lambda s: (s, 0, 0, 0, 0, 0)),
        out_shape=jax.ShapeDtypeStruct((2, 2, 2, 4, CELL, CELL), BF16),
        compiler_params=pltpu.CompilerParams(vmem_limit_bytes=32 * 1024 * 1024),
        cost_estimate=cost(4 * rows * D * D, 4 * D * D + 12 * rows * D),
        name="weigh",
    )(place, normed_t, branch_t, *grads, *mixtures)


def finish(inputs, middle_grad, grads, vectors, bundles):
    rows = inputs.shape[0]
    count = len(bundles.arrays)
    parts = 4

    def kernel(place, vec, x_ref, mid_ref, g0, g1, *refs):
        sources = refs[:count]
        pieces, sum_ref, weights, sems = refs[count:]
        bundles.start(place, sources, put_projections(weights, sems))
        normal_rows, inverse = normal(x_ref[...].astype(F32))
        back = None
        for k in range(3):
            wait_all(weights.at[k], sems.at[k])
            term = dot(jnp.concatenate([g0[k], g1[k]], axis=1), weights[k], NT)
            back = term if back is None else back + term
        result = (mid_ref[...] + back_norm(back, normal_rows, inverse, vec[0:1, :])).astype(BF16)
        for k in range(parts):
            pieces[k] = result[:, k * CELL : (k + 1) * CELL]
        sum_ref[0:1, :] = column_sum(back * normal_rows)
        sum_ref[1:2, :] = column_sum(back)

    return pl.pallas_call(
        kernel,
        in_specs=[SMEM] + [WHOLE] * 5 + [ANY] * count,
        out_specs=[WHOLE] * 2,
        out_shape=[jax.ShapeDtypeStruct((parts, rows, CELL), BF16), jax.ShapeDtypeStruct((8, D), F32)],
        scratch_shapes=[pltpu.VMEM((3, D, D), BF16), pltpu.SemaphoreType.DMA((3,))],
        compiler_params=pltpu.CompilerParams(vmem_limit_bytes=32 * 1024 * 1024),
        cost_estimate=cost(6 * rows * D * D, 6 * D * D + 14 * rows * D),
        name="finish",
    )(bundles.place, vectors, inputs, middle_grad, *grads, *bundles.arrays)


def unpack_projections(place, own, other):
    def kernel(place, a_ref, b_ref, *refs):
        outs, buf = refs[:4], refs[4]
        core = place[0] & 1
        buf[core] = a_ref[...]
        buf[1 - core] = b_ref[...]
        for share in range(4):
            for half in range(2):
                cell = buf[share % 2, share // 2, half]
                at = slice(half * CELL, (half + 1) * CELL)
                if share < 3:
                    outs[share][:, at] = cell.astype(F32)
                else:
                    outs[share][at, :] = cell.astype(F32).T

    tall, wide = (jax.ShapeDtypeStruct(s, F32) for s in ((2 * CELL, CELL), (CELL, 2 * CELL)))
    return pl.pallas_call(
        kernel,
        in_specs=[SMEM, WHOLE, WHOLE],
        out_specs=[WHOLE] * 4,
        out_shape=[wide, wide, wide, tall],
        scratch_shapes=[pltpu.VMEM((2, 2, 2, CELL, CELL), BF16)],
        compiler_params=pltpu.CompilerParams(vmem_limit_bytes=LIMIT),
        cost_estimate=cost(0, 3 * 16 * CELL * CELL),
        name="unpack_projections",
    )(place, own, other)


def unpack_feed(place, own, other):
    def kernel(place, a_ref, b_ref, up_ref, down_ref, buf):
        core = place[0] & 1
        buf[core] = a_ref[...]
        buf[1 - core] = b_ref[...]
        for part in range(2):
            for sub in range(2):
                for half in range(2):
                    at = (4 * part + 2 * sub + half) * CELL
                    up_ref[:, at : at + CELL] = buf[sub, part, 0, half].astype(F32)
                    down_ref[at : at + CELL, :] = buf[sub, part, 1, half].astype(F32).T

    return pl.pallas_call(
        kernel,
        in_specs=[SMEM, WHOLE, WHOLE],
        out_specs=[WHOLE] * 2,
        out_shape=[jax.ShapeDtypeStruct((CELL, 8 * CELL), F32), jax.ShapeDtypeStruct((8 * CELL, CELL), F32)],
        scratch_shapes=[pltpu.VMEM((2, 2, 2, 2, CELL, CELL), BF16)],
        compiler_params=pltpu.CompilerParams(vmem_limit_bytes=LIMIT),
        cost_estimate=cost(0, 6 * 16 * CELL * CELL),
        name="unpack_feed",
    )(place, own, other)


def join(x_parts):
    parts, rows, cols = x_parts.shape

    def kernel(x_ref, out, out_t):
        for k in range(parts):
            at = slice(k * cols, (k + 1) * cols)
            out[:, at] = x_ref[k]
            out_t[at, :] = x_ref[k].T

    return pl.pallas_call(
        kernel,
        in_specs=[WHOLE],
        out_specs=[WHOLE] * 2,
        out_shape=[
            jax.ShapeDtypeStruct((rows, cols * parts), BF16),
            jax.ShapeDtypeStruct((cols * parts, rows), BF16),
        ],
        compiler_params=pltpu.CompilerParams(vmem_limit_bytes=24 * 1024 * 1024),
        cost_estimate=cost(0, 6 * rows * cols * parts),
        name="join",
    )(x_parts)


def layer_body(*args):
    (
        layer_input,
        output_grad,
        first_gain,
        first_shift,
        query_weight,
        key_weight,
        value_weight,
        query_bias,
        value_bias,
        out_weight,
        out_bias,
        second_gain,
        second_shift,
        up_weight,
        up_bias,
        down_weight,
        down_bias,
    ) = args
    shape = tuple(lax.axis_size(a) for a in AXES)
    fast = shape == (4, 2, 4)
    width = first_gain.shape[0]
    head = query_bias.shape[0]
    feed_width = up_bias.shape[0]
    index = [lax.axis_index(a) for a in AXES]
    place = jnp.stack(index if fast else [jnp.int32(0)] * 3).astype(jnp.int32)

    small = [first_gain, first_shift, out_bias, second_gain, second_shift, down_bias, query_bias, value_bias, up_bias]
    if fast:
        get_j = Gather(pack(place, (query_weight, key_weight, value_weight, out_weight), small), place)
        get_j.z(2)
        x_block, ups, downs = pin([], layer_input, up_weight, down_weight)
        x_copies = part_rows(x_block)
        ups = ups.reshape(CELL, 2, 2, 2, CELL).transpose(2, 1, 3, 0, 4)
        downs = downs.reshape(2, 2, 2, CELL, CELL).transpose(1, 0, 2, 3, 4)
        feeds = lax.dynamic_index_in_dim(jnp.concatenate([ups, downs]), index[0], 0, keepdims=False)
        get_j.z(1)
        x_parts = exchange(pin([get_j], x_copies))
        get_j.xy(0)
        get_j.xy(1)
        x_parts, feeds = pin([], x_parts, feeds)
        get_a, get_b = (Gather(feeds[i : i + 1], place) for i in range(2))
        get_a.z(2)
        get_j.core()
        joined = get_j.bundles()
        vectors = None
        get_a.z(1)
        x_parts, output_grad = pin([get_a, get_b], x_parts, output_grad)
        get_a.xy(0)
        get_b.z(2)
    else:
        wide = spread_vector(jnp.concatenate(small[:6]), "gy").reshape(-1, 6, width)
        wide = wide.transpose(1, 0, 2).reshape(6, D)
        tall = spread_vector(jnp.concatenate(small[6:]), "gx")
        vectors = jnp.stack(
            [
                wide[0],
                wide[1],
                tall[:, :head].reshape(-1),
                tall[:, head : 2 * head].reshape(-1),
                wide[2],
                wide[3],
                wide[4],
                wide[5],
            ]
        )
        bias_up = tall[:, 2 * head :].reshape(2, 2, D).transpose(1, 0, 2).reshape(2, 1, 2 * D)
        by_parts = lambda rows: rows.reshape(rows.shape[0], 4, CELL).transpose(1, 0, 2)
        x_parts = by_parts(lax.all_to_all(layer_input, "gy", split_axis=0, concat_axis=1, tiled=True))
        grad_parts = by_parts(lax.all_to_all(output_grad, "gy", split_axis=0, concat_axis=1, tiled=True))
        joined = whole_bundles(
            jnp.stack(
                [projection_cells(whole_weight(w, "gy", "gx")) for w in (query_weight, key_weight, value_weight)]
                + [out_cells(whole_weight(out_weight, "gx", "gy"))]
            ),
            place,
        )
        ups = up_cells(whole_weight(up_weight, "gy", "gx"))
        downs = down_cells(whole_weight(down_weight, "gx", "gy"))
        both = [jnp.concatenate([ups[i], downs[i]]) for i in range(2)]
        fed = [split_bundles(c, place) for c in both]

    qkv, inputs, normed_t, vectors, bias_given = project(x_parts, vectors, joined)
    if fast:
        bias_up = bias_given
        qkv = pin([get_a, get_b], qkv)
        get_a.xy(1)
        get_b.z(1)
    mixture_0, lse_0 = attend(qkv, 0, 4)
    if fast:
        qkv, mixture_0, output_grad = pin([get_b], qkv, mixture_0, output_grad)
        grad_parts = exchange(part_rows(output_grad))
    mixture_1, lse_1 = attend(qkv, 4, 8)
    mixtures = (mixture_0, mixture_1)
    if fast:
        mixtures = pin([get_a, get_b], mixtures)
        get_b.xy(0)
        get_a.core()
        fed = [get_a.bundles()]
    middle, normed_two, normed_two_t = mix_out(mixtures, inputs, vectors, joined)
    cotangent, cotangent_t = join(grad_parts)
    if fast:
        normed_two = pin([get_b], normed_two)
        get_b.xy(1)
    acts = (normed_two, normed_two_t, cotangent, cotangent_t)
    *sums, mine_a, theirs_a, bias_a = feed(acts, bias_up[0], fed[0], None)
    if fast:
        sums, theirs_a = pin([get_b], sums, theirs_a)
        get_b.core()
        fed.append(get_b.bundles())
        put_a = Scatter(place, theirs_a)
        put_a.core()
    *sums, mine_b, theirs_b, bias_b = feed(acts, bias_up[1], fed[1], sums)
    if fast:
        put_b = Scatter(place, theirs_b)
        put_b.core()
        sums, mine_a = pin([put_a], sums, mine_a)
        put_a.split(mine_a)
        sums = pin([put_a], sums)
        put_a.xy(0)
    results, middle_grad, branch_t, mixture_grad, sums_two = turn(middle, cotangent, *sums, vectors, joined)
    if fast:
        mine_b, mixture_grad, results = pin([put_b], mine_b, mixture_grad, results)
        put_b.split(mine_b)
        mixture_grad = pin([put_b], mixture_grad)
        results = exchange(results)
    grads_0, heads_0 = attend_back(qkv, mixtures[0], lse_0, mixture_grad, 0, 4)
    if fast:
        mixture_grad, grads_0 = pin([put_a], mixture_grad, grads_0)
        put_a.xy(1)
        put_b.xy(0)
    grads_1, heads_1 = attend_back(qkv, mixtures[1], lse_1, mixture_grad, 4, 8)
    grads = (grads_0, grads_1)
    if fast:
        grads, results = pin([put_a], grads, results)
        put_a.z(1)
    theirs_c = weigh(place, normed_t, branch_t, grads, mixtures, True)
    if fast:
        put_c = Scatter(place, theirs_c)
        put_c.core()
        grads, theirs_c = pin([put_b], grads, theirs_c)
        put_b.xy(1)
    mine_c = weigh(place, normed_t, branch_t, grads, mixtures, False)
    if fast:
        mine_c, middle_grad = pin([put_a, put_b, put_c], mine_c, middle_grad)
        put_c.split(mine_c)
        middle_grad = pin([put_c], middle_grad)
        put_c.xy(0)
        put_a.z(2)
        put_b.z(1)
    input_grads, sums_one = finish(inputs, middle_grad, grads, vectors, joined)

    bias_up_grad = jnp.stack([bias_a, bias_b]).transpose(1, 0, 2, 3, 4).reshape(2, -1)
    sums_heads = jnp.concatenate([heads_0[:2], heads_1[:2]], axis=1)
    wide_sums = jnp.concatenate([sums_one[:2], sums_two[:4]])
    if fast:
        by_z = wide_sums.reshape(6, 1, 4, CELL).transpose(1, 2, 0, 3).reshape(1, 4, 6 * CELL)
        by_x = jnp.concatenate(
            [sums_heads.reshape(2, 2, head).transpose(1, 0, 2).reshape(2, 2 * head), bias_up_grad], axis=1
        )
        totals = jnp.concatenate(
            [jnp.broadcast_to(by_z, (2, 4, 6 * CELL)), jnp.broadcast_to(by_x[:, None], (2, 4, by_x.shape[1]))], axis=2
        )
        input_grads, totals = pin([put_c, put_b], input_grads, totals)
        put_c.xy(1)
        input_grads = exchange(input_grads)
        put_b.z(2)
        put_f = Scatter(place, None)
        put_f.arrays = [jnp.concatenate([put_a.arrays[0], put_b.arrays[0]])]
        put_f.spread(2)
        totals = halve_sum(totals, index[1], "gx", 1)
        totals = halve_sum(totals.reshape(2, 2, -1), index[2] >> 1, "gy", 2)
        result = results
        put_c.z(1)
        put_f.spread(1)
        totals = halve_sum(totals, index[2] & 1, "gy", 1)
        result = unite_rows(result)
        put_c.z(2)
        totals = totals + swap(totals, "dp", 1)
        up_grad, down_grad = unpack_feed(place, put_f.arrays[0], put_f.arrays[1])
        put_c.spread(2)
        totals = totals + swap(totals, "dp", 2)
        input_grad = unite_rows(input_grads)
        up_grad, down_grad, totals, result = pin([put_c], up_grad, down_grad, totals, result)
        put_c.spread(1)
        query_grad, key_grad, value_grad, out_grad = unpack_projections(
            place, put_c.arrays[0][0], put_c.arrays[1][0]
        )
        wide_grads = [totals[i * CELL : (i + 1) * CELL] for i in range(6)]
        head_grads = [totals[6 * CELL + i * head : 6 * CELL + (i + 1) * head] for i in range(2)]
        up_bias_grad = totals[6 * CELL + 2 * head :]
    else:
        back = lambda parts: lax.all_to_all(
            parts.transpose(1, 0, 2).reshape(parts.shape[1], D), "gy", split_axis=1, concat_axis=0, tiled=True
        )
        result, input_grad = back(results), back(input_grads)
        shares = whole_shares(mine_c, theirs_c).astype(F32)
        query_grad, key_grad, value_grad = (
            weight_block(shares[i].transpose(2, 3, 1, 0, 4).reshape(D, D), "gy", "gx") for i in range(3)
        )
        out_grad = weight_block(shares[3].transpose(1, 0, 4, 2, 3).reshape(D, D), "gx", "gy")
        shares = jnp.stack([whole_shares(mine_a, theirs_a), whole_shares(mine_b, theirs_b)]).astype(F32)
        up_grad = weight_block(shares[:, :2].transpose(4, 5, 3, 0, 1, 2, 6).reshape(D, -1), "gy", "gx")
        down_grad = weight_block(shares[:, 2:].transpose(3, 0, 1, 2, 6, 4, 5).reshape(-1, D), "gx", "gy")
        wide_sums, sums_heads, bias_up_grad = lax.psum((wide_sums, sums_heads, bias_up_grad), AXES)
        wide_grads = [lax.dynamic_slice_in_dim(wide_sums[i], index[2] * width, width) for i in range(6)]
        head_grads = [lax.dynamic_slice_in_dim(sums_heads[i], index[1] * head, head) for i in range(2)]
        up_bias_grad = lax.dynamic_slice_in_dim(bias_up_grad.reshape(-1), index[1] * feed_width, feed_width)

    return (
        result,
        input_grad,
        wide_grads[0],
        wide_grads[1],
        query_grad,
        key_grad,
        value_grad,
        head_grads[0],
        head_grads[1],
        out_grad,
        wide_grads[2],
        wide_grads[3],
        wide_grads[4],
        up_grad,
        up_bias_grad,
        down_grad,
        wide_grads[5],
    )


def solution(mesh):
    tokens = P(("dp", "gx"), "gy")
    wide, tall = P("gy"), P("gx")
    down_rows, across = P("gy", "gx"), P("gx", "gy")
    params = (
        wide, wide, down_rows, down_rows, down_rows, tall, tall, across, wide,
        wide, wide, down_rows, tall, across, wide,
    )
    return jax.shard_map(
        layer_body,
        mesh=mesh,
        in_specs=(tokens, tokens) + params,
        out_specs=(tokens, tokens) + params,
        check_vma=False,
    )
```

```python
import jax
import jax.numpy as jnp
from jax import lax
from jax.experimental import pallas as pl
from jax.experimental.pallas import tpu as pltpu
from jax.sharding import PartitionSpec as P

D = 1024
HEAD_DIM = 64
SEQ = 577
EPSILON = 1e-06
F32 = jnp.float32
BF16 = jnp.bfloat16

CELL = 256
NT = (((1,), (1,)), ((), ()))
TN = (((0,), (0,)), ((), ()))
ANY = pl.BlockSpec(memory_space=pl.ANY)
WHOLE = pl.BlockSpec(memory_space=pltpu.VMEM)
SMEM = pl.BlockSpec(memory_space=pltpu.SMEM)
LIMIT = 60 * 1024 * 1024
FEED_LIMIT = 60 * 1024 * 1024


def dot(left, right, dims=(((1,), (0,)), ((), ()))):
    return lax.dot_general(left, right, dims, preferred_element_type=F32)


def cost(flops, moved, transcendentals=0):
    return pl.CostEstimate(flops=8 * flops, bytes_accessed=moved, transcendentals=0)


AXES = ("dp", "gx", "gy")


def swap(value, axis, step):
    return lax.ppermute(value, axis, [(i, i ^ step) for i in range(lax.axis_size(axis))])


def shifted(offsets, axis, step):
    place = AXES.index(axis)
    return [o[:place] + (o[place] ^ step,) + o[place + 1 :] for o in offsets]


def doubled(pieces, offsets, axis, step):
    return (
        jnp.concatenate([pieces, swap(pieces, axis, step)], axis=0),
        offsets + shifted(offsets, axis, step),
    )


class Gather:
    orders = ((("gx", 1), ("dp", 2)), (("dp", 2), ("gx", 1)))

    def __init__(self, piece, place):
        self.place = place
        self.arrays = [piece]
        self.offsets = [[(0, 0, 0)]]

    def z(self, step):
        got, offsets = doubled(self.arrays[0], self.offsets[0], "gy", step)
        self.arrays, self.offsets = [got], [offsets]

    def xy(self, turn):
        if turn == 0:
            self.arrays = [self.arrays[0][:, half] for half in range(2)]
            self.offsets = self.offsets * 2
            for half in range(2):
                self.arrays[half], self.offsets[half] = doubled(
                    self.arrays[half], self.offsets[half], *self.orders[half][turn]
                )
        else:
            self.arrays = self.arrays + [swap(self.arrays[half], *self.orders[half][turn]) for half in range(2)]
            self.offsets = self.offsets + [shifted(self.offsets[half], *self.orders[half][turn]) for half in range(2)]

    def core(self):
        self.arrays = self.arrays + [swap(a, "dp", 1) for a in self.arrays]
        self.offsets = self.offsets + [shifted(o, "dp", 1) for o in self.offsets]

    def bundles(self):
        return Bundles(self.place, [(a, o, i % 2) for i, (a, o) in enumerate(zip(self.arrays, self.offsets))])


def fold(value, dim, bit, axis, step):
    kept = lax.dynamic_index_in_dim(value, bit, dim, keepdims=False)
    sent = lax.dynamic_index_in_dim(value, 1 - bit, dim, keepdims=False)
    return (kept.astype(F32) + swap(sent, axis, step).astype(F32)).astype(BF16)


def halve_sum(value, bit, axis, step):
    kept = lax.dynamic_index_in_dim(value, bit, 0, keepdims=False)
    sent = lax.dynamic_index_in_dim(value, 1 - bit, 0, keepdims=False)
    return kept + swap(sent, axis, step)


class Scatter:
    def __init__(self, place, theirs):
        self.place = place
        self.share, self.x_at, self.z_at = (lax.axis_index(a) for a in AXES)
        self.arrays = [theirs]

    def core(self):
        self.arrays = [swap(self.arrays[0], "dp", 1)]

    def split(self, mine):
        self.arrays = list(add_split(self.place, mine, self.arrays[0]))

    def xy(self, turn):
        high = self.share >> 1
        if turn == 0:
            kept_a, sent_a, kept_b, sent_b = self.arrays
            got_a, got_b = swap(sent_a, "dp", 2), swap(sent_b, "gx", 1)
            add = lambda u, v: (u.astype(F32) + v.astype(F32)).astype(BF16)
            self.arrays = [add(kept_a, got_a), add(kept_b, got_b)]
        else:
            first, second = self.arrays
            first, second = fold(first, 0, self.x_at, "gx", 1), fold(second, 0, high, "dp", 2)
            self.arrays = [jnp.stack([first, second]).reshape(1, 2, 2, 2, CELL, CELL)]

    def z(self, step):
        dim, bit = (3, self.z_at & 1) if step == 1 else (2, self.z_at >> 1)
        self.arrays = [fold(self.arrays[0], dim, bit, "gy", step)]

    def spread(self, step):
        both = self.arrays[0]
        other = swap(both, "dp", step)
        if step == 2:
            bit = self.share >> 1
            self.arrays = [jnp.stack([jnp.where(bit == 0, both, other), jnp.where(bit == 0, other, both)], axis=1)]
        else:
            self.arrays = [both, other]


def add_split(place, mine, got):
    block = (1, 1, 1, 4, CELL, CELL)
    flip = lambda bit, sent: 1 - bit if sent else bit
    over_dp = lambda sent: lambda j, p: (flip(p[0] >> 1, sent), 0, j, 0, 0, 0)
    over_gx = lambda sent: lambda j, p: (j, 1, flip(p[1], sent), 0, 0, 0)
    maps = [over_dp(0), over_dp(1), over_gx(0), over_gx(1)]

    def kernel(place, *refs):
        for i in range(4):
            refs[8 + i][0] = (refs[i][0, 0, 0].astype(F32) + refs[4 + i][0, 0, 0].astype(F32)).astype(BF16)

    return pl.pallas_call(
        kernel,
        grid_spec=pltpu.PrefetchScalarGridSpec(
            num_scalar_prefetch=1,
            grid=(2,),
            in_specs=[pl.BlockSpec(block, f) for f in maps] * 2,
            out_specs=[pl.BlockSpec((1, 4, CELL, CELL), lambda j, p: (j, 0, 0, 0))] * 4,
        ),
        out_shape=[jax.ShapeDtypeStruct((2, 4, CELL, CELL), BF16)] * 4,
        compiler_params=pltpu.CompilerParams(vmem_limit_bytes=24 * 1024 * 1024),
        cost_estimate=cost(0, 2 * 3 * 32 * CELL * CELL),
        name="add_split",
    )(place, mine, mine, mine, mine, got, got, got, got)


def pin(chains, *values):
    arrays = [c.arrays for c in chains]
    values, arrays = lax.optimization_barrier((values, arrays))
    for c, held in zip(chains, arrays):
        c.arrays = list(held)
    return values[0] if len(values) == 1 else values


def spread_vector(vector, axis):
    size = lax.axis_size(axis)
    pieces, offsets = vector[None], [0]
    step = size >> 1
    while step:
        pieces = jnp.concatenate([pieces, swap(pieces, axis, step)], axis=0)
        offsets = offsets + [o ^ step for o in offsets]
        step >>= 1
    index = lax.axis_index(axis)
    wanted = jnp.arange(size)[:, None]
    total = jnp.zeros((size, vector.shape[0]), F32)
    for i, offset in enumerate(offsets):
        total = total + jnp.where(wanted == (index ^ offset), pieces[i][None].astype(F32), 0.0)
    return total


def part_rows(block):
    parts = 4
    rows, cols = block.shape[0] // parts, block.shape[1]

    def kernel(x_ref, out):
        for z in range(parts):
            out[z] = x_ref[z * rows : (z + 1) * rows, :]

    return pl.pallas_call(
        kernel,
        in_specs=[WHOLE],
        out_specs=WHOLE,
        out_shape=jax.ShapeDtypeStruct((parts, rows, cols), BF16),
        compiler_params=pltpu.CompilerParams(vmem_limit_bytes=16 * 1024 * 1024),
        cost_estimate=cost(0, 4 * block.size),
        name="part_rows",
    )(block)


def unite_rows(block):
    parts, rows, cols = block.shape

    def kernel(x_ref, out):
        for z in range(parts):
            out[z * rows : (z + 1) * rows, :] = x_ref[z]

    return pl.pallas_call(
        kernel,
        in_specs=[WHOLE],
        out_specs=WHOLE,
        out_shape=jax.ShapeDtypeStruct((parts * rows, cols), BF16),
        compiler_params=pltpu.CompilerParams(vmem_limit_bytes=16 * 1024 * 1024),
        cost_estimate=cost(0, 4 * block.size),
        name="unite_rows",
    )(block)


def exchange(block):
    return lax.all_to_all(block, "gy", split_axis=0, concat_axis=0, tiled=True)


def pack(place, weights, small):
    def kernel(place, q, k, v, o, *refs):
        vectors, out, sem = refs[: len(small)], refs[-2], refs[-1]
        for share, ref in enumerate((q, k, v, o)):

            @pl.when(place[0] == share)
            def _():
                for half in range(2):
                    at = pl.ds(half * CELL, CELL)
                    source = ref.at[:, at] if share < 3 else ref.at[at, :]
                    pltpu.make_async_copy(source, out.at[0, half, 0:CELL], sem.at[half]).start()

        rows = [r[...].reshape(-1, CELL).astype(F32) for r in vectors]
        blank = jnp.zeros((6, CELL), F32)
        out[0, 0, CELL : CELL + 16, :] = jnp.concatenate(rows[:8] + [blank], axis=0).astype(BF16)
        out[0, 1, CELL : CELL + 16, :] = jnp.concatenate([rows[8], blank, blank[:2]], axis=0).astype(BF16)
        for half in range(2):
            cell = out.at[0, half, 0:CELL]
            pltpu.make_async_copy(cell, cell, sem.at[half]).wait()

    return pl.pallas_call(
        kernel,
        in_specs=[SMEM] + [ANY] * 4 + [WHOLE] * len(small),
        out_specs=WHOLE,
        out_shape=jax.ShapeDtypeStruct((1, 2, CELL + 16, CELL), BF16),
        scratch_shapes=[pltpu.SemaphoreType.DMA((2,))],
        compiler_params=pltpu.CompilerParams(vmem_limit_bytes=LIMIT),
        cost_estimate=cost(0, 8 * CELL * CELL),
        name="pack",
    )(place, *weights, *small)


def whole_weight(block, rows_axis, cols_axis):
    return lax.all_gather(lax.all_gather(block, rows_axis, axis=0, tiled=True), cols_axis, axis=1, tiled=True)


def weight_block(grad, rows_axis, cols_axis):
    part = lax.psum_scatter(grad, rows_axis, scatter_dimension=0, tiled=True)
    return lax.psum(lax.psum_scatter(part, cols_axis, scatter_dimension=1, tiled=True), "dp")


def projection_cells(weight):
    return weight.reshape(4, CELL, 2, 2, CELL).transpose(3, 2, 0, 1, 4)


def out_cells(weight):
    return weight.reshape(2, 2, CELL, 4, CELL).transpose(1, 0, 3, 2, 4)


def up_cells(weight):
    return weight.reshape(4, CELL, 2, 2, 2, 2, CELL).transpose(3, 4, 5, 2, 0, 1, 6)


def down_cells(weight):
    return weight.reshape(2, 2, 2, 2, CELL, 4, CELL).transpose(1, 2, 3, 0, 5, 4, 6)


def whole_bundles(cells, place):
    offsets = [(d, x, z) for d in range(4) for x in range(2) for z in range(4)]
    return Bundles(place, [(cells[:, half].reshape(-1, CELL, CELL), offsets, half) for half in range(2)])


def split_bundles(cells, place):
    parts = []
    for low in range(2):
        offsets = [(d, x, z) for d in (low, low + 2) for x in range(2) for z in range(4)]
        parts += [(cells[low::2, half].reshape(-1, CELL, CELL), offsets, half) for half in range(2)]
    return Bundles(place, parts)


def whole_shares(mine, theirs):
    return jnp.stack([mine, theirs], axis=1).reshape((4,) + mine.shape[1:])


class Bundles:
    def __init__(self, place, parts):
        self.place = place
        self.arrays = [p[0] for p in parts]
        self.meta = [(p[1], p[2]) for p in parts]

    def start(self, place_ref, refs, put):
        for ref, meta in zip(refs, self.meta):
            self.start_one(place_ref, ref, meta, put)

    @staticmethod
    def start_one(place_ref, ref, meta, put):
        offsets, half = meta
        for i, (od, ox, oz) in enumerate(offsets):
            put(ref.at[i, 0:CELL], place_ref[0] ^ od, half, place_ref[1] ^ ox, place_ref[2] ^ oz)


def window(ref, row, col):
    return ref.at[pl.ds(pl.multiple_of(row, CELL), CELL), pl.ds(pl.multiple_of(col, CELL), CELL)]


def put_projections(weights, sems):
    def put(source, share, half, x, z):
        @pl.when(share < 3)
        def _():
            dest = window(weights.at[share], z * CELL, (2 * x + half) * CELL)
            pltpu.make_async_copy(source, dest, sems.at[share]).start()

    return put


def put_out(weight, sem):
    def put(source, share, half, x, z):
        @pl.when(share == 3)
        def _():
            pltpu.make_async_copy(source, window(weight, (2 * x + half) * CELL, z * CELL), sem).start()

    return put


def put_feed(up, down, sems, core):
    def put(source, share, half, x, z):
        at = (2 * x + half) * CELL
        own = 1 - ((share ^ core) & 1)

        @pl.when(share < 2)
        def _():
            pltpu.make_async_copy(source, window(up.at[own], z * CELL, at), sems.at[own, 0]).start()

        @pl.when(share >= 2)
        def _():
            pltpu.make_async_copy(source, window(down.at[own], at, z * CELL), sems.at[own, 1]).start()

    return put


def wait_all(ref, sem):
    pltpu.make_async_copy(ref, ref, sem).wait()


def normal(values):
    center = values - jnp.mean(values, axis=1, keepdims=True)
    inverse = lax.rsqrt(jnp.mean(center * center, axis=1, keepdims=True) + EPSILON)
    return center * inverse, inverse


def back_norm(grad, normal_rows, inverse, gain):
    scaled = grad * gain
    mean_one = jnp.mean(scaled, axis=1, keepdims=True)
    mean_two = jnp.mean(scaled * normal_rows, axis=1, keepdims=True)
    return inverse * (scaled - mean_one - normal_rows * mean_two)


def column_sum(values):
    return jnp.sum(values, axis=0, keepdims=True)


def project(x_parts, vectors, bundles):
    parts, rows, cols = x_parts.shape
    count = len(bundles.arrays)
    given = vectors is not None

    def kernel(place, x_parts, *refs):
        if given:
            vec, *refs = refs
        sources = refs[:count]
        q_ref, x_ref, nt_ref, *refs = refs[count:]
        if not given:
            vec, up_ref, vbuf, vsem, *refs = refs
        weights, n_ref, sems = refs
        step = pl.program_id(0)

        @pl.when(step == 0)
        def _():
            if not given:
                for ref, (offsets, half) in zip(sources, bundles.meta):
                    for i, (od, ox, oz) in enumerate(offsets):
                        if od == 0:
                            dest = vbuf.at[half, place[1] ^ ox, place[2] ^ oz]
                            pltpu.make_async_copy(ref.at[i, CELL : CELL + 16], dest, vsem).start()
            bundles.start(place, sources, put_projections(weights, sems))
            if not given:
                wait_all(vbuf, vsem)
                tall = lambda row: [vbuf[0, x, 0, row + i : row + i + 1, :] for x in range(2) for i in range(2)]
                wide = lambda row: [vbuf[0, 0, z, row : row + 1, :] for z in range(4)]
                pieces = [wide(0), wide(1), tall(6), tall(8), wide(2), wide(3), wide(4), wide(5)]
                for i, cut in enumerate(pieces):
                    vec[i : i + 1, :] = jnp.concatenate(cut, axis=1).astype(F32)
                for part in range(2):
                    cut = [vbuf[1, x, 0, 4 * part + i : 4 * part + i + 1, :] for x in range(2) for i in range(4)]
                    up_ref[part] = jnp.concatenate(cut, axis=1).astype(F32)
            x = jnp.concatenate([x_parts[z] for z in range(parts)], axis=1)
            x_ref[...] = x
            normal_rows, _ = normal(x.astype(F32))
            normed = (normal_rows * vec[0:1, :] + vec[1:2, :]).astype(BF16)
            n_ref[...] = normed
            nt_ref[...] = normed.T

        for share in range(3):

            @pl.when(step == share)
            def _():
                wait_all(weights.at[share], sems.at[share])
                total = dot(n_ref[...], weights[share])
                if share != 1:
                    total = total + vec[2 + share // 2 : 3 + share // 2, :]
                q_ref[0] = total.astype(BF16)

    extra = [] if given else [jax.ShapeDtypeStruct((8, D), F32), jax.ShapeDtypeStruct((2, 1, 2 * D), F32)]
    outs = pl.pallas_call(
        kernel,
        grid=(3,),
        in_specs=[SMEM, WHOLE] + [WHOLE] * given + [ANY] * count,
        out_specs=[pl.BlockSpec((1, rows, D), lambda s: (s, 0, 0)), WHOLE, WHOLE] + [WHOLE] * len(extra),
        out_shape=[
            jax.ShapeDtypeStruct((3, rows, D), BF16),
            jax.ShapeDtypeStruct((rows, D), BF16),
            jax.ShapeDtypeStruct((D, rows), BF16),
        ]
        + extra,
        scratch_shapes=([] if given else [pltpu.VMEM((2, 2, 4, 16, CELL), BF16), pltpu.SemaphoreType.DMA])
        + [
            pltpu.VMEM((3, D, D), BF16),
            pltpu.VMEM((rows, D), BF16),
            pltpu.SemaphoreType.DMA((3,)),
        ],
        compiler_params=pltpu.CompilerParams(vmem_limit_bytes=32 * 1024 * 1024),
        cost_estimate=cost(6 * rows * D * D, 6 * D * D + 12 * rows * D),
        name="project",
    )(bundles.place, x_parts, *([vectors] if given else []), *bundles.arrays)
    return outs if not given else (*outs, vectors, None)


def attend(qkv, begin, end):
    rows = qkv.shape[1]
    pairs = end - begin

    def kernel(q_ref, k_ref, v_ref, o_ref, lse_ref, buf):
        q, k, v = q_ref[0], k_ref[0], v_ref[0]
        first = lax.broadcasted_iota(jnp.int32, (1, 128), 1) < 64
        scale = HEAD_DIM**-0.5
        outs = []
        for h in range(2):
            mine = first if h == 0 else jnp.logical_not(first)
            qh = jnp.where(mine, q.astype(F32) * scale, 0.0).astype(BF16)
            s = dot(qh, k, NT)
            top = jnp.max(s, axis=1, keepdims=True)
            p = jnp.exp(s - top)
            total = jnp.sum(p, axis=1, keepdims=True)
            outs.append(dot(p.astype(BF16), v) / total)
            buf[0:rows, h : h + 1] = top + jnp.log(total)
        o_ref[...] = jnp.where(first, outs[0], outs[1]).astype(BF16)
        lse_ref[0] = buf[...].T[0:8, 0:rows]

    spec = lambda i: pl.BlockSpec((1, rows, 128), lambda s, i=i: (i, 0, s + begin))
    return pl.pallas_call(
        kernel,
        grid=(pairs,),
        in_specs=[spec(0), spec(1), spec(2)],
        out_specs=[pl.BlockSpec((rows, 128), lambda s: (0, s)), pl.BlockSpec((1, 8, rows), lambda s: (s, 0, 0))],
        out_shape=[
            jax.ShapeDtypeStruct((rows, pairs * 128), BF16),
            jax.ShapeDtypeStruct((pairs, 8, rows), F32),
        ],
        scratch_shapes=[pltpu.VMEM((640, 128), F32)],
        compiler_params=pltpu.CompilerParams(vmem_limit_bytes=LIMIT),
        cost_estimate=cost(2048 * pairs * rows * rows, 1024 * pairs * rows, 2 * pairs * rows * rows),
        name="attend",
    )(qkv, qkv, qkv)


def attend_back(qkv, mixture, lse, mixture_grad, begin, end):
    rows = qkv.shape[1]
    pairs = end - begin

    def kernel(q_ref, k_ref, v_ref, o_ref, lse_ref, do_ref, g_ref, b_ref):
        q, k, v, grad = q_ref[0], k_ref[0], v_ref[0], do_ref[...]
        first = lax.broadcasted_iota(jnp.int32, (1, 128), 1) < 64
        scale = HEAD_DIM**-0.5
        pick = lax.broadcasted_iota(jnp.int32, (8, 128), 0) == lax.broadcasted_iota(jnp.int32, (8, 128), 1) // 64
        product = grad.astype(F32) * o_ref[...].astype(F32)
        delta = lax.dot_general(
            jnp.where(pick, 1.0, 0.0), product, NT, precision=lax.Precision.HIGHEST, preferred_element_type=F32
        )
        dqs, dks, dvs = [], [], []
        for h in range(2):
            mine = first if h == 0 else jnp.logical_not(first)
            qh = jnp.where(mine, q.astype(F32) * scale, 0.0).astype(BF16)
            gh = jnp.where(mine, grad, jnp.zeros_like(grad))
            p = jnp.exp(dot(k, qh, NT) - lse_ref[0, h : h + 1, :])
            dp = dot(v, gh, NT)
            ds = (p * (dp - delta[h : h + 1, :])).astype(BF16)
            dvs.append(dot(p.astype(BF16), grad))
            dks.append(dot(ds, q))
            dqs.append(dot(k, ds, TN))
        dq = (jnp.concatenate([dqs[0][:64], dqs[1][64:]], axis=0) * scale).T.astype(BF16)
        dk = (jnp.where(first, dks[0], dks[1]) * scale).astype(BF16)
        dv = jnp.where(first, dvs[0], dvs[1]).astype(BF16)
        g_ref[0], g_ref[1], g_ref[2] = dq, dk, dv
        b_ref[0:1, :] = column_sum(dq.astype(F32))
        b_ref[1:2, :] = column_sum(dv.astype(F32))

    spec = lambda i: pl.BlockSpec((1, rows, 128), lambda s, i=i: (i, 0, s + begin))
    flat = pl.BlockSpec((rows, 128), lambda s: (0, s))
    wide = pl.BlockSpec((rows, 128), lambda s: (0, s + begin))
    return pl.pallas_call(
        kernel,
        grid=(pairs,),
        in_specs=[spec(0), spec(1), spec(2), flat, pl.BlockSpec((1, 8, rows), lambda s: (s, 0, 0)), wide],
        out_specs=[pl.BlockSpec((3, rows, 128), lambda s: (0, 0, s)), pl.BlockSpec((8, 128), lambda s: (0, s))],
        out_shape=[
            jax.ShapeDtypeStruct((3, rows, pairs * 128), BF16),
            jax.ShapeDtypeStruct((8, pairs * 128), F32),
        ],
        compiler_params=pltpu.CompilerParams(vmem_limit_bytes=32 * 1024 * 1024),
        cost_estimate=cost(6000 * pairs * rows * rows, 2048 * pairs * rows, 2 * pairs * rows * rows),
        name="attend_back",
    )(qkv, qkv, qkv, mixture, lse, mixture_grad)


def mix_out(mixtures, inputs, vectors, bundles):
    rows = inputs.shape[0]
    count = len(bundles.arrays)

    def kernel(place, vec, m_ref, o_ref, x_ref, *refs):
        sources = refs[:count]
        mid_ref, n_ref, nt_ref, weight, sem = refs[count:]
        bundles.start(place, sources, put_out(weight, sem))
        wait_all(weight, sem)
        mixture = jnp.concatenate([m_ref[...], o_ref[...]], axis=1)
        middle = x_ref[...].astype(F32) + (dot(mixture, weight[...]) + vec[4:5, :])
        mid_ref[...] = middle
        normal_rows, _ = normal(middle)
        normed = (normal_rows * vec[5:6, :] + vec[6:7, :]).astype(BF16)
        n_ref[...] = normed
        nt_ref[...] = normed.T

    return pl.pallas_call(
        kernel,
        in_specs=[SMEM] + [WHOLE] * 4 + [ANY] * count,
        out_specs=[WHOLE] * 3,
        out_shape=[
            jax.ShapeDtypeStruct((rows, D), F32),
            jax.ShapeDtypeStruct((rows, D), BF16),
            jax.ShapeDtypeStruct((D, rows), BF16),
        ],
        scratch_shapes=[pltpu.VMEM((D, D), BF16), pltpu.SemaphoreType.DMA],
        compiler_params=pltpu.CompilerParams(vmem_limit_bytes=32 * 1024 * 1024),
        cost_estimate=cost(2 * rows * D * D, 2 * D * D + 10 * rows * D),
        name="mix_out",
    )(bundles.place, vectors, *mixtures, inputs, *bundles.arrays)


def gelu_pair(h):
    below = 0.5 * (1.0 + lax.erf(h * 0.7071067811865476))
    bell = jnp.exp(h * h * -0.5) * 0.3989422804014327
    return h * below, below + h * bell


def feed(acts, up_bias, bundles, partials):
    rows = acts[0].shape[0]
    tile = 2 * CELL
    count = len(bundles.arrays)
    olds = [] if partials is None else list(partials)
    carried = len(olds)

    def kernel(place, bias, n_ref, nt_ref, g_ref, gt_ref, *refs):
        olds, sources = refs[:carried], refs[carried : carried + count]
        out_acc, back_acc, mine, theirs, bias_ref, up, down, sems = refs[carried + count :]
        step = pl.program_id(0)
        own = step // 2
        x = lax.rem(step, 2)
        core = place[0] & 1
        sub = jnp.where(step < 2, 1 - core, core)

        @pl.when(step == 0)
        def _():
            order = list(range(count // 2, count)) + list(range(count // 2))
            put = put_feed(up, down, sems, core)
            for i in order:
                Bundles.start_one(place, sources[i], bundles.meta[i], put)
            for acc, old in zip((out_acc, back_acc), olds):
                acc[...] = old[...]
            if not carried:
                out_acc[...] = jnp.zeros_like(out_acc)
                back_acc[...] = jnp.zeros_like(back_acc)

        for i in range(2):

            @pl.when(step == 2 * i)
            def _():
                wait_all(up.at[i], sems.at[i, 0])
                wait_all(down.at[i], sems.at[i, 1])

        at = pl.multiple_of(x * tile, tile)
        bias_at = pl.multiple_of((2 * x + sub) * tile, tile)
        up_tile = up[own, :, pl.ds(at, tile)]
        down_tile = down[own, pl.ds(at, tile), :]
        pre = dot(n_ref[...], up_tile) + bias[0:1, pl.ds(bias_at, tile)]
        hidden, slope = gelu_pair(pre)
        hidden = hidden.astype(BF16)
        out_acc[...] += dot(hidden, down_tile)
        pre_grad = (dot(g_ref[...], down_tile, NT) * slope).astype(BF16)
        back_acc[...] += dot(pre_grad, up_tile, NT)
        bias_ref[0, 0] = column_sum(pre_grad.astype(F32))
        up_grad, down_grad = dot(nt_ref[...], pre_grad).astype(BF16), dot(gt_ref[...], hidden).astype(BF16)

        def leave(cells):
            for i, grad in enumerate((up_grad, down_grad)):
                for half in range(2):
                    for z in range(4):
                        cell = grad[z * CELL : (z + 1) * CELL, half * CELL : (half + 1) * CELL]
                        cells[i, half, 0, z] = cell

        @pl.when(step < 2)
        def _():
            leave(theirs)

        @pl.when(step >= 2)
        def _():
            leave(mine)

    acc = jax.ShapeDtypeStruct((rows, D), F32)
    full = lambda shape: pl.BlockSpec(shape, lambda s, p: (0,) * len(shape))
    block = (2, 2, 1, 4, CELL, CELL)
    cells = jax.ShapeDtypeStruct((2, 2, 2, 4, CELL, CELL), BF16)
    ins = [up_bias, *acts, *olds]
    low = lambda s, p: jnp.where(s < 2, 1 - (p[0] & 1), p[0] & 1)
    return pl.pallas_call(
        kernel,
        grid_spec=pltpu.PrefetchScalarGridSpec(
            num_scalar_prefetch=1,
            grid=(4,),
            in_specs=[full(v.shape) for v in ins] + [ANY] * count,
            out_specs=[
                full((rows, D)),
                full((rows, D)),
                pl.BlockSpec(block, lambda s, p: (0, 0, jnp.maximum(s - 2, 0), 0, 0, 0)),
                pl.BlockSpec(block, lambda s, p: (0, 0, jnp.minimum(s, 1), 0, 0, 0)),
                pl.BlockSpec((1, 1, 1, tile), lambda s, p: (lax.rem(s, 2), low(s, p), 0, 0)),
            ],
            scratch_shapes=[
                pltpu.VMEM((2, D, 2 * tile), BF16),
                pltpu.VMEM((2, 2 * tile, D), BF16),
                pltpu.SemaphoreType.DMA((2, 2)),
            ],
        ),
        out_shape=[acc, acc, cells, cells, jax.ShapeDtypeStruct((2, 2, 1, tile), F32)],
        compiler_params=pltpu.CompilerParams(vmem_limit_bytes=FEED_LIMIT),
        cost_estimate=cost(48 * rows * D * tile, 32 * D * tile + 28 * rows * D, 8 * rows * tile),
        name="feed",
    )(bundles.place, *ins, *bundles.arrays)


def turn(middle, cotangent, out_sum, back_sum, vectors, bundles):
    rows = middle.shape[0]
    count = len(bundles.arrays)
    parts = 4

    def kernel(place, vec, mid_ref, g_ref, out_ref, back_ref, *refs):
        sources = refs[:count]
        pieces, grad_ref, branch_t, mix_ref, sum_ref, weight, sem = refs[count:]
        bundles.start(place, sources, put_out(weight, sem))
        middle = mid_ref[...]
        result = (middle + (out_ref[...] + vec[7:8, :])).astype(BF16)
        for k in range(parts):
            pieces[k] = result[:, k * CELL : (k + 1) * CELL]
        normal_rows, inverse = normal(middle)
        back = back_ref[...]
        grads = g_ref[...].astype(F32)
        middle_grad = grads + back_norm(back, normal_rows, inverse, vec[5:6, :])
        grad_ref[...] = middle_grad
        branch = middle_grad.astype(BF16)
        branch_t[...] = branch.T
        sum_ref[0:1, :] = column_sum(branch.astype(F32))
        sum_ref[1:2, :] = column_sum(back * normal_rows)
        sum_ref[2:3, :] = column_sum(back)
        sum_ref[3:4, :] = column_sum(grads)
        wait_all(weight, sem)
        mix_ref[...] = dot(branch, weight[...], NT).astype(BF16)

    full = jax.ShapeDtypeStruct((rows, D), BF16)
    return pl.pallas_call(
        kernel,
        in_specs=[SMEM] + [WHOLE] * 5 + [ANY] * count,
        out_specs=[WHOLE] * 5,
        out_shape=[
            jax.ShapeDtypeStruct((parts, rows, CELL), BF16),
            jax.ShapeDtypeStruct((rows, D), F32),
            jax.ShapeDtypeStruct((D, rows), BF16),
            full,
            jax.ShapeDtypeStruct((8, D), F32),
        ],
        scratch_shapes=[
            pltpu.VMEM((D, D), BF16),
            pltpu.SemaphoreType.DMA,
        ],
        compiler_params=pltpu.CompilerParams(vmem_limit_bytes=LIMIT),
        cost_estimate=cost(2 * rows * D * D, 2 * D * D + 24 * rows * D),
        name="turn",
    )(bundles.place, vectors, middle, cotangent, out_sum, back_sum, *bundles.arrays)


def weigh(place, normed_t, branch_t, grads, mixtures, other):
    rows = normed_t.shape[1]

    def kernel(place, n_t, b_t, g0, g1, m0, m1, cells):
        core = place[0] & 1
        share = 2 * pl.program_id(0) + (1 - core if other else core)

        def fill(left, right):
            for x in range(2):
                for half in range(2):
                    grad = dot(left, right(x, half * CELL)).astype(BF16)
                    cells[0, half, x] = grad.reshape(4, CELL, CELL)

        for k in range(3):

            @pl.when(share == k)
            def _():
                fill(n_t[...], lambda x, at: (g0, g1)[x][k, :, at : at + CELL])

        @pl.when(share == 3)
        def _():
            fill(b_t[...], lambda x, at: (m0, m1)[x][:, at : at + CELL])

    return pl.pallas_call(
        kernel,
        grid=(2,),
        in_specs=[SMEM] + [WHOLE] * 6,
        out_specs=pl.BlockSpec((1, 2, 2, 4, CELL, CELL), lambda s: (s, 0, 0, 0, 0, 0)),
        out_shape=jax.ShapeDtypeStruct((2, 2, 2, 4, CELL, CELL), BF16),
        compiler_params=pltpu.CompilerParams(vmem_limit_bytes=32 * 1024 * 1024),
        cost_estimate=cost(4 * rows * D * D, 4 * D * D + 12 * rows * D),
        name="weigh",
    )(place, normed_t, branch_t, *grads, *mixtures)


def finish(inputs, middle_grad, grads, vectors, bundles):
    rows = inputs.shape[0]
    count = len(bundles.arrays)
    parts = 4

    def kernel(place, vec, x_ref, mid_ref, g0, g1, *refs):
        sources = refs[:count]
        pieces, sum_ref, weights, sems = refs[count:]
        bundles.start(place, sources, put_projections(weights, sems))
        normal_rows, inverse = normal(x_ref[...].astype(F32))
        back = None
        for k in range(3):
            wait_all(weights.at[k], sems.at[k])
            term = dot(jnp.concatenate([g0[k], g1[k]], axis=1), weights[k], NT)
            back = term if back is None else back + term
        result = (mid_ref[...] + back_norm(back, normal_rows, inverse, vec[0:1, :])).astype(BF16)
        for k in range(parts):
            pieces[k] = result[:, k * CELL : (k + 1) * CELL]
        sum_ref[0:1, :] = column_sum(back * normal_rows)
        sum_ref[1:2, :] = column_sum(back)

    return pl.pallas_call(
        kernel,
        in_specs=[SMEM] + [WHOLE] * 5 + [ANY] * count,
        out_specs=[WHOLE] * 2,
        out_shape=[jax.ShapeDtypeStruct((parts, rows, CELL), BF16), jax.ShapeDtypeStruct((8, D), F32)],
        scratch_shapes=[pltpu.VMEM((3, D, D), BF16), pltpu.SemaphoreType.DMA((3,))],
        compiler_params=pltpu.CompilerParams(vmem_limit_bytes=32 * 1024 * 1024),
        cost_estimate=cost(6 * rows * D * D, 6 * D * D + 14 * rows * D),
        name="finish",
    )(bundles.place, vectors, inputs, middle_grad, *grads, *bundles.arrays)


def unpack_projections(place, own, other):
    def kernel(place, a_ref, b_ref, *refs):
        outs, buf = refs[:4], refs[4]
        core = place[0] & 1
        buf[core] = a_ref[...]
        buf[1 - core] = b_ref[...]
        for share in range(4):
            for half in range(2):
                cell = buf[share % 2, share // 2, half]
                at = slice(half * CELL, (half + 1) * CELL)
                if share < 3:
                    outs[share][:, at] = cell.astype(F32)
                else:
                    outs[share][at, :] = cell.astype(F32).T

    tall, wide = (jax.ShapeDtypeStruct(s, F32) for s in ((2 * CELL, CELL), (CELL, 2 * CELL)))
    return pl.pallas_call(
        kernel,
        in_specs=[SMEM, WHOLE, WHOLE],
        out_specs=[WHOLE] * 4,
        out_shape=[wide, wide, wide, tall],
        scratch_shapes=[pltpu.VMEM((2, 2, 2, CELL, CELL), BF16)],
        compiler_params=pltpu.CompilerParams(vmem_limit_bytes=LIMIT),
        cost_estimate=cost(0, 3 * 16 * CELL * CELL),
        name="unpack_projections",
    )(place, own, other)


def unpack_feed(place, own, other):
    def kernel(place, a_ref, b_ref, up_ref, down_ref, buf):
        core = place[0] & 1
        buf[core] = a_ref[...]
        buf[1 - core] = b_ref[...]
        for part in range(2):
            for sub in range(2):
                for half in range(2):
                    at = (4 * part + 2 * sub + half) * CELL
                    up_ref[:, at : at + CELL] = buf[sub, part, 0, half].astype(F32)
                    down_ref[at : at + CELL, :] = buf[sub, part, 1, half].astype(F32).T

    return pl.pallas_call(
        kernel,
        in_specs=[SMEM, WHOLE, WHOLE],
        out_specs=[WHOLE] * 2,
        out_shape=[jax.ShapeDtypeStruct((CELL, 8 * CELL), F32), jax.ShapeDtypeStruct((8 * CELL, CELL), F32)],
        scratch_shapes=[pltpu.VMEM((2, 2, 2, 2, CELL, CELL), BF16)],
        compiler_params=pltpu.CompilerParams(vmem_limit_bytes=LIMIT),
        cost_estimate=cost(0, 6 * 16 * CELL * CELL),
        name="unpack_feed",
    )(place, own, other)


def join(x_parts):
    parts, rows, cols = x_parts.shape

    def kernel(x_ref, out, out_t):
        for k in range(parts):
            at = slice(k * cols, (k + 1) * cols)
            out[:, at] = x_ref[k]
            out_t[at, :] = x_ref[k].T

    return pl.pallas_call(
        kernel,
        in_specs=[WHOLE],
        out_specs=[WHOLE] * 2,
        out_shape=[
            jax.ShapeDtypeStruct((rows, cols * parts), BF16),
            jax.ShapeDtypeStruct((cols * parts, rows), BF16),
        ],
        compiler_params=pltpu.CompilerParams(vmem_limit_bytes=24 * 1024 * 1024),
        cost_estimate=cost(0, 6 * rows * cols * parts),
        name="join",
    )(x_parts)


def layer_body(*args):
    (
        layer_input,
        output_grad,
        first_gain,
        first_shift,
        query_weight,
        key_weight,
        value_weight,
        query_bias,
        value_bias,
        out_weight,
        out_bias,
        second_gain,
        second_shift,
        up_weight,
        up_bias,
        down_weight,
        down_bias,
    ) = args
    shape = tuple(lax.axis_size(a) for a in AXES)
    fast = shape == (4, 2, 4)
    width = first_gain.shape[0]
    head = query_bias.shape[0]
    feed_width = up_bias.shape[0]
    index = [lax.axis_index(a) for a in AXES]
    place = jnp.stack(index if fast else [jnp.int32(0)] * 3).astype(jnp.int32)

    small = [first_gain, first_shift, out_bias, second_gain, second_shift, down_bias, query_bias, value_bias, up_bias]
    if fast:
        get_j = Gather(pack(place, (query_weight, key_weight, value_weight, out_weight), small), place)
        get_j.z(2)
        x_block, ups, downs = pin([], layer_input, up_weight, down_weight)
        x_copies = part_rows(x_block)
        ups = ups.reshape(CELL, 2, 2, 2, CELL).transpose(2, 1, 3, 0, 4)
        downs = downs.reshape(2, 2, 2, CELL, CELL).transpose(1, 0, 2, 3, 4)
        feeds = lax.dynamic_index_in_dim(jnp.concatenate([ups, downs]), index[0], 0, keepdims=False)
        get_j.z(1)
        x_parts = exchange(pin([get_j], x_copies))
        get_j.xy(0)
        get_j.xy(1)
        x_parts, feeds = pin([], x_parts, feeds)
        get_a, get_b = (Gather(feeds[i : i + 1], place) for i in range(2))
        get_a.z(2)
        get_j.core()
        joined = get_j.bundles()
        vectors = None
        get_a.z(1)
        x_parts, output_grad = pin([get_a, get_b], x_parts, output_grad)
        get_a.xy(0)
        get_b.z(2)
    else:
        wide = spread_vector(jnp.concatenate(small[:6]), "gy").reshape(-1, 6, width)
        wide = wide.transpose(1, 0, 2).reshape(6, D)
        tall = spread_vector(jnp.concatenate(small[6:]), "gx")
        vectors = jnp.stack(
            [
                wide[0],
                wide[1],
                tall[:, :head].reshape(-1),
                tall[:, head : 2 * head].reshape(-1),
                wide[2],
                wide[3],
                wide[4],
                wide[5],
            ]
        )
        bias_up = tall[:, 2 * head :].reshape(2, 2, D).transpose(1, 0, 2).reshape(2, 1, 2 * D)
        by_parts = lambda rows: rows.reshape(rows.shape[0], 4, CELL).transpose(1, 0, 2)
        x_parts = by_parts(lax.all_to_all(layer_input, "gy", split_axis=0, concat_axis=1, tiled=True))
        grad_parts = by_parts(lax.all_to_all(output_grad, "gy", split_axis=0, concat_axis=1, tiled=True))
        joined = whole_bundles(
            jnp.stack(
                [projection_cells(whole_weight(w, "gy", "gx")) for w in (query_weight, key_weight, value_weight)]
                + [out_cells(whole_weight(out_weight, "gx", "gy"))]
            ),
            place,
        )
        ups = up_cells(whole_weight(up_weight, "gy", "gx"))
        downs = down_cells(whole_weight(down_weight, "gx", "gy"))
        both = [jnp.concatenate([ups[i], downs[i]]) for i in range(2)]
        fed = [split_bundles(c, place) for c in both]

    qkv, inputs, normed_t, vectors, bias_given = project(x_parts, vectors, joined)
    if fast:
        bias_up = bias_given
        qkv = pin([get_a, get_b], qkv)
        get_a.xy(1)
        get_b.z(1)
    mixture_0, lse_0 = attend(qkv, 0, 4)
    if fast:
        qkv, mixture_0, output_grad = pin([get_b], qkv, mixture_0, output_grad)
        grad_parts = exchange(part_rows(output_grad))
    mixture_1, lse_1 = attend(qkv, 4, 8)
    mixtures = (mixture_0, mixture_1)
    if fast:
        mixtures = pin([get_a, get_b], mixtures)
        get_b.xy(0)
        get_a.core()
        fed = [get_a.bundles()]
    middle, normed_two, normed_two_t = mix_out(mixtures, inputs, vectors, joined)
    cotangent, cotangent_t = join(grad_parts)
    if fast:
        normed_two = pin([get_b], normed_two)
        get_b.xy(1)
    acts = (normed_two, normed_two_t, cotangent, cotangent_t)
    *sums, mine_a, theirs_a, bias_a = feed(acts, bias_up[0], fed[0], None)
    if fast:
        sums, theirs_a = pin([get_b], sums, theirs_a)
        get_b.core()
        fed.append(get_b.bundles())
        put_a = Scatter(place, theirs_a)
        put_a.core()
    *sums, mine_b, theirs_b, bias_b = feed(acts, bias_up[1], fed[1], sums)
    if fast:
        put_b = Scatter(place, theirs_b)
        put_b.core()
        sums, mine_a = pin([put_a], sums, mine_a)
        put_a.split(mine_a)
        sums = pin([put_a], sums)
        put_a.xy(0)
    results, middle_grad, branch_t, mixture_grad, sums_two = turn(middle, cotangent, *sums, vectors, joined)
    if fast:
        mine_b, mixture_grad, results = pin([put_b], mine_b, mixture_grad, results)
        put_b.split(mine_b)
        mixture_grad = pin([put_b], mixture_grad)
        results = exchange(results)
    grads_0, heads_0 = attend_back(qkv, mixtures[0], lse_0, mixture_grad, 0, 4)
    if fast:
        mixture_grad, grads_0 = pin([put_a], mixture_grad, grads_0)
        put_a.xy(1)
        put_b.xy(0)
    grads_1, heads_1 = attend_back(qkv, mixtures[1], lse_1, mixture_grad, 4, 8)
    grads = (grads_0, grads_1)
    if fast:
        grads, results = pin([put_a], grads, results)
        put_a.z(1)
    theirs_c = weigh(place, normed_t, branch_t, grads, mixtures, True)
    if fast:
        put_c = Scatter(place, theirs_c)
        put_c.core()
        grads, theirs_c = pin([put_b], grads, theirs_c)
        put_b.xy(1)
    mine_c = weigh(place, normed_t, branch_t, grads, mixtures, False)
    if fast:
        mine_c, middle_grad = pin([put_a, put_b, put_c], mine_c, middle_grad)
        put_c.split(mine_c)
        middle_grad = pin([put_c], middle_grad)
        put_c.xy(0)
        put_a.z(2)
        put_b.z(1)
    input_grads, sums_one = finish(inputs, middle_grad, grads, vectors, joined)

    bias_up_grad = jnp.stack([bias_a, bias_b]).transpose(1, 0, 2, 3, 4).reshape(2, -1)
    sums_heads = jnp.concatenate([heads_0[:2], heads_1[:2]], axis=1)
    wide_sums = jnp.concatenate([sums_one[:2], sums_two[:4]])
    if fast:
        by_z = wide_sums.reshape(6, 1, 4, CELL).transpose(1, 2, 0, 3).reshape(1, 4, 6 * CELL)
        by_x = jnp.concatenate(
            [sums_heads.reshape(2, 2, head).transpose(1, 0, 2).reshape(2, 2 * head), bias_up_grad], axis=1
        )
        totals = jnp.concatenate(
            [jnp.broadcast_to(by_z, (2, 4, 6 * CELL)), jnp.broadcast_to(by_x[:, None], (2, 4, by_x.shape[1]))], axis=2
        )
        input_grads, totals = pin([put_c, put_b], input_grads, totals)
        put_c.xy(1)
        input_grads = exchange(input_grads)
        put_b.z(2)
        put_f = Scatter(place, None)
        put_f.arrays = [jnp.concatenate([put_a.arrays[0], put_b.arrays[0]])]
        put_f.spread(2)
        totals = halve_sum(totals, index[1], "gx", 1)
        totals = halve_sum(totals.reshape(2, 2, -1), index[2] >> 1, "gy", 2)
        result = results
        put_c.z(1)
        put_f.spread(1)
        totals = halve_sum(totals, index[2] & 1, "gy", 1)
        result = unite_rows(result)
        put_c.z(2)
        totals = totals + swap(totals, "dp", 1)
        up_grad, down_grad = unpack_feed(place, put_f.arrays[0], put_f.arrays[1])
        put_c.spread(2)
        totals = totals + swap(totals, "dp", 2)
        input_grad = unite_rows(input_grads)
        up_grad, down_grad, totals, result = pin([put_c], up_grad, down_grad, totals, result)
        put_c.spread(1)
        query_grad, key_grad, value_grad, out_grad = unpack_projections(
            place, put_c.arrays[0][0], put_c.arrays[1][0]
        )
        wide_grads = [totals[i * CELL : (i + 1) * CELL] for i in range(6)]
        head_grads = [totals[6 * CELL + i * head : 6 * CELL + (i + 1) * head] for i in range(2)]
        up_bias_grad = totals[6 * CELL + 2 * head :]
    else:
        back = lambda parts: lax.all_to_all(
            parts.transpose(1, 0, 2).reshape(parts.shape[1], D), "gy", split_axis=1, concat_axis=0, tiled=True
        )
        result, input_grad = back(results), back(input_grads)
        shares = whole_shares(mine_c, theirs_c).astype(F32)
        query_grad, key_grad, value_grad = (
            weight_block(shares[i].transpose(2, 3, 1, 0, 4).reshape(D, D), "gy", "gx") for i in range(3)
        )
        out_grad = weight_block(shares[3].transpose(1, 0, 4, 2, 3).reshape(D, D), "gx", "gy")
        shares = jnp.stack([whole_shares(mine_a, theirs_a), whole_shares(mine_b, theirs_b)]).astype(F32)
        up_grad = weight_block(shares[:, :2].transpose(4, 5, 3, 0, 1, 2, 6).reshape(D, -1), "gy", "gx")
        down_grad = weight_block(shares[:, 2:].transpose(3, 0, 1, 2, 6, 4, 5).reshape(-1, D), "gx", "gy")
        wide_sums, sums_heads, bias_up_grad = lax.psum((wide_sums, sums_heads, bias_up_grad), AXES)
        wide_grads = [lax.dynamic_slice_in_dim(wide_sums[i], index[2] * width, width) for i in range(6)]
        head_grads = [lax.dynamic_slice_in_dim(sums_heads[i], index[1] * head, head) for i in range(2)]
        up_bias_grad = lax.dynamic_slice_in_dim(bias_up_grad.reshape(-1), index[1] * feed_width, feed_width)

    return (
        result,
        input_grad,
        wide_grads[0],
        wide_grads[1],
        query_grad,
        key_grad,
        value_grad,
        head_grads[0],
        head_grads[1],
        out_grad,
        wide_grads[2],
        wide_grads[3],
        wide_grads[4],
        up_grad,
        up_bias_grad,
        down_grad,
        wide_grads[5],
    )


def solution(mesh):
    tokens = P(("dp", "gx"), "gy")
    wide, tall = P("gy"), P("gx")
    down_rows, across = P("gy", "gx"), P("gx", "gy")
    params = (
        wide, wide, down_rows, down_rows, down_rows, tall, tall, across, wide,
        wide, wide, down_rows, tall, across, wide,
    )
    return jax.shard_map(
        layer_body,
        mesh=mesh,
        in_specs=(tokens, tokens) + params,
        out_specs=(tokens, tokens) + params,
        check_vma=False,
    )
```
